1024 devices in a mesh: gy: 32 (over y_lo, z), gz: 32 (over y_hi, x, core).
Axes of the slice: x: 4, y: 8 (y_hi: 4, y_lo: 2; y = y_hi * 2 + y_lo), z: 16, core: 2. Of those that a mesh axis runs over, the one named last changes fastest.
Arguments:
- populations: float32 [19, 4, 256, 4096], P(None, None, 'gy', 'gz')
- marker_owner: int32 [524288, 1], P(('gy', 'gz')), may hold values from 0 to 31; in each aligned block of 512 rows (0 to 511, 512 to 1023, ...) at most 24 rows name the same one
- marker_cell: int32 [3, 524288], P(None, ('gy', 'gz')), may hold values from 0 to 126, as said below
- marker_frac: float32 [3, 524288], P(None, ('gy', 'gz')), may hold values from 0 to 1
- marker_speed: float32 [3, 524288], P(None, ('gy', 'gz')), may hold values from -0.2 to 0.2
- marker_count: int32 [1024], P(('gy', 'gz')), may hold values from 256 to 512
Outputs:
- populations_out: float32 [19, 4, 256, 4096], P(None, None, 'gy', 'gz')
- marker_force: float32 [3, 524288], P(None, ('gy', 'gz'))
The draws below stay inside these ranges and needn't reach their ends.
Inputs may be any that keep to these rules, and one draw needn't show every extreme that they name: `marker_owner`: among the 512 markers of one device at most 24 name one owner. `marker_cell`: row 0 is below 4, row 1 below 7, row 2 below 127, so the stencil lies in the owner's block.
All inputs are finite; a program needn't handle non-finite values.
Results may differ from the reference program's by a relative error of at most 0.0003.
Values sent between devices are 32-bit elements; how exact they have to be, the bound alone decides.
No kernel may reach another device: no remote copies, remote signals or barrier semaphores. Data moves between devices by JAX's collectives and lax.ppermute only.
A program may use at most 64 MiB of HBM per device.

```python
import math
import jax
import jax.numpy as jnp
import numpy as np

X = 4
CY = 8
CZ = 128
MDEV = 512
STEPS = 2
CAP = 24
NY = 256
NZ = 4096
PENCILS = 1024
MARKERS = 524288
N_GZ = 32


velocity_table = ((0, 0, 0), (1, 0, 0), (-1, 0, 0), (0, 1, 0), (0, -1, 0), (0, 0, 1), (0, 0, -1), (1, 1, 0), (-1, -1, 0), (1, -1, 0), (-1, 1, 0), (1, 0, 1), (-1, 0, -1), (1, 0, -1), (-1, 0, 1), (0, 1, 1), (0, -1, -1), (0, 1, -1), (0, -1, 1))


weight_table = (1.0 / 3.0,) + (1.0 / 18.0,) * 6 + (1.0 / 36.0,) * 12


def draw_populations(key, part):
    key = jax.random.fold_in(key, 1)
    keys = jax.random.split(key, 3)
    shape = (X, NY, NZ)
    density = jax.random.uniform(keys[0], shape, jnp.float32, 0.9, 1.1)
    speeds = jnp.clip(0.04 * jax.random.normal(keys[1], (3,) + shape, jnp.float32), -0.12, 0.12)
    noise = jnp.clip(0.25 * jax.random.normal(keys[2], (19,) + shape, jnp.float32), -0.6, 0.6)
    speed_sq = speeds[0] * speeds[0] + speeds[1] * speeds[1] + speeds[2] * speeds[2]
    result = []
    for member in range(19):
        along = jnp.zeros(shape, jnp.float32)
        for axis_no in range(3):
            component = velocity_table[member][axis_no]
            if component != 0:
                along = along + component * speeds[axis_no]
        equil = weight_table[member] * density * (1.0 + 3.0 * along + 4.5 * along * along - 1.5 * speed_sq)
        result.append(equil * (1.0 + noise[member]))
    return jnp.stack(result).astype(jnp.float32)


def draw_marker_cell(key, part):
    key = jax.random.fold_in(key, 2)
    keys = jax.random.split(key, 3)
    row_x = jax.random.randint(keys[0], (MARKERS,), 0, X).at[0].set(X - 1)
    row_y = jax.random.randint(keys[1], (MARKERS,), 0, CY - 1).at[0].set(CY - 2)
    row_z = jax.random.randint(keys[2], (MARKERS,), 0, CZ - 1).at[0].set(CZ - 2)
    return jnp.stack([row_x, row_y, row_z]).astype(jnp.int32)


def draw_marker_count(key, part):
    key = jax.random.fold_in(key, 3)
    counts = jax.random.randint(key, (PENCILS,), MDEV // 2, MDEV + 1)
    counts = counts.at[0].set(MDEV).at[PENCILS - 1].set(MDEV // 2)
    return counts.astype(jnp.int32)


def block_scale(own_key, dims, cuts, least, top_value):
    factor_of, own = 1.0, jax.random.fold_in(own_key, 6)
    for position, shards_of in cuts:
        heights = jnp.exp(jax.random.uniform(jax.random.fold_in(own, position), (shards_of,), jnp.float32, least / len(cuts), top_value / len(cuts)))
        factor_of = factor_of * jnp.repeat(heights, dims[position] // shards_of).reshape([-1 if axis == position else 1 for axis in range(len(dims))])
    return factor_of


def shared_out(stream_key, own, number, rows, number_of, top, limit, skew):
    ranking = jax.random.permutation(stream_key, number_of)
    packed, ordinary = shares(number_of, rows * top, limit, skew, True), shares(number_of, rows * top, limit, skew, False)
    places = jnp.arange(number_of)

    def named(tallies, rotation):
        used = int((tallies > 0).sum())
        fixed = max(1, used // 4)
        moved = fixed + (places - fixed + rotation * (used - fixed)) % max(1, number_of - fixed)
        return jnp.zeros((number_of,), jnp.int32).at[ranking[jnp.where(places < fixed, places, moved)]].set(jnp.asarray(tallies, jnp.int32))

    tallies = jnp.where(number % 4 == 0, named(packed, number // 4), named(ordinary, number - number // 4 - 1))
    mixed = jax.random.permutation(jax.random.fold_in(own, 3), number_of)
    donor, sink = mixed[0:number_of // 2 * 2:2], mixed[1:number_of // 2 * 2:2]
    slack = jnp.minimum(tallies[donor] - 1, limit - tallies[sink]) // 2
    slack = jnp.where((donor == ranking[0]) | (sink == ranking[0]) | (tallies[sink] == 0), 0, jnp.maximum(slack, 0))
    moved = jax.random.randint(jax.random.fold_in(own, 4), (number_of // 2,), 0, 1 << 20) % (slack + 1)
    tallies = tallies.at[donor].add(-moved).at[sink].add(moved)
    labels = jnp.searchsorted(jnp.cumsum(tallies), jnp.arange(rows * top), side="right").astype(jnp.int32)
    grid = labels.reshape(top, rows).T
    grid = grid[jax.random.permutation(jax.random.fold_in(own, 1), rows)]
    rotation = jax.random.randint(jax.random.fold_in(own, 2), (rows, 1), 0, top)
    return jnp.take_along_axis(grid, (jnp.arange(top)[None, :] + rotation) % top, axis=1)


def shares(amount, total, bound, skew, full):
    loads = [(1 << 20) // math.isqrt(standing ** skew) + 1 for standing in range(1, amount + 1)]
    largest = bound if full else min(bound, max(-(-total // amount), total * loads[0] // sum(loads)))
    least = 1 if total - largest >= amount - 1 else 0
    given, rest = [largest] + [least] * (amount - 1), total - largest - least * (amount - 1)
    while rest > 0:
        free = [i for i in range(1, amount) if given[i] < largest] or [i for i in range(1, amount) if given[i] < bound]
        whole, left = sum([loads[i] for i in free]), rest
        for i in free:
            extra = min(bound - given[i], max(1, left * loads[i] // whole), rest)
            given[i] = given[i] + extra
            rest = rest - extra
    return np.array(given)


def scatter_about(stream_key, shape, scale, bound, cuts=(), held_as=jnp.bfloat16):
    drawn = jax.random.normal(stream_key, shape, jnp.float32) * scale
    if len(cuts) > 0:
        drawn = block_scale(stream_key, shape, cuts, -0.22, 0.18) * drawn
    return jnp.clip(drawn, min=-bound, max=bound).astype(held_as)


def setup_inputs(seed: int = 0) -> dict:
    key_list = jax.random.split(jax.random.key(seed), 7)
    populations = draw_populations(jax.random.fold_in(key_list[6], 71), 0)
    marker_owner_keys = jax.random.split(jax.random.fold_in(key_list[1], 1), MARKERS // MDEV)
    marker_owner_turns = jax.random.permutation(jax.random.fold_in(key_list[1], 3), MARKERS // MDEV)
    marker_owner = jax.vmap(lambda own, number: shared_out(jax.random.fold_in(key_list[1], 2), own, number, MDEV, N_GZ, 1, CAP, 2))(marker_owner_keys, marker_owner_turns).reshape((MARKERS, 1))
    marker_cell = draw_marker_cell(jax.random.fold_in(key_list[6], 71), 0)
    marker_frac = jnp.clip(1.0 * jax.random.uniform(key_list[3], (3, MARKERS), jnp.float32) ** block_scale(key_list[3], (3, MARKERS), ((1, 1024),), -0.2, 0.2), 0.0, 1.0)
    marker_speed = scatter_about(key_list[4], (3, MARKERS), 0.05, 0.2, ((1, 1024),), jnp.float32)
    marker_count = draw_marker_count(jax.random.fold_in(key_list[6], 71), 0)
    return {"populations": populations, "marker_owner": marker_owner, "marker_cell": marker_cell, "marker_frac": marker_frac, "marker_speed": marker_speed, "marker_count": marker_count}


velocity_table = ((0, 0, 0), (1, 0, 0), (-1, 0, 0), (0, 1, 0), (0, -1, 0), (0, 0, 1), (0, 0, -1), (1, 1, 0), (-1, -1, 0), (1, -1, 0), (-1, 1, 0), (1, 0, 1), (-1, 0, -1), (1, 0, -1), (-1, 0, 1), (0, 1, 1), (0, -1, -1), (0, 1, -1), (0, -1, 1))
weight_table = (1.0 / 3.0,) + (1.0 / 18.0,) * 6 + (1.0 / 36.0,) * 12
opposite = (0, 2, 1, 4, 3, 6, 5, 8, 7, 10, 9, 12, 11, 14, 13, 16, 15, 18, 17)
stress_pairs = ((0, 0), (1, 1), (2, 2), (0, 1), (0, 2), (1, 2))
tau_base = 0.52
smag_const = 0.17
ref_speed = 0.05

def moments(pops):
    density = pops[0]
    for member in range(1, 19):
        density = density + pops[member]
    momentum = [jnp.zeros_like(density) for axis_no in range(3)]
    for member in range(19):
        for axis_no in range(3):
            component = velocity_table[member][axis_no]
            if component != 0:
                momentum[axis_no] = momentum[axis_no] + component * pops[member]
    return (density, jnp.stack([part / density for part in momentum]))

def projected(member, speeds):
    total = jnp.zeros_like(speeds[0])
    for axis_no in range(3):
        component = velocity_table[member][axis_no]
        if component != 0:
            total = total + component * speeds[axis_no]
    return total

def equilibrium(member, density, speeds, speed_sq):
    along = projected(member, speeds)
    return weight_table[member] * density * (1.0 + 3.0 * along + 4.5 * along * along - 1.5 * speed_sq)

def collide(pops, density, velocity, force):
    speeds = [velocity[0], velocity[1], velocity[2]]
    speed_sq = speeds[0] * speeds[0] + speeds[1] * speeds[1] + speeds[2] * speeds[2]
    stress = [jnp.zeros_like(density) for pair_no in range(6)]
    for member in range(19):
        excess = pops[member] - equilibrium(member, density, speeds, speed_sq)
        for pair_no in range(6):
            first, second = stress_pairs[pair_no]
            product = velocity_table[member][first] * velocity_table[member][second]
            if product != 0:
                stress[pair_no] = stress[pair_no] + product * excess
    norm_sq = stress[0] * stress[0] + stress[1] * stress[1] + stress[2] * stress[2]
    norm_sq = norm_sq + 2.0 * (stress[3] * stress[3] + stress[4] * stress[4] + stress[5] * stress[5])
    factor = 18.0 * math.sqrt(2.0) * smag_const * smag_const
    relax = 0.5 * (tau_base + jnp.sqrt(tau_base * tau_base + factor * jnp.sqrt(norm_sq) / density))
    shifted = [speeds[axis_no] + relax * force[axis_no] / density for axis_no in range(3)]
    shifted_sq = shifted[0] * shifted[0] + shifted[1] * shifted[1] + shifted[2] * shifted[2]
    result = []
    for member in range(19):
        target = equilibrium(member, density, shifted, shifted_sq)
        result.append(pops[member] - (pops[member] - target) / relax)
    return jnp.stack(result)

def stencil(base_x, base_y, base_z, fracs, planes, size_y, size_z):
    along_x = (1.0 - fracs[0], fracs[0])
    along_y = (1.0 - fracs[1], fracs[1])
    along_z = (1.0 - fracs[2], fracs[2])
    corners = []
    for step_x in range(2):
        for step_y in range(2):
            for step_z in range(2):
                weight = along_x[step_x] * along_y[step_y] * along_z[step_z]
                place = ((base_x + step_x) % planes * size_y + base_y + step_y) * size_z + base_z + step_z
                corners.append((place.astype(jnp.int32), weight))
    return corners

def interpolate(flat_velocity, corners):
    total = corners[0][1] * flat_velocity[:, corners[0][0]]
    for place, weight in corners[1:]:
        total = total + weight * flat_velocity[:, place]
    return total

def spread(force, corners, cells):
    field = jnp.zeros((3, cells), jnp.float32)
    for place, weight in corners:
        field = field.at[:, place].add(weight * force)
    return field

def stream_global(post):
    size_y = post.shape[2]
    rows = jnp.arange(size_y, dtype=jnp.int32)[None, :, None]
    result = []
    for member in range(19):
        shift_x, shift_y, shift_z = velocity_table[member]
        moved = jnp.roll(post[member], (shift_x, shift_y, shift_z), (0, 1, 2))
        if shift_y == 1:
            moved = jnp.where(rows == 0, post[opposite[member]], moved)
        if shift_y == -1:
            moved = jnp.where(rows == size_y - 1, post[opposite[member]], moved)
        result.append(moved)
    return jnp.stack(result)

def reference(populations, marker_owner, marker_cell, marker_frac, marker_speed, marker_count):
    marker_ids = jnp.arange(MARKERS, dtype=jnp.int32)
    device = marker_ids // MDEV
    row_gy = device // N_GZ
    live = (marker_ids % MDEV < marker_count[device]).astype(jnp.float32)
    owner = marker_owner[:, 0]
    base_y = row_gy * CY + marker_cell[1]
    base_z = owner * CZ + marker_cell[2]
    corners = stencil(marker_cell[0], base_y, base_z, marker_frac, X, NY, NZ)
    pops = populations
    force = jnp.zeros((3, MARKERS), jnp.float32)
    for step_no in range(STEPS):
        density, velocity = moments(pops)
        flat_velocity = velocity.reshape(3, -1)
        sampled = interpolate(flat_velocity, corners)
        force = live * (marker_speed - sampled)
        field = spread(force, corners, flat_velocity.shape[1]).reshape(velocity.shape)
        post = collide(pops, density, velocity, field)
        pops = stream_global(post)
    return (pops, force / ref_speed)
```

```python
import math

import jax
import jax.numpy as jnp
from jax import lax
from jax.experimental import pallas as pl
from jax.experimental.pallas import tpu as pltpu
from jax.sharding import PartitionSpec as P

INTERPRET = False

velocity_table = (
    (0, 0, 0),
    (1, 0, 0),
    (-1, 0, 0),
    (0, 1, 0),
    (0, -1, 0),
    (0, 0, 1),
    (0, 0, -1),
    (1, 1, 0),
    (-1, -1, 0),
    (1, -1, 0),
    (-1, 1, 0),
    (1, 0, 1),
    (-1, 0, -1),
    (1, 0, -1),
    (-1, 0, 1),
    (0, 1, 1),
    (0, -1, -1),
    (0, 1, -1),
    (0, -1, 1),
)
opposite = (0, 2, 1, 4, 3, 6, 5, 8, 7, 10, 9, 12, 11, 14, 13, 16, 15, 18, 17)
rising = tuple(i for i in range(19) if velocity_table[i][1] == 1)
falling = tuple(i for i in range(19) if velocity_table[i][1] == -1)
tau_base = 0.52
smag_const = 0.17
ref_speed = 0.05

PLANES = 4
ROWS = 8
LANES = 128
WIDE = 256
HALO = 4
CAP = 24
GROUP = 8
WORDS = 9
SPAN = GROUP * WORDS
OWN_GROUPS = CAP // GROUP
DUP_GROUPS = 2 * CAP // GROUP
GROUPS = OWN_GROUPS + DUP_GROUPS
MESSAGE = 768
BLOCK = 256

f32 = jnp.float32
bf16 = jnp.bfloat16


def iota(shape, dim):
    return lax.broadcasted_iota(jnp.int32, shape, dim)


def split_two(value):
    high = value.astype(bf16)
    return high, (value - high.astype(f32)).astype(bf16)


def call(kernel, out_shape, args, in_specs=None, out_specs=None, scratch=()):
    vmem = pl.BlockSpec(memory_space=pltpu.VMEM)
    single = not isinstance(out_shape, (list, tuple))
    return pl.pallas_call(
        kernel,
        out_shape=out_shape,
        in_specs=in_specs or [vmem] * len(args),
        out_specs=out_specs or (vmem if single else [vmem] * len(out_shape)),
        scratch_shapes=list(scratch),
        compiler_params=pltpu.CompilerParams(vmem_limit_bytes=32 * 1024 * 1024),
        interpret=INTERPRET,
    )(*args)


def edge_kernel(pops_ref, out_ref):
    lane = iota((ROWS, LANES), 1)
    for tile in range(5):
        total = jnp.zeros((ROWS, LANES), f32)
        for place in range(16):
            item = tile * 16 + place
            if item >= 19 * PLANES:
                break
            moved = pltpu.roll(pops_ref[item // PLANES, item % PLANES], HALO + 8 * place, 1)
            total = jnp.where(lane // 8 == place, moved, total)
        out_ref[:, tile * LANES : (tile + 1) * LANES] = total


def pack_kernel(count_ref, owner_ref, cell_ref, frac_ref, speed_ref, send_ref, rank_ref):
    owners, markers = send_ref.shape[0], owner_ref.shape[1]
    member = iota((1, markers), 1)
    live = member < count_ref[0]
    owner = jnp.where(live, owner_ref[...], -1)
    base_z = cell_ref[2:3, :]
    upper = base_z >= LANES - HALO
    lower = base_z <= HALO - 2
    twin = jnp.where(
        upper, jnp.where(owner == owners - 1, 0, owner + 1), jnp.where(owner == 0, owners - 1, owner - 1)
    )
    twin = jnp.where(live & (upper | lower), twin, -1)
    device = iota((owners, markers), 0)
    own_hit = (device == owner).astype(f32)
    twin_hit = (device == twin).astype(f32)
    hits = jnp.concatenate([own_hit, twin_hit], 0)
    below = (iota((LANES, LANES), 0) < iota((LANES, LANES), 1)).astype(bf16)
    before = jnp.zeros((2 * owners, 1), f32)
    ranks = []
    for start in range(0, markers, LANES):
        part = hits[:, start : start + LANES]
        inner = jnp.dot(part.astype(bf16), below, preferred_element_type=f32)
        picked = part * (inner + before)
        ranks.append(
            jnp.concatenate(
                [
                    jnp.sum(picked[:owners], 0, keepdims=True),
                    jnp.sum(picked[owners:], 0, keepdims=True),
                ],
                0,
            )
        )
        before = before + jnp.sum(part, 1, keepdims=True)
    rank = jnp.concatenate(ranks, 1)
    rank_ref[...] = rank[0:1, :]
    row = iota((8, markers), 0)

    value = jnp.where(row == 0, cell_ref[0:1, :] + 1, jnp.where(row == 1, cell_ref[1:2, :], base_z))
    value = value.astype(f32)
    for number in range(3):
        value = jnp.where(row == 3 + number, frac_ref[number : number + 1, :], value)
    for number in range(2):
        value = jnp.where(row == 6 + number, speed_ref[number : number + 1, :], value)
    high, low = split_two(value)
    high, low = high.astype(f32), low.astype(f32)

    last = speed_ref[2:3, :]
    last_high, last_low = split_two(jnp.broadcast_to(last, (8, markers)))
    last_high, last_low = last_high.astype(f32), last_low.astype(f32)

    def packed(hit, which, first, groups):
        place = rank[which : which + 1, :]
        rows_high, rows_low = [], []
        for group in range(groups):
            for slot in range(GROUP):
                match = place == first + (group * GROUP + slot)
                rows_high.append(jnp.where(match, high, 0.0))
                rows_low.append(jnp.where(match, low, 0.0))
            match = place == (iota((8, markers), 0) + (first + group * GROUP)).astype(f32)
            rows_high.append(jnp.where(match, last_high, 0.0))
            rows_low.append(jnp.where(match, last_low, 0.0))
        dims = (((1,), (1,)), ((), ()))
        left = hit.astype(bf16)
        return lax.dot_general(
            left, jnp.concatenate(rows_high, 0).astype(bf16), dims, preferred_element_type=f32
        ) + lax.dot_general(
            left, jnp.concatenate(rows_low, 0).astype(bf16), dims, preferred_element_type=f32
        )

    own = packed(own_hit, 0, 0, OWN_GROUPS)
    near = packed(twin_hit, 1, 0, 1)
    head = OWN_GROUPS * SPAN
    send_ref[...] = jnp.zeros(send_ref.shape, f32)
    send_ref[:, 0:head] = own
    send_ref[:, head : head + SPAN] = near

    @pl.when(jnp.max(rank[1:2, :]) > GROUP - 0.5)
    def _():
        for group in range(1, DUP_GROUPS):
            send_ref[:, head + group * SPAN : head + (group + 1) * SPAN] = packed(
                twin_hit, 1, group * GROUP, 1
            )


def unpacked(columns, group):
    first = group * SPAN
    halves, lasts = [], []
    for half in range(2):
        total, tail = None, None
        for part in range(4):
            slot = half * 4 + part
            piece = columns[first + 8 * slot : first + 8 * slot + 8, :]
            extra = columns[first + 64 + slot : first + 65 + slot, :]
            extra = jnp.broadcast_to(extra, (8, LANES))
            if part:
                piece = pltpu.roll(piece, 32 * part, 1)
                extra = pltpu.roll(extra, 32 * part, 1)
            total = piece if total is None else total + piece
            tail = extra if tail is None else tail + extra
        halves.append(total)
        lasts.append(tail)
    return jnp.concatenate([jnp.concatenate(halves, 1), jnp.concatenate(lasts, 1)], 0)


def marker_block(mark, field):
    count = mark.shape[1]
    base_x, base_y, base_z = mark[0:1, :], mark[1:2, :], mark[2:3, :]
    frac_x, frac_y, frac_z = mark[3:4, :], mark[4:5, :], mark[5:6, :]
    speeds = (mark[6:7, :], mark[7:8, :], mark[8:9, :])
    row = iota((ROWS, count), 0).astype(f32)
    along_y = jnp.where(row == base_y, 1.0 - frac_y, jnp.where(row == base_y + 1.0, frac_y, 0.0))
    weights = []
    next_x = jnp.where(base_x == float(PLANES), 0.0, base_x)
    for plane in range(PLANES):
        weight = jnp.where(base_x == plane + 1.0, 1.0 - frac_x, 0.0)
        weight = jnp.where((base_x > 0.5) & (next_x == float(plane)), frac_x, weight)
        weights.append(along_y * weight)
    spot = jnp.where(iota((LANES, count), 0).astype(f32) == base_z, 1.0, 0.0).astype(bf16)
    high, low = split_two(field)
    shifted = pltpu.roll(field, LANES - 1, 1)
    next_high, next_low = split_two(shifted)
    left = jnp.concatenate(
        [jnp.concatenate([high, low], 1), jnp.concatenate([next_high, next_low], 1)], 0
    )
    near = jnp.dot(left, jnp.concatenate([spot, spot], 0), preferred_element_type=f32)
    forces, spreads = [], []
    for axis_no in range(3):
        total = None
        for plane in range(PLANES):
            at = axis_no * 32 + plane * 8
            here, there = near[at : at + 8, :], near[96 + at : 96 + at + 8, :]
            value = weights[plane] * (here + frac_z * (there - here))
            total = value if total is None else total + value
        force = speeds[axis_no] - jnp.sum(total, 0, keepdims=True)
        forces.append(force)
        for plane in range(PLANES):
            spreads.append(weights[plane] * force)
    spreads = jnp.concatenate(spreads, 0)
    ahead = spreads * frac_z
    high, low = split_two(spreads - ahead)
    ahead_high, ahead_low = split_two(ahead)
    sums = lax.dot_general(
        jnp.concatenate([high, low, ahead_high, ahead_low], 0),
        spot,
        (((1,), (1,)), ((), ())),
        preferred_element_type=f32,
    )
    here = sums[0:96] + sums[96:192]
    there = sums[192:288] + sums[288:384]
    return forces, here + pltpu.roll(there, 1, 1)


def marker_pass(field_ref, force_ref, marks_ref, more, returned_ref):
    field = field_ref[:, 0:LANES]
    total = jnp.zeros((96, LANES), f32)
    kept = []
    for group in range(OWN_GROUPS):
        forces, sums = marker_block(marks_ref[:, group * BLOCK : (group + 1) * BLOCK], field)
        total = total + sums
        kept.append(forces)
    force_ref[:, 0:LANES] = total
    start = OWN_GROUPS * BLOCK
    _, sums = marker_block(marks_ref[:, start : start + BLOCK], field_ref[:, LANES:WIDE])
    force_ref[:, LANES:WIDE] = sums

    @pl.when(more)
    def _():
        def one(group, carry):
            at = pl.multiple_of(group * BLOCK, BLOCK)
            _, sums = marker_block(marks_ref[:, pl.ds(at, BLOCK)], field_ref[:, LANES:WIDE])
            force_ref[:, LANES:WIDE] = force_ref[:, LANES:WIDE] + sums
            return carry

        lax.fori_loop(OWN_GROUPS + 1, GROUPS, one, 0)

    if returned_ref is not None:
        row = iota((8, LANES), 0)
        pieces = []
        for forces in kept:
            pair = jnp.zeros((8, LANES), f32)
            for half in range(2):
                for axis_no in range(3):
                    value = forces[axis_no][:, half * LANES : (half + 1) * LANES]
                    pair = jnp.where(row == 4 * half + axis_no, value, pair)
            for part in range(4):
                pieces.append(pltpu.roll(pair, LANES - 32 * part, 1) if part else pair)
        pieces.append(jnp.zeros((LANES - 8 * len(pieces), LANES), f32))
        turned = jnp.concatenate(pieces, 0).T
        returned_ref[...] = turned[0:32, :]


def moments_of(pops):
    density = pops[0]
    for member in range(1, 19):
        density = density + pops[member]
    parts = []
    for axis_no in range(3):
        total = None
        for member in range(19):
            component = velocity_table[member][axis_no]
            if component == 1:
                total = pops[member] if total is None else total + pops[member]
        for member in range(19):
            if velocity_table[member][axis_no] == -1:
                total = total - pops[member]
        parts.append(total)
    inverse = 1.0 / density
    return density, [part * inverse for part in parts]


def moment_pass(read, field_ref, density_ref, reach):
    lane = iota((ROWS, WIDE), 1)
    known = (lane < LANES + reach) | (lane >= WIDE - reach)
    for plane in range(PLANES):
        density, speeds = moments_of([read(member, plane) for member in range(19)])
        density_ref[plane] = density
        for axis_no in range(3):
            at = axis_no * 32 + plane * 8
            field_ref[at : at + 8, :] = jnp.where(known, speeds[axis_no], 0.0)


def collide_pass(read, field_ref, density_ref, force_ref, post_ref, up_ref, down_ref):
    factor = 18.0 * math.sqrt(2.0) * smag_const * smag_const
    for plane in range(PLANES):
        pops = [read(member, plane) for member in range(19)]
        density = density_ref[plane]
        speeds = [field_ref[a * 32 + plane * 8 : a * 32 + plane * 8 + 8, :] for a in range(3)]
        pulls = [force_ref[a * 32 + plane * 8 : a * 32 + plane * 8 + 8, :] for a in range(3)]
        moved = [density * part for part in speeds]
        pair_sum = [pops[2 * k + 1] + pops[2 * k + 2] for k in range(9)]
        third = density * (1.0 / 3.0)
        xx = pair_sum[0] + pair_sum[3] + pair_sum[4] + pair_sum[5] + pair_sum[6]
        yy = pair_sum[1] + pair_sum[3] + pair_sum[4] + pair_sum[7] + pair_sum[8]
        zz = pair_sum[2] + pair_sum[5] + pair_sum[6] + pair_sum[7] + pair_sum[8]
        xx = xx - third - moved[0] * speeds[0]
        yy = yy - third - moved[1] * speeds[1]
        zz = zz - third - moved[2] * speeds[2]
        xy = pair_sum[3] - pair_sum[4] - moved[0] * speeds[1]
        xz = pair_sum[5] - pair_sum[6] - moved[0] * speeds[2]
        yz = pair_sum[7] - pair_sum[8] - moved[1] * speeds[2]
        norm_sq = xx * xx + yy * yy + zz * zz + 2.0 * (xy * xy + xz * xz + yz * yz)
        inverse = 1.0 / density
        relax = 0.5 * (
            tau_base + jnp.sqrt(tau_base * tau_base + factor * jnp.sqrt(norm_sq) * inverse)
        )
        pull = relax * inverse
        shifted = [speeds[a] + pull * pulls[a] for a in range(3)]
        shifted_sq = shifted[0] * shifted[0] + shifted[1] * shifted[1] + shifted[2] * shifted[2]
        rate = 1.0 / relax
        keep = 1.0 - rate
        scale = rate * density
        base = scale * (1.0 - 1.5 * shifted_sq)
        quad = 4.5 * scale
        results = {0: keep * pops[0] + base * (1.0 / 3.0)}
        for pair in range(9):
            plus = 2 * pair + 1
            along = None
            for axis_no in range(3):
                component = velocity_table[plus][axis_no]
                if component == 1:
                    along = shifted[axis_no] if along is None else along + shifted[axis_no]
            for axis_no in range(3):
                if velocity_table[plus][axis_no] == -1:
                    along = along - shifted[axis_no]
            weight = 1.0 / 18.0 if pair < 3 else 1.0 / 36.0
            even = weight * (base + quad * along * along)
            odd = (3.0 * weight) * (scale * along)
            results[plus] = keep * pops[plus] + (even + odd)
            results[plus + 1] = keep * pops[plus + 1] + (even - odd)
        for member in range(19):
            post_ref[member, plane] = results[member]
        for number in range(5):
            for half in range(2):
                at = number * 8 + plane * 2 + half
                lanes = slice(half * LANES, (half + 1) * LANES)
                up_ref[at : at + 1, :] = results[rising[number]][ROWS - 1 : ROWS, lanes]
                down_ref[at : at + 1, :] = results[falling[number]][0:1, lanes]


def streamed(post_ref, below_ref, above_ref, first_wall, last_wall, member, plane):
    shift_x, shift_y, shift_z = velocity_table[member]
    source = (plane - shift_x) % PLANES
    value = post_ref[member, source]
    row = iota((ROWS, WIDE), 0)
    if shift_y == 1:
        at = rising.index(member) * 8 + source * 2
        rim = jnp.concatenate([below_ref[at : at + 1, :], below_ref[at + 1 : at + 2, :]], 1)
        value = jnp.where(row == 0, rim, pltpu.roll(value, 1, 0))
    if shift_y == -1:
        at = falling.index(member) * 8 + source * 2
        rim = jnp.concatenate([above_ref[at : at + 1, :], above_ref[at + 1 : at + 2, :]], 1)
        value = jnp.where(row == ROWS - 1, rim, pltpu.roll(value, ROWS - 1, 0))
    if shift_z:
        value = pltpu.roll(value, shift_z % WIDE, 1)
    if shift_y == 1:
        value = jnp.where(row == first_wall, post_ref[opposite[member], plane], value)
    if shift_y == -1:
        value = jnp.where(row == last_wall, post_ref[opposite[member], plane], value)
    return value


def first_kernel(
    pops_ref, left_ref, right_ref, got_ref, post_ref, up_ref, down_ref, marks_ref, more_ref,
    wide_ref, field_ref, density_ref, force_ref,
):
    lane = iota((ROWS, LANES), 1)
    for tile in range(5):
        lanes = slice(tile * LANES, (tile + 1) * LANES)
        ends = jnp.where(lane % 8 < HALO, left_ref[:, lanes], right_ref[:, lanes])
        for place in range(16):
            item = tile * 16 + place
            if item >= 19 * PLANES:
                break
            member, plane = item // PLANES, item % PLANES
            wide_ref[member, plane, :, 0:LANES] = pops_ref[member, plane]
            wide_ref[member, plane, :, LANES:WIDE] = pltpu.roll(ends, LANES - HALO - 8 * place, 1)

    def read(member, plane):
        return wide_ref[member, plane]

    moment_pass(read, field_ref, density_ref, HALO)
    zeros = jnp.zeros((LANES - 32, LANES), f32)

    def turned(tile):
        return jnp.concatenate([got_ref[:, tile * LANES : (tile + 1) * LANES], zeros], 0).T

    columns = jnp.concatenate([turned(tile) for tile in range(3)], 0)
    for group in range(OWN_GROUPS + 1):
        marks_ref[:, group * BLOCK : (group + 1) * BLOCK] = unpacked(columns, group)
    rest = (OWN_GROUPS + 1) * SPAN
    more = jnp.max(got_ref[:, rest:MESSAGE]) > 0.5
    more_ref[0] = more.astype(jnp.int32)

    @pl.when(more)
    def _():
        every = jnp.concatenate([turned(tile) for tile in range(MESSAGE // LANES)], 0)
        for group in range(OWN_GROUPS + 1, GROUPS):
            marks_ref[:, group * BLOCK : (group + 1) * BLOCK] = unpacked(every, group)

    marker_pass(field_ref, force_ref, marks_ref, more, None)
    collide_pass(read, field_ref, density_ref, force_ref, post_ref, up_ref, down_ref)


def second_kernel(
    wall_ref, more_ref, old_ref, below_ref, above_ref, marks_ref, post_ref, up_ref, down_ref, returned_ref,
    wide_ref, field_ref, density_ref, force_ref,
):
    first_wall, last_wall = wall_ref[0], wall_ref[1]
    for plane in range(PLANES):
        for member in range(19):
            wide_ref[member, plane] = streamed(
                old_ref, below_ref, above_ref, first_wall, last_wall, member, plane
            )

    def read(member, plane):
        return wide_ref[member, plane]

    moment_pass(read, field_ref, density_ref, HALO - 2)
    marker_pass(field_ref, force_ref, marks_ref, more_ref[0] != 0, returned_ref)
    collide_pass(read, field_ref, density_ref, force_ref, post_ref, up_ref, down_ref)


def last_kernel(wall_ref, old_ref, below_ref, above_ref, out_ref):
    first_wall, last_wall = wall_ref[0], wall_ref[1]
    for plane in range(PLANES):
        for member in range(19):
            value = streamed(old_ref, below_ref, above_ref, first_wall, last_wall, member, plane)
            out_ref[member, plane] = value[:, 0:LANES]


def home_kernel(count_ref, owner_ref, rank_ref, back_ref, out_ref):
    owners, markers = back_ref.shape[0], owner_ref.shape[1]
    live = iota((1, markers), 1) < count_ref[0]
    owner = jnp.where(live, owner_ref[...], -1)
    hit = (iota((LANES, markers), 0) == owner).astype(f32)
    turned = jnp.concatenate([back_ref[...], jnp.zeros((LANES - owners, LANES), f32)], 0).T
    found = jnp.dot(turned, hit, precision=lax.Precision.HIGHEST, preferred_element_type=f32)
    rank = rank_ref[...]
    row = iota((8, markers), 0)
    total = jnp.zeros((8, markers), f32)
    for place in range(12):
        slot = ((place // 4) * 8 + place % 4 + (row // 4) * 4).astype(f32)
        total = total + jnp.where(rank == slot, found[place * 8 : place * 8 + 8, :], 0.0)
    out_ref[...] = (total[0:3, :] + total[4:7, :]) / ref_speed


def body(populations, marker_owner, marker_cell, marker_frac, marker_speed, marker_count):
    count_gy, count_gz = lax.axis_size("gy"), lax.axis_size("gz")
    markers = marker_owner.shape[0]
    smem = pl.BlockSpec(memory_space=pltpu.SMEM)
    vmem = pl.BlockSpec(memory_space=pltpu.VMEM)
    shape = jax.ShapeDtypeStruct

    def shifts(axis, value_up, value_down):
        size = lax.axis_size(axis)
        return (
            lax.ppermute(value_up, axis, [(i, (i + 1) % size) for i in range(size)]),
            lax.ppermute(value_down, axis, [((i + 1) % size, i) for i in range(size)]),
        )

    edges = call(edge_kernel, shape((ROWS, 5 * LANES), f32), [populations])
    left, right = shifts("gz", edges, edges)
    owner = marker_owner.reshape(1, markers)
    send, rank = call(
        pack_kernel,
        [shape((count_gz, MESSAGE), f32), shape((1, markers), f32)],
        [marker_count, owner, marker_cell, marker_frac, marker_speed],
        in_specs=[smem] + [vmem] * 4,
    )
    got = lax.all_to_all(send, "gz", split_axis=0, concat_axis=0, tiled=True)
    wide = shape((19, PLANES, ROWS, WIDE), f32)
    face = shape((40, LANES), f32)
    scratch = [
        pltpu.VMEM((19, PLANES, ROWS, WIDE), f32),
        pltpu.VMEM((96, WIDE), f32),
        pltpu.VMEM((PLANES, ROWS, WIDE), f32),
        pltpu.VMEM((96, WIDE), f32),
    ]
    post, up, down, marks, more = call(
        first_kernel,
        [wide, face, face, shape((16, GROUPS * BLOCK), f32), shape((1,), jnp.int32)],
        [populations, left, right, got],
        out_specs=[vmem] * 4 + [smem],
        scratch=scratch,
    )
    row = lax.axis_index("gy")
    walls = jnp.stack([jnp.where(row == 0, 0, -1), jnp.where(row == count_gy - 1, ROWS - 1, -1)])
    walls = walls.astype(jnp.int32)
    below, above = shifts("gy", up, down)
    post, up, down, returned = call(
        second_kernel,
        [wide, face, face, shape((count_gz, LANES), f32)],
        [walls, more, post, below, above, marks],
        in_specs=[smem] * 2 + [vmem] * 4,
        scratch=scratch,
    )
    below, above = shifts("gy", up, down)
    back = lax.all_to_all(returned, "gz", split_axis=0, concat_axis=0, tiled=True)
    pops = call(
        last_kernel,
        shape(populations.shape, f32),
        [walls, post, below, above],
        in_specs=[smem] + [vmem] * 3,
    )
    force = call(
        home_kernel,
        shape((3, markers), f32),
        [marker_count, owner, rank, back],
        in_specs=[smem] + [vmem] * 3,
    )
    return pops, force


def solution(mesh):
    return jax.shard_map(
        body,
        mesh=mesh,
        in_specs=(
            P(None, None, "gy", "gz"),
            P(("gy", "gz"), None),
            P(None, ("gy", "gz")),
            P(None, ("gy", "gz")),
            P(None, ("gy", "gz")),
            P(("gy", "gz")),
        ),
        out_specs=(P(None, None, "gy", "gz"), P(None, ("gy", "gz"))),
        check_vma=False,
    )
```

```python
import math

import jax
import jax.numpy as jnp
from jax import lax
from jax.experimental import pallas as pl
from jax.experimental.pallas import tpu as pltpu
from jax.sharding import PartitionSpec as P

INTERPRET = False

velocity_table = (
    (0, 0, 0),
    (1, 0, 0),
    (-1, 0, 0),
    (0, 1, 0),
    (0, -1, 0),
    (0, 0, 1),
    (0, 0, -1),
    (1, 1, 0),
    (-1, -1, 0),
    (1, -1, 0),
    (-1, 1, 0),
    (1, 0, 1),
    (-1, 0, -1),
    (1, 0, -1),
    (-1, 0, 1),
    (0, 1, 1),
    (0, -1, -1),
    (0, 1, -1),
    (0, -1, 1),
)
opposite = (0, 2, 1, 4, 3, 6, 5, 8, 7, 10, 9, 12, 11, 14, 13, 16, 15, 18, 17)
rising = tuple(i for i in range(19) if velocity_table[i][1] == 1)
falling = tuple(opposite[i] for i in rising)
level = tuple(i for i in range(19) if velocity_table[i][1] == 0)
ahead_z = tuple(i for i in range(19) if velocity_table[i][2] == 1)
back_z = tuple(opposite[i] for i in ahead_z)
tau_base = 0.52
smag_const = 0.17
ref_speed = 0.05

PLANES = 4
ROWS = 8
LANES = 128
SLOTS = 24
SHARE = 32
FEW = 4
SPARE = SLOTS - FEW
FIRST_SPARE = SHARE
FIRST_Z = SHARE + 2 * SPARE
FIRST_RIM = 76
FIRST_FACE = SHARE
RIM_WORDS = 13
AT_SPEED, AT_POPS, AT_NEXT, AT_MARKS, AT_Z, FACE_ROWS = 0, 12, 68, 88, 152, 160

f32 = jnp.float32
bf16 = jnp.bfloat16


def iota(shape, dim):
    return lax.broadcasted_iota(jnp.int32, shape, dim)


def roll(value, shift, axis):
    shift = shift % value.shape[axis]
    return pltpu.roll(value, shift, axis) if shift else value


def split_two(value):
    high = value.astype(bf16)
    return high, (value - high.astype(f32)).astype(bf16)


def call(kernel, out_shape, args, in_specs, scratch=()):
    vmem = pl.BlockSpec(memory_space=pltpu.VMEM)
    return pl.pallas_call(
        kernel,
        out_shape=out_shape,
        in_specs=in_specs,
        out_specs=[vmem] * len(out_shape),
        scratch_shapes=list(scratch),
        compiler_params=pltpu.CompilerParams(vmem_limit_bytes=32 * 1024 * 1024),
        interpret=INTERPRET,
    )(*args)


def moments_of(pops):
    density = pops[0]
    for member in range(1, 19):
        density = density + pops[member]
    parts = []
    for axis_no in range(3):
        total = None
        for member in range(19):
            if velocity_table[member][axis_no] == 1:
                total = pops[member] if total is None else total + pops[member]
        for member in range(19):
            if velocity_table[member][axis_no] == -1:
                total = total - pops[member]
        parts.append(total)
    inverse = 1.0 / density
    return density, [part * inverse for part in parts]


def relax_of(pops, density, speeds):
    factor = 18.0 * math.sqrt(2.0) * smag_const * smag_const
    moved = [density * part for part in speeds]
    pair = [pops[2 * k + 1] + pops[2 * k + 2] for k in range(9)]
    third = density * (1.0 / 3.0)
    xx = pair[0] + pair[3] + pair[4] + pair[5] + pair[6] - third - moved[0] * speeds[0]
    yy = pair[1] + pair[3] + pair[4] + pair[7] + pair[8] - third - moved[1] * speeds[1]
    zz = pair[2] + pair[5] + pair[6] + pair[7] + pair[8] - third - moved[2] * speeds[2]
    xy = pair[3] - pair[4] - moved[0] * speeds[1]
    xz = pair[5] - pair[6] - moved[0] * speeds[2]
    yz = pair[7] - pair[8] - moved[1] * speeds[2]
    norm_sq = xx * xx + yy * yy + zz * zz + 2.0 * (xy * xy + xz * xz + yz * yz)
    return 0.5 * (tau_base + jnp.sqrt(tau_base * tau_base + factor * jnp.sqrt(norm_sq) / density))


def along_of(member, speeds):
    total = None
    for axis_no in range(3):
        if velocity_table[member][axis_no] == 1:
            total = speeds[axis_no] if total is None else total + speeds[axis_no]
    for axis_no in range(3):
        if velocity_table[member][axis_no] == -1:
            total = total - speeds[axis_no]
    return total


def relaxed(pops, density, speeds, relax, pulls):
    pull = relax / density
    shifted = [speeds[a] + pull * pulls[a] for a in range(3)]
    shifted_sq = shifted[0] * shifted[0] + shifted[1] * shifted[1] + shifted[2] * shifted[2]
    rate = 1.0 / relax
    keep = 1.0 - rate
    scale = rate * density
    base = scale * (1.0 - 1.5 * shifted_sq)
    quad = 4.5 * scale
    results = [keep * pops[0] + base * (1.0 / 3.0)]
    for pair in range(9):
        plus = 2 * pair + 1
        along = along_of(plus, shifted)
        weight = 1.0 / 18.0 if pair < 3 else 1.0 / 36.0
        even = weight * (base + quad * along * along)
        odd = (3.0 * weight) * (scale * along)
        results.append(keep * pops[plus] + (even + odd))
        results.append(keep * pops[plus + 1] + (even - odd))
    return results


def along_x(mark, plane):
    base, frac = mark[0:1, :], mark[2:3, :]
    following = jnp.where(base == float(PLANES), 0.0, base)
    weight = jnp.where(base - 1.0 == plane, 1.0 - frac, 0.0)
    return jnp.where((base > 0.5) & (following == plane), frac, weight)


def block_weights(mark):
    base, frac = mark[1:2, :], mark[3:4, :]
    row = iota((ROWS, mark.shape[1]), 0).astype(f32)
    along_y = jnp.where(row == base, 1.0 - frac, jnp.where(row == base + 1.0, frac, 0.0))
    return [along_y * along_x(mark, float(plane)) for plane in range(PLANES)]


def spots(base_z):
    count = base_z.shape[1]
    return jnp.where(iota((LANES, count), 0).astype(f32) == base_z, 1.0, 0.0).astype(bf16)


def pairs_of(field):
    high, low = split_two(field)
    next_high, next_low = split_two(roll(field, -1, 1))
    return jnp.concatenate(
        [jnp.concatenate([high, low], 1), jnp.concatenate([next_high, next_low], 1)], 0
    )


def gathered(pairs, spot):
    return jnp.dot(pairs, jnp.concatenate([spot, spot], 0), preferred_element_type=f32)


def scattered(here, there, spot):
    size = here.shape[0]
    high, low = split_two(here)
    next_high, next_low = split_two(there)
    sums = lax.dot_general(
        jnp.concatenate([high, low, next_high, next_low], 0),
        spot,
        (((1,), (1,)), ((), ())),
        preferred_element_type=f32,
    )
    first = sums[0:size] + sums[size : 2 * size]
    second = sums[2 * size : 3 * size] + sums[3 * size :]
    return first + roll(second, 1, 1)


def forces_of(mark, weights, here, there):
    frac = mark[4:5, :]
    forces, spreads = [], []
    for axis_no in range(3):
        total = None
        for plane in range(PLANES):
            at = axis_no * PLANES + plane
            value = weights[plane] * (here[at] + frac * (there[at] - here[at]))
            total = value if total is None else total + value
        force = mark[5 + axis_no : 6 + axis_no, :] - jnp.sum(total, 0, keepdims=True)
        forces.append(force)
        for plane in range(PLANES):
            spreads.append(weights[plane] * force)
    return forces, spreads


def first_kernel(
    info_ref, count_ref, owner_hbm, cell_hbm, frac_hbm, speed_hbm, pops_hbm,
    send_ref, rank_ref, field_ref, density_ref, relax_ref,
    owner_ref, cell_ref, frac_ref, speed_ref, pops_ref, sems,
):
    copies = [
        pltpu.make_async_copy(source, target, sems.at[number])
        for number, (source, target) in enumerate(
            [
                (owner_hbm, owner_ref),
                (cell_hbm, cell_ref),
                (frac_hbm, frac_ref),
                (speed_hbm, speed_ref),
                (pops_hbm, pops_ref),
            ]
        )
    ]
    for copy in copies:
        copy.start()
    for copy in copies:
        copy.wait()
    owners, markers = send_ref.shape[0], owner_ref.shape[1]
    live = iota((1, markers), 1) < count_ref[0]
    owner = jnp.where(live, owner_ref[...], -1)
    base_z = cell_ref[2:3, :]
    upper, lower = base_z == LANES - 2, base_z == 0
    twin = jnp.where(
        upper,
        jnp.where(owner == owners - 1, 0, owner + 1),
        jnp.where(owner == 0, owners - 1, owner - 1),
    )
    twin = jnp.where(live & (upper | lower), twin, -1)
    hit = iota((owners, markers), 0) == owner
    hits = jnp.concatenate(
        [hit.astype(f32), (hit & upper).astype(f32), (hit & lower).astype(f32)], 0
    )
    below = (iota((LANES, LANES), 0) < iota((LANES, LANES), 1)).astype(bf16)
    before = jnp.zeros((3 * owners, 1), f32)
    ranks = [[], [], []]
    for start in range(0, markers, LANES):
        part = hits[:, start : start + LANES]
        inner = jnp.dot(part.astype(bf16), below, preferred_element_type=f32)
        picked = part * (inner + before)
        for kind in range(3):
            ranks[kind].append(
                jnp.sum(picked[kind * owners : (kind + 1) * owners], 0, keepdims=True)
            )
        before = before + jnp.sum(part, 1, keepdims=True)
    rank, rank_up, rank_low = [jnp.concatenate(kind, 1) for kind in ranks]
    rank_ref[...] = rank
    lane_up = jnp.where(rank_up < FEW, SLOTS + rank_up, FIRST_SPARE - FEW + rank_up)
    lane_low = jnp.where(
        rank_low < FEW, SLOTS + FEW + rank_low, FIRST_SPARE + SPARE - FEW + rank_low
    )
    lane_twin = jnp.where(upper, lane_up, lane_low)
    lane_z = FIRST_Z + jnp.where(rank >= 16.0, 2.0, jnp.where(rank >= 8.0, 1.0, 0.0))
    slot_z = rank - 8.0 * (lane_z - FIRST_Z)
    lane = iota((LANES, markers), 0).astype(f32)
    spot_own = (lane == rank).astype(bf16)
    spot_twin = (lane == lane_twin).astype(bf16)
    spot_z = (lane == lane_z).astype(bf16)
    row = iota((8, markers), 0)
    words = jnp.where(row == 0, cell_ref[0:1, :] + 1, cell_ref[1:2, :]).astype(f32)
    for number in range(3):
        words = jnp.where(row == 2 + number, frac_ref[number : number + 1, :], words)
        words = jnp.where(row == 5 + number, speed_ref[number : number + 1, :], words)
    high, low = split_two(words)
    high, low = high.astype(f32), low.astype(f32)
    words_z = jnp.where(row.astype(f32) == slot_z, base_z.astype(f32), 0.0)

    def to_owners(value, target):
        rows = [jnp.where(target == number, value, 0.0) for number in range(owners)]
        return jnp.concatenate(rows, 0).astype(bf16)

    def placed(left, spot):
        return lax.dot_general(left, spot, (((1,), (1,)), ((), ())), preferred_element_type=f32)

    tiles = placed(to_owners(high, owner), spot_own) + placed(to_owners(low, owner), spot_own)
    tiles = tiles + placed(to_owners(high, twin), spot_twin)
    tiles = tiles + placed(to_owners(low, twin), spot_twin)
    tiles = tiles + placed(to_owners(words_z, owner), spot_z)
    send_ref[...] = tiles.reshape(owners, 8, LANES)

    lane = iota((ROWS, LANES), 1)
    to_right, to_left = jnp.zeros((ROWS, LANES), f32), jnp.zeros((ROWS, LANES), f32)
    for plane in range(PLANES):
        pops = [pops_ref[member, plane] for member in range(19)]
        density, speeds = moments_of(pops)
        relax = relax_of(pops, density, speeds)
        density_ref[plane] = density
        relax_ref[plane] = relax
        for axis_no in range(3):
            at = axis_no * 32 + plane * 8
            field_ref[at : at + 8, :] = speeds[axis_no]
        common = [density, *speeds, relax]
        for word in range(RIM_WORDS):
            place = FIRST_RIM + word * PLANES + plane
            if word < 5:
                right, left, shift = common[word], common[word], 0
            elif word < 10:
                right, left, shift = pops[ahead_z[word - 5]], pops[back_z[word - 5]], 0
            else:
                right, left, shift = speeds[word - 10], speeds[word - 10], 1
            here = lane == place
            to_right = jnp.where(here, roll(right, place - (LANES - 1) + shift, 1), to_right)
            to_left = jnp.where(here, roll(left, place - shift, 1), to_left)
    left, right = info_ref[0], info_ref[1]
    send_ref[left] = send_ref[left] + to_left
    send_ref[right] = send_ref[right] + to_right


def second_kernel(
    info_ref, pops_ref, got_ref, field_ref, density_ref, relax_ref,
    next_ref, up_ref, down_ref,
    post_ref, near_ref, far_ref, left_ref, right_ref,
):
    left, right = info_ref[0], info_ref[1]
    lane = iota((ROWS, LANES), 1)
    row = iota((ROWS, LANES), 0)
    sources = got_ref.shape[0]

    chosen = iota((LANES, LANES), 1) % SHARE
    chosen = (iota((LANES, LANES), 0) == FIRST_Z + chosen // 8) & (chosen < SLOTS)
    every_z = jnp.dot(
        got_ref[...].reshape(sources * 8, LANES).astype(bf16),
        chosen.astype(bf16),
        preferred_element_type=f32,
    )
    marks, bases = [], []
    for tile in range(sources // 4):
        words, place = None, None
        for part in range(4):
            source = tile * 4 + part
            value = roll(got_ref[source], SHARE * part, 1)
            spot = every_z[source * 8 : source * 8 + 8, :]
            if part:
                words = jnp.where(lane // SHARE == part, value, words)
                place = jnp.where(lane // SHARE == part, spot, place)
            else:
                words, place = value, spot
        place = jnp.sum(jnp.where(lane % 8 == row, place, 0.0), 0, keepdims=True)
        place = jnp.where(iota((1, LANES), 1) % SHARE < SLOTS, place, -5.0)
        marks.append(words)
        bases.append(place)
        for ref in (up_ref, down_ref):
            ref[AT_MARKS + tile * 8 : AT_MARKS + tile * 8 + 8, :] = words
            ref[AT_Z + tile : AT_Z + tile + 1, :] = place

    ends = jnp.where(lane >= FIRST_RIM, got_ref[left], roll(got_ref[right], 64, 1))
    rim = [roll(ends, -(FIRST_RIM + PLANES * word), 1) for word in range(RIM_WORDS)]

    def spread_lane(value, at):
        return jnp.broadcast_to(value[:, at : at + 1], (ROWS, LANES))

    for axis_no in range(3):
        for plane in range(PLANES):
            at = axis_no * PLANES + plane
            near_ref[at] = spread_lane(rim[10 + axis_no], plane)
            near_ref[12 + at] = spread_lane(rim[1 + axis_no], 64 + plane)
            far_ref[at] = spread_lane(rim[1 + axis_no], plane)
            far_ref[12 + at] = spread_lane(rim[10 + axis_no], 64 + plane)
    left_ref[...] = jnp.zeros_like(left_ref)
    right_ref[...] = jnp.zeros_like(right_ref)

    def twins(mark, of_left, of_right):
        def both(ref):
            return [
                jnp.where(of_left, ref[at], jnp.where(of_right, ref[12 + at], 0.0))
                for at in range(12)
            ]

        return both(near_ref), both(far_ref)

    def keep_twins(mark, spreads, of_left, of_right):
        frac = mark[4:5, :]
        for at in range(12):
            ahead = spreads[at] * frac
            rows = slice(at * 8, at * 8 + 8)
            left_ref[rows, :] = left_ref[rows, :] + jnp.where(of_left, ahead, 0.0)
            right_ref[rows, :] = right_ref[rows, :] + jnp.where(of_right, spreads[at] - ahead, 0.0)

    of_left = (lane % SHARE >= SLOTS) & (lane % SHARE < SLOTS + FEW)
    of_right = lane % SHARE >= SLOTS + FEW
    near, far = twins(None, of_left, of_right)
    pairs = pairs_of(field_ref[...])
    force = jnp.zeros((96, LANES), f32)
    for block in range(sources // 8):
        mark = jnp.concatenate(marks[2 * block : 2 * block + 2], 1)
        spot = spots(jnp.concatenate(bases[2 * block : 2 * block + 2], 1))
        found = gathered(pairs, spot)
        weights = block_weights(mark)
        here = [found[at * 8 : at * 8 + 8] + jnp.concatenate([near[at]] * 2, 1) for at in range(12)]
        there = [
            found[96 + at * 8 : 104 + at * 8] + jnp.concatenate([far[at]] * 2, 1) for at in range(12)
        ]
        _, spreads = forces_of(mark, weights, here, there)
        for half in range(2):
            lanes = slice(half * LANES, (half + 1) * LANES)
            keep_twins(mark[:, lanes], [part[:, lanes] for part in spreads], of_left, of_right)
        spreads = jnp.concatenate(spreads, 0)
        ahead = spreads * mark[4:5, :]
        force = force + scattered(spreads - ahead, ahead, spot)

    further = jnp.where((lane >= FIRST_SPARE) & (lane < FIRST_Z), 1.0, 0.0)
    most = got_ref[0]
    for source in range(1, sources):
        most = jnp.maximum(most, got_ref[source])

    @pl.when(jnp.max(most * further) > 0.5)
    def _():
        lefts = lane < SPARE
        rights = (lane >= SPARE) & (lane < 2 * SPARE)
        near, far = twins(None, lefts, rights)

        def one(source, carry):
            mark = roll(got_ref[source], -FIRST_SPARE, 1)
            mark = jnp.where(lane < 2 * SPARE, mark, 0.0)
            _, spreads = forces_of(mark, block_weights(mark), near, far)
            keep_twins(mark, spreads, lefts, rights)
            return carry

        lax.fori_loop(0, sources, one, 0)

    left_high, left_low = split_two(left_ref[...])
    right_high, right_low = split_two(right_ref[...])
    column = iota((4 * LANES, LANES), 1) < 64
    whole = (iota((4 * LANES, LANES), 0) < 2 * LANES) == column
    sums = jnp.dot(
        jnp.concatenate([left_high, left_low, right_high, right_low], 1),
        jnp.where(whole, 1.0, 0.0).astype(bf16),
        preferred_element_type=f32,
    )
    pulls = []
    for axis_no in range(3):
        total = None
        for plane in range(PLANES):
            at = axis_no * 32 + plane * 8
            value = sums[at : at + 8, :]
            total = value if total is None else jnp.where(lane % PLANES == plane, value, total)
        pulls.append(total)
    density, speeds, relax = rim[0], rim[1:4], rim[4]
    pull = relax / density
    shifted = [speeds[a] + pull * pulls[a] for a in range(3)]
    shifted_sq = shifted[0] * shifted[0] + shifted[1] * shifted[1] + shifted[2] * shifted[2]
    rate = 1.0 / relax
    side = jnp.where(lane < 64, 1.0, -1.0)
    rim_post = []
    for number, member in enumerate(ahead_z):
        along = side * along_of(member, shifted)
        weight = 1.0 / 18.0 if number == 0 else 1.0 / 36.0
        target = weight * density * (1.0 + 3.0 * along + 4.5 * along * along - 1.5 * shifted_sq)
        rim_post.append((1.0 - rate) * rim[5 + number] + rate * target)

    for plane in range(PLANES):
        ats = [a * 32 + plane * 8 for a in range(3)]
        results = relaxed(
            [pops_ref[member, plane] for member in range(19)],
            density_ref[plane],
            [field_ref[at : at + 8, :] for at in ats],
            relax_ref[plane],
            [force[at : at + 8, :] for at in ats],
        )
        for member in range(19):
            post_ref[member, plane] = results[member]

    for plane in range(PLANES):
        pops = []
        for member in range(19):
            shift_x, shift_y, shift_z = velocity_table[member]
            source = (plane - shift_x) % PLANES
            value = post_ref[member, source]
            if shift_z == 1:
                edge = roll(rim_post[ahead_z.index(member)], -source, 1)
                value = jnp.where(lane == 0, edge, roll(value, 1, 1))
            if shift_z == -1:
                edge = roll(rim_post[back_z.index(member)], 63 - source, 1)
                value = jnp.where(lane == LANES - 1, edge, roll(value, -1, 1))
            if shift_y == 1:
                at = AT_NEXT + rising.index(member) * PLANES + plane
                up_ref[at : at + 1, :] = value[ROWS - 1 : ROWS, :]
                value = jnp.where(row == 0, post_ref[opposite[member], plane], roll(value, 1, 0))
            if shift_y == -1:
                at = AT_NEXT + falling.index(member) * PLANES + plane
                down_ref[at : at + 1, :] = value[0:1, :]
                value = jnp.where(
                    row == ROWS - 1, post_ref[opposite[member], plane], roll(value, -1, 0)
                )
            next_ref[member, plane] = value
            pops.append(value)
        _, speeds = moments_of(pops)
        for axis_no in range(3):
            at = AT_SPEED + axis_no * PLANES + plane
            up_ref[at : at + 1, :] = speeds[axis_no][ROWS - 2 : ROWS - 1, :]
            down_ref[at : at + 1, :] = speeds[axis_no][1:2, :]
        for number, member in enumerate(level + rising):
            at = AT_POPS + number * PLANES + plane
            up_ref[at : at + 1, :] = pops[member][ROWS - 1 : ROWS, :]
        for number, member in enumerate(level + falling):
            at = AT_POPS + number * PLANES + plane
            down_ref[at : at + 1, :] = pops[member][0:1, :]


def third_kernel(
    info_ref, next_ref, up_ref, down_ref, below_ref, above_ref,
    moved_ref, back_ref,
    wide_ref, field_ref, density_ref, post_ref, outer_ref,
):
    left, right, first_open, last_open, first_wall, last_wall = [info_ref[i] for i in range(6)]
    lane = iota((ROWS, LANES), 1)
    row = iota((ROWS, LANES), 0)
    sources = back_ref.shape[0]

    def four(ref, at):
        return ref[at : at + PLANES, :]

    for plane in range(PLANES):
        pops = []
        for member in range(19):
            value = next_ref[member, plane]
            if member in rising:
                at = AT_NEXT + rising.index(member) * PLANES + plane
                value = jnp.where(row == first_open, below_ref[at : at + 1, :], value)
            if member in falling:
                at = AT_NEXT + falling.index(member) * PLANES + plane
                value = jnp.where(row == last_open, above_ref[at : at + 1, :], value)
            wide_ref[member, plane] = value
            pops.append(value)
        density, speeds = moments_of(pops)
        density_ref[plane] = density
        for axis_no in range(3):
            at = axis_no * 32 + plane * 8
            field_ref[at : at + 8, :] = speeds[axis_no]

    outer = []
    for member in range(19):
        if member in falling:
            low = four(down_ref, AT_NEXT + falling.index(member) * PLANES)
        else:
            low = four(below_ref, AT_POPS + (level + rising).index(member) * PLANES)
        if member in rising:
            top = four(up_ref, AT_NEXT + rising.index(member) * PLANES)
        else:
            top = four(above_ref, AT_POPS + (level + falling).index(member) * PLANES)
        outer.append(jnp.concatenate([low, top], 0))
    outer_density, outer_speeds = moments_of(outer)
    lows, tops = [], []
    for axis_no in range(3):
        at = AT_SPEED + axis_no * PLANES
        second = jnp.concatenate([four(above_ref, at), four(below_ref, at)], 0)
        lows.append(jnp.where(row < PLANES, outer_speeds[axis_no], second))
        tops.append(jnp.where(row < PLANES, second, outer_speeds[axis_no]))

    def beyond(ref, field, base_y):
        pairs = pairs_of(jnp.concatenate(field, 0))
        total = jnp.zeros((24, LANES), f32)
        for block in range(sources // 8):
            tile = AT_MARKS + 16 * block
            mark = jnp.concatenate([ref[tile : tile + 8, :], ref[tile + 8 : tile + 16, :]], 1)
            at = AT_Z + 2 * block
            base = jnp.concatenate([ref[at : at + 1, :], ref[at + 1 : at + 2, :]], 1)
            spot = spots(base)
            found = gathered(pairs, spot)
            place = iota((ROWS, 2 * LANES), 0)
            frac = mark[3:4, :]
            weight = along_x(mark, (place % PLANES).astype(f32))
            weight = weight * jnp.where(place < PLANES, frac, 1.0 - frac)
            weight = jnp.where(mark[1:2, :] == base_y, weight, 0.0)
            frac = mark[4:5, :]
            spreads = []
            for axis_no in range(3):
                here = found[axis_no * 8 : axis_no * 8 + 8]
                there = found[24 + axis_no * 8 : 32 + axis_no * 8]
                value = weight * (here + frac * (there - here))
                force = mark[5 + axis_no : 6 + axis_no, :] - jnp.sum(value, 0, keepdims=True)
                spreads.append(weight * force)
            spreads = jnp.concatenate(spreads, 0)
            ahead = spreads * frac
            total = total + scattered(spreads - ahead, ahead, spot)
        return total

    from_below = beyond(below_ref, lows, float(ROWS - 2))
    from_above = beyond(above_ref, tops, 0.0)
    outer_pulls = [
        jnp.where(row < PLANES, from_below[a * 8 : a * 8 + 8], from_above[a * 8 : a * 8 + 8])
        for a in range(3)
    ]
    relax = relax_of(outer, outer_density, outer_speeds)
    outer_post = relaxed(outer, outer_density, outer_speeds, relax, outer_pulls)
    for number in range(5):
        outer_ref[number] = jnp.where(
            row < PLANES, outer_post[rising[number]], outer_post[falling[number]]
        )

    pairs = pairs_of(field_ref[...])
    total = jnp.zeros((96, LANES), f32)
    for block in range(sources // 8):
        tile = AT_MARKS + 16 * block
        mark = jnp.concatenate([up_ref[tile : tile + 8, :], up_ref[tile + 8 : tile + 16, :]], 1)
        at = AT_Z + 2 * block
        spot = spots(jnp.concatenate([up_ref[at : at + 1, :], up_ref[at + 1 : at + 2, :]], 1))
        found = gathered(pairs, spot)
        forces, spreads = forces_of(
            mark,
            block_weights(mark),
            [found[at * 8 : at * 8 + 8] for at in range(12)],
            [found[96 + at * 8 : 104 + at * 8] for at in range(12)],
        )
        spreads = jnp.concatenate(spreads, 0)
        ahead = spreads * mark[4:5, :]
        total = total + scattered(spreads - ahead, ahead, spot)
        for half in range(2):
            lanes = slice(half * LANES, (half + 1) * LANES)
            value = forces[2][:, lanes]
            value = jnp.where(row == 1, forces[1][:, lanes], value)
            value = jnp.where(row == 0, forces[0][:, lanes], value)
            for part in range(4):
                back_ref[block * 8 + half * 4 + part] = roll(value, -SHARE * part, 1)

    for plane in range(PLANES):
        ats = [a * 32 + plane * 8 for a in range(3)]
        pops = [wide_ref[member, plane] for member in range(19)]
        speeds = [field_ref[at : at + 8, :] for at in ats]
        density = density_ref[plane]
        relax = relax_of(pops, density, speeds)
        results = relaxed(pops, density, speeds, relax, [total[at : at + 8, :] for at in ats])
        for member in range(19):
            post_ref[member, plane] = results[member]

    to_right, to_left = jnp.zeros((ROWS, LANES), f32), jnp.zeros((ROWS, LANES), f32)
    for plane in range(PLANES):
        for member in range(19):
            shift_x, shift_y, shift_z = velocity_table[member]
            source = (plane - shift_x) % PLANES
            value = post_ref[member, source]
            if shift_y == 1:
                edge = outer_ref[rising.index(member), source : source + 1, :]
                value = jnp.where(row == 0, edge, roll(value, 1, 0))
            if shift_y == -1:
                at = PLANES + source
                edge = outer_ref[falling.index(member), at : at + 1, :]
                value = jnp.where(row == ROWS - 1, edge, roll(value, -1, 0))
            if shift_z:
                value = roll(value, shift_z, 1)
            if shift_z == 1:
                place = FIRST_FACE + ahead_z.index(member) * PLANES + plane
                to_right = jnp.where(lane == place, roll(value, place, 1), to_right)
            if shift_z == -1:
                place = FIRST_FACE + back_z.index(member) * PLANES + plane
                to_left = jnp.where(lane == place, roll(value, place + 1, 1), to_left)
            if shift_y == 1:
                value = jnp.where(row == first_wall, post_ref[opposite[member], plane], value)
            if shift_y == -1:
                value = jnp.where(row == last_wall, post_ref[opposite[member], plane], value)
            moved_ref[member, plane] = value
    faces = (lane >= FIRST_FACE) & (lane < FIRST_FACE + 5 * PLANES)
    back_ref[left] = jnp.where(faces, to_left, back_ref[left])
    back_ref[right] = jnp.where(faces, to_right, back_ref[right])


def last_kernel(info_ref, count_ref, moved_ref, got_ref, owner_ref, rank_ref, pops_ref, force_ref):
    left, right, _, _, first_wall, last_wall = [info_ref[i] for i in range(6)]
    lane = iota((ROWS, LANES), 1)
    row = iota((ROWS, LANES), 0)
    from_left, from_right = got_ref[left], got_ref[right]
    for member in range(19):
        _, shift_y, shift_z = velocity_table[member]
        for plane in range(PLANES):
            value = moved_ref[member, plane]
            if shift_z:
                if shift_z == 1:
                    place = FIRST_FACE + ahead_z.index(member) * PLANES + plane
                    edge, here = roll(from_left, -place, 1), lane == 0
                else:
                    place = FIRST_FACE + back_z.index(member) * PLANES + plane
                    edge, here = roll(from_right, LANES - 1 - place, 1), lane == LANES - 1
                if shift_y == 1:
                    here = here & (row != first_wall)
                if shift_y == -1:
                    here = here & (row != last_wall)
                value = jnp.where(here, edge, value)
            pops_ref[member, plane] = value
    owners, markers = got_ref.shape[0], owner_ref.shape[1]
    live = iota((1, markers), 1) < count_ref[0]
    owner = jnp.where(live, owner_ref[...], -1)
    spot = (iota((LANES, markers), 0).astype(f32) == rank_ref[...]).astype(bf16)
    high, low = split_two(got_ref[...].reshape(owners * 8, LANES))
    found = jnp.dot(
        jnp.concatenate([high, low], 1),
        jnp.concatenate([spot, spot], 0),
        preferred_element_type=f32,
    )
    total = jnp.zeros((8, markers), f32)
    for number in range(owners):
        total = jnp.where(owner == number, found[number * 8 : number * 8 + 8, :], total)
    force_ref[...] = total[0:3, :] / ref_speed


def body(populations, marker_owner, marker_cell, marker_frac, marker_speed, marker_count):
    count_gy, count_gz = lax.axis_size("gy"), lax.axis_size("gz")
    markers = marker_owner.shape[0]
    smem = pl.BlockSpec(memory_space=pltpu.SMEM)
    vmem = pl.BlockSpec(memory_space=pltpu.VMEM)
    hbm = pl.BlockSpec(memory_space=pl.ANY)
    shape = jax.ShapeDtypeStruct
    row, column = lax.axis_index("gy"), lax.axis_index("gz")
    first, last = row == 0, row == count_gy - 1
    info = jnp.stack(
        [
            (column + count_gz - 1) % count_gz,
            (column + 1) % count_gz,
            jnp.where(first, -1, 0),
            jnp.where(last, -1, ROWS - 1),
            jnp.where(first, 0, -1),
            jnp.where(last, ROWS - 1, -1),
        ]
    ).astype(jnp.int32)
    owner = marker_owner.reshape(1, markers)
    tiles = shape((count_gz, 8, LANES), f32)
    field = shape((96, LANES), f32)
    cells = shape((PLANES, ROWS, LANES), f32)
    lattice = shape(populations.shape, f32)
    send, rank, speeds, density, relax = call(
        first_kernel,
        [tiles, shape((1, markers), f32), field, cells, cells],
        [info, marker_count, owner, marker_cell, marker_frac, marker_speed, populations],
        [smem] * 2 + [hbm] * 5,
        scratch=[
            pltpu.VMEM((1, markers), jnp.int32),
            pltpu.VMEM((3, markers), jnp.int32),
            pltpu.VMEM((3, markers), f32),
            pltpu.VMEM((3, markers), f32),
            pltpu.VMEM(populations.shape, f32),
            pltpu.SemaphoreType.DMA((5,)),
        ],
    )
    got = lax.all_to_all(send, "gz", split_axis=0, concat_axis=0, tiled=True)
    face = shape((FACE_ROWS, LANES), f32)
    next_pops, up, down = call(
        second_kernel,
        [lattice, face, face],
        [info, populations, got, speeds, density, relax],
        [smem] + [vmem] * 5,
        scratch=[
            pltpu.VMEM(populations.shape, f32),
            pltpu.VMEM((24, ROWS, LANES), f32),
            pltpu.VMEM((24, ROWS, LANES), f32),
            pltpu.VMEM((96, LANES), f32),
            pltpu.VMEM((96, LANES), f32),
        ],
    )
    below = lax.ppermute(up, "gy", [(i, (i + 1) % count_gy) for i in range(count_gy)])
    above = lax.ppermute(down, "gy", [((i + 1) % count_gy, i) for i in range(count_gy)])
    moved, back = call(
        third_kernel,
        [lattice, tiles],
        [info, next_pops, up, down, below, above],
        [smem] + [vmem] * 5,
        scratch=[
            pltpu.VMEM(populations.shape, f32),
            pltpu.VMEM((96, LANES), f32),
            pltpu.VMEM((PLANES, ROWS, LANES), f32),
            pltpu.VMEM(populations.shape, f32),
            pltpu.VMEM((5, ROWS, LANES), f32),
        ],
    )
    back = lax.all_to_all(back, "gz", split_axis=0, concat_axis=0, tiled=True)
    pops, force = call(
        last_kernel,
        [lattice, shape((3, markers), f32)],
        [info, marker_count, moved, back, owner, rank],
        [smem] * 2 + [vmem] * 4,
    )
    return pops, force


def solution(mesh):
    return jax.shard_map(
        body,
        mesh=mesh,
        in_specs=(
            P(None, None, "gy", "gz"),
            P(("gy", "gz"), None),
            P(None, ("gy", "gz")),
            P(None, ("gy", "gz")),
            P(None, ("gy", "gz")),
            P(("gy", "gz")),
        ),
        out_specs=(P(None, None, "gy", "gz"), P(None, ("gy", "gz"))),
        check_vma=False,
    )
```

```python
import math

import jax
import jax.numpy as jnp
from jax import lax
from jax.experimental import pallas as pl
from jax.experimental.pallas import tpu as pltpu
from jax.sharding import PartitionSpec as P

INTERPRET = False

velocity_table = (
    (0, 0, 0),
    (1, 0, 0),
    (-1, 0, 0),
    (0, 1, 0),
    (0, -1, 0),
    (0, 0, 1),
    (0, 0, -1),
    (1, 1, 0),
    (-1, -1, 0),
    (1, -1, 0),
    (-1, 1, 0),
    (1, 0, 1),
    (-1, 0, -1),
    (1, 0, -1),
    (-1, 0, 1),
    (0, 1, 1),
    (0, -1, -1),
    (0, 1, -1),
    (0, -1, 1),
)
opposite = (0, 2, 1, 4, 3, 6, 5, 8, 7, 10, 9, 12, 11, 14, 13, 16, 15, 18, 17)
rising = tuple(i for i in range(19) if velocity_table[i][1] == 1)
falling = tuple(opposite[i] for i in rising)
level = tuple(i for i in range(19) if velocity_table[i][1] == 0)
ahead_z = tuple(i for i in range(19) if velocity_table[i][2] == 1)
back_z = tuple(opposite[i] for i in ahead_z)
tau_base = 0.52
smag_const = 0.17
ref_speed = 0.05

PLANES = 4
ROWS = 8
LANES = 128
SLOTS = 24
SHARE = 32
FEW = 4
SPARE = SLOTS - FEW
FIRST_SPARE = SHARE
FIRST_Z = SHARE + 2 * SPARE
FIRST_RIM = 76
LATE_FACE = 3 * SHARE
EARLY = 16
RIM_WORDS = 13
AT_SPEED, AT_POPS, AT_NEXT, AT_MARKS, AT_Z, FACE_ROWS = 0, 12, 68, 88, 152, 160

f32 = jnp.float32
bf16 = jnp.bfloat16


def iota(shape, dim):
    return lax.broadcasted_iota(jnp.int32, shape, dim)


def roll(value, shift, axis):
    shift = shift % value.shape[axis]
    return pltpu.roll(value, shift, axis) if shift else value


def split_two(value):
    high = value.astype(bf16)
    return high, (value - high.astype(f32)).astype(bf16)


def call(kernel, out_shape, args, in_specs, scratch=()):
    vmem = pl.BlockSpec(memory_space=pltpu.VMEM)
    return pl.pallas_call(
        kernel,
        out_shape=out_shape,
        in_specs=in_specs,
        out_specs=[vmem] * len(out_shape),
        scratch_shapes=list(scratch),
        compiler_params=pltpu.CompilerParams(vmem_limit_bytes=32 * 1024 * 1024),
        interpret=INTERPRET,
    )(*args)


def moments_of(pops):
    density = pops[0]
    for member in range(1, 19):
        density = density + pops[member]
    parts = []
    for axis_no in range(3):
        total = None
        for member in range(19):
            if velocity_table[member][axis_no] == 1:
                total = pops[member] if total is None else total + pops[member]
        for member in range(19):
            if velocity_table[member][axis_no] == -1:
                total = total - pops[member]
        parts.append(total)
    inverse = 1.0 / density
    return density, [part * inverse for part in parts]


def relax_of(pops, density, speeds):
    factor = 18.0 * math.sqrt(2.0) * smag_const * smag_const
    moved = [density * part for part in speeds]
    pair = [pops[2 * k + 1] + pops[2 * k + 2] for k in range(9)]
    third = density * (1.0 / 3.0)
    xx = pair[0] + pair[3] + pair[4] + pair[5] + pair[6] - third - moved[0] * speeds[0]
    yy = pair[1] + pair[3] + pair[4] + pair[7] + pair[8] - third - moved[1] * speeds[1]
    zz = pair[2] + pair[5] + pair[6] + pair[7] + pair[8] - third - moved[2] * speeds[2]
    xy = pair[3] - pair[4] - moved[0] * speeds[1]
    xz = pair[5] - pair[6] - moved[0] * speeds[2]
    yz = pair[7] - pair[8] - moved[1] * speeds[2]
    norm_sq = xx * xx + yy * yy + zz * zz + 2.0 * (xy * xy + xz * xz + yz * yz)
    return 0.5 * (tau_base + jnp.sqrt(tau_base * tau_base + factor * jnp.sqrt(norm_sq) / density))


def along_of(member, speeds):
    total = None
    for axis_no in range(3):
        if velocity_table[member][axis_no] == 1:
            total = speeds[axis_no] if total is None else total + speeds[axis_no]
    for axis_no in range(3):
        if velocity_table[member][axis_no] == -1:
            total = total - speeds[axis_no]
    return total


def relaxed(pops, density, speeds, relax, pulls):
    pull = relax / density
    shifted = [speeds[a] + pull * pulls[a] for a in range(3)]
    shifted_sq = shifted[0] * shifted[0] + shifted[1] * shifted[1] + shifted[2] * shifted[2]
    rate = 1.0 / relax
    keep = 1.0 - rate
    scale = rate * density
    base = scale * (1.0 - 1.5 * shifted_sq)
    quad = 4.5 * scale
    results = [keep * pops[0] + base * (1.0 / 3.0)]
    for pair in range(9):
        plus = 2 * pair + 1
        along = along_of(plus, shifted)
        weight = 1.0 / 18.0 if pair < 3 else 1.0 / 36.0
        even = weight * (base + quad * along * along)
        odd = (3.0 * weight) * (scale * along)
        results.append(keep * pops[plus] + (even + odd))
        results.append(keep * pops[plus + 1] + (even - odd))
    return results


def along_x(mark, plane):
    base, frac = mark[0:1, :], mark[2:3, :]
    following = jnp.where(base == float(PLANES), 0.0, base)
    weight = jnp.where(base - 1.0 == plane, 1.0 - frac, 0.0)
    return jnp.where((base > 0.5) & (following == plane), frac, weight)


def block_weights(mark):
    base, frac = mark[1:2, :], mark[3:4, :]
    row = iota((ROWS, mark.shape[1]), 0).astype(f32)
    along_y = jnp.where(row == base, 1.0 - frac, jnp.where(row == base + 1.0, frac, 0.0))
    return [along_y * along_x(mark, float(plane)) for plane in range(PLANES)]


def spots(base_z):
    count = base_z.shape[1]
    return jnp.where(iota((LANES, count), 0).astype(f32) == base_z, 1.0, 0.0).astype(bf16)


def pairs_of(field):
    high, low = split_two(field)
    next_high, next_low = split_two(roll(field, -1, 1))
    return jnp.concatenate(
        [jnp.concatenate([high, low], 1), jnp.concatenate([next_high, next_low], 1)], 0
    )


def gathered(pairs, spot):
    return jnp.dot(pairs, jnp.concatenate([spot, spot], 0), preferred_element_type=f32)


def sums_of(here, there, spot):
    size = here.shape[0]
    high, low = split_two(here)
    next_high, next_low = split_two(there)
    sums = lax.dot_general(
        jnp.concatenate([high, low, next_high, next_low], 0),
        spot,
        (((1,), (1,)), ((), ())),
        preferred_element_type=f32,
    )
    first = sums[0:size] + sums[size : 2 * size]
    second = sums[2 * size : 3 * size] + sums[3 * size :]
    return first, second


def scattered(here, there, spot):
    first, second = sums_of(here, there, spot)
    return first + roll(second, 1, 1)


def forces_of(mark, weights, here, there):
    frac = mark[4:5, :]
    forces, spreads = [], []
    for axis_no in range(3):
        total = None
        for plane in range(PLANES):
            at = axis_no * PLANES + plane
            value = weights[plane] * (here[at] + frac * (there[at] - here[at]))
            total = value if total is None else total + value
        force = mark[5 + axis_no : 6 + axis_no, :] - jnp.sum(total, 0, keepdims=True)
        forces.append(force)
        for plane in range(PLANES):
            spreads.append(weights[plane] * force)
    return forces, spreads


def first_kernel(
    info_ref, count_ref, owner_hbm, cell_hbm, frac_hbm, speed_hbm, pops_hbm,
    send_ref, rank_ref, field_ref, density_ref, relax_ref,
    owner_ref, cell_ref, frac_ref, speed_ref, pops_ref, sems,
):
    copies = [
        pltpu.make_async_copy(source, target, sems.at[number])
        for number, (source, target) in enumerate(
            [
                (owner_hbm, owner_ref),
                (cell_hbm, cell_ref),
                (frac_hbm, frac_ref),
                (speed_hbm, speed_ref),
                (pops_hbm, pops_ref),
            ]
        )
    ]
    for copy in copies:
        copy.start()
    for copy in copies[0:4]:
        copy.wait()
    owners, markers = send_ref.shape[0], owner_ref.shape[1]
    live = iota((1, markers), 1) < count_ref[0]
    owner = jnp.where(live, owner_ref[...], -1)
    base_z = cell_ref[2:3, :]
    upper, lower = base_z == LANES - 2, base_z == 0
    twin = jnp.where(
        upper,
        jnp.where(owner == owners - 1, 0, owner + 1),
        jnp.where(owner == 0, owners - 1, owner - 1),
    )
    twin = jnp.where(live & (upper | lower), twin, -1)
    hit = iota((owners, markers), 0) == owner
    hits = jnp.concatenate(
        [hit.astype(f32), (hit & upper).astype(f32), (hit & lower).astype(f32)], 0
    )
    below = (iota((LANES, LANES), 0) < iota((LANES, LANES), 1)).astype(bf16)
    before = jnp.zeros((3 * owners, 1), f32)
    ranks = [[], [], []]
    for start in range(0, markers, LANES):
        part = hits[:, start : start + LANES]
        inner = jnp.dot(part.astype(bf16), below, preferred_element_type=f32)
        picked = part * (inner + before)
        for kind in range(3):
            ranks[kind].append(
                jnp.sum(picked[kind * owners : (kind + 1) * owners], 0, keepdims=True)
            )
        before = before + jnp.sum(part, 1, keepdims=True)
    rank, rank_up, rank_low = [jnp.concatenate(kind, 1) for kind in ranks]
    rank_ref[...] = rank
    lane_up = jnp.where(rank_up < FEW, SLOTS + rank_up, FIRST_SPARE - FEW + rank_up)
    lane_low = jnp.where(
        rank_low < FEW, SLOTS + FEW + rank_low, FIRST_SPARE + SPARE - FEW + rank_low
    )
    lane_twin = jnp.where(upper, lane_up, lane_low)
    lane_z = FIRST_Z + jnp.where(rank >= 16.0, 2.0, jnp.where(rank >= 8.0, 1.0, 0.0))
    slot_z = rank - 8.0 * (lane_z - FIRST_Z)
    lane = iota((LANES, markers), 0).astype(f32)
    spot_own = (lane == rank).astype(bf16)
    spot_twin = (lane == lane_twin).astype(bf16)
    spot_z = (lane == lane_z).astype(bf16)
    row = iota((8, markers), 0)
    words = jnp.where(row == 0, cell_ref[0:1, :] + 1, cell_ref[1:2, :]).astype(f32)
    for number in range(3):
        words = jnp.where(row == 2 + number, frac_ref[number : number + 1, :], words)
        words = jnp.where(row == 5 + number, speed_ref[number : number + 1, :], words)
    high, low = split_two(words)
    high, low = high.astype(f32), low.astype(f32)
    words_z = jnp.where(row.astype(f32) == slot_z, base_z.astype(f32), 0.0)

    def to_owners(value, target):
        rows = [jnp.where(target == number, value, 0.0) for number in range(owners)]
        return jnp.concatenate(rows, 0).astype(bf16)

    def placed(left, spot):
        return lax.dot_general(left, spot, (((1,), (1,)), ((), ())), preferred_element_type=f32)

    tiles = placed(to_owners(high, owner), spot_own) + placed(to_owners(low, owner), spot_own)
    tiles = tiles + placed(to_owners(high, twin), spot_twin)
    tiles = tiles + placed(to_owners(low, twin), spot_twin)
    tiles = tiles + placed(to_owners(words_z, owner), spot_z)
    send_ref[...] = tiles.reshape(owners, 8, LANES)

    copies[4].wait()
    lane = iota((ROWS, LANES), 1)
    to_right, to_left = jnp.zeros((ROWS, LANES), f32), jnp.zeros((ROWS, LANES), f32)
    for plane in range(PLANES):
        pops = [pops_ref[member, plane] for member in range(19)]
        density, speeds = moments_of(pops)
        relax = relax_of(pops, density, speeds)
        density_ref[plane] = density
        relax_ref[plane] = relax
        for axis_no in range(3):
            at = axis_no * 32 + plane * 8
            field_ref[at : at + 8, :] = speeds[axis_no]
        common = [density, *speeds, relax]
        for word in range(RIM_WORDS):
            place = FIRST_RIM + word * PLANES + plane
            if word < 5:
                right, left, shift = common[word], common[word], 0
            elif word < 10:
                right, left, shift = pops[ahead_z[word - 5]], pops[back_z[word - 5]], 0
            else:
                right, left, shift = speeds[word - 10], speeds[word - 10], 1
            here = lane == place
            to_right = jnp.where(here, roll(right, place - (LANES - 1) + shift, 1), to_right)
            to_left = jnp.where(here, roll(left, place - shift, 1), to_left)
    left, right = info_ref[0], info_ref[1]
    send_ref[left] = send_ref[left] + to_left
    send_ref[right] = send_ref[right] + to_right


def second_kernel(
    info_ref, pops_ref, got_ref, field_ref, density_ref, relax_ref,
    next_ref, up_ref, down_ref,
    post_ref, near_ref, far_ref, twin_ref,
):
    left, right = info_ref[0], info_ref[1]
    lane = iota((ROWS, LANES), 1)
    row = iota((ROWS, LANES), 0)
    sources = got_ref.shape[0]

    chosen = iota((LANES, LANES), 1) % SHARE
    chosen = (iota((LANES, LANES), 0) == FIRST_Z + chosen // 8) & (chosen < SLOTS)
    every_z = jnp.dot(
        got_ref[...].reshape(sources * 8, LANES).astype(bf16),
        chosen.astype(bf16),
        preferred_element_type=f32,
    )
    marks, bases = [], []
    for tile in range(sources // 4):
        words, place = None, None
        for part in range(4):
            source = tile * 4 + part
            value = roll(got_ref[source], SHARE * part, 1)
            spot = every_z[source * 8 : source * 8 + 8, :]
            if part:
                words = jnp.where(lane // SHARE == part, value, words)
                place = jnp.where(lane // SHARE == part, spot, place)
            else:
                words, place = value, spot
        place = jnp.sum(jnp.where(lane % 8 == row, place, 0.0), 0, keepdims=True)
        place = jnp.where(iota((1, LANES), 1) % SHARE < SLOTS, place, -5.0)
        marks.append(words)
        bases.append(place)
        for ref in (up_ref, down_ref):
            ref[AT_MARKS + tile * 8 : AT_MARKS + tile * 8 + 8, :] = words
            ref[AT_Z + tile : AT_Z + tile + 1, :] = place

    ends = jnp.where(lane >= FIRST_RIM, got_ref[left], roll(got_ref[right], 64, 1))
    rim = [roll(ends, -(FIRST_RIM + PLANES * word), 1) for word in range(RIM_WORDS)]

    def spread_lane(value, at):
        return jnp.broadcast_to(value[:, at : at + 1], (ROWS, LANES))

    for axis_no in range(3):
        for plane in range(PLANES):
            at = axis_no * PLANES + plane
            near_ref[at] = spread_lane(rim[10 + axis_no], plane)
            near_ref[12 + at] = spread_lane(rim[1 + axis_no], 64 + plane)
            far_ref[at] = spread_lane(rim[1 + axis_no], plane)
            far_ref[12 + at] = spread_lane(rim[10 + axis_no], 64 + plane)

    def twins(of_left, of_right):
        def both(ref):
            return [
                jnp.where(of_left, ref[at], jnp.where(of_right, ref[12 + at], 0.0))
                for at in range(12)
            ]

        return both(near_ref), both(far_ref)

    def sides(lefts, rights, count):
        place, member = iota((LANES, count), 0), iota((LANES, count), 1)
        chosen = jnp.where(place < 64, lefts(member).astype(f32), rights(member).astype(f32))
        return chosen.astype(bf16)

    of_left = (lane % SHARE >= SLOTS) & (lane % SHARE < SLOTS + FEW)
    of_right = lane % SHARE >= SLOTS + FEW
    near, far = twins(of_left, of_right)
    side = sides(
        lambda member: (member % SHARE >= SLOTS) & (member % SHARE < SLOTS + FEW),
        lambda member: member % SHARE >= SLOTS + FEW,
        2 * LANES,
    )
    of_rim = jnp.zeros((96, LANES), f32)
    rim_left = iota((96, LANES), 1) < 64
    pairs = pairs_of(field_ref[...])
    force = jnp.zeros((96, LANES), f32)
    for block in range(sources // 8):
        mark = jnp.concatenate(marks[2 * block : 2 * block + 2], 1)
        spot = spots(jnp.concatenate(bases[2 * block : 2 * block + 2], 1))
        found = gathered(pairs, spot)
        weights = block_weights(mark)
        here = [found[at * 8 : at * 8 + 8] + jnp.concatenate([near[at]] * 2, 1) for at in range(12)]
        there = [
            found[96 + at * 8 : 104 + at * 8] + jnp.concatenate([far[at]] * 2, 1) for at in range(12)
        ]
        _, spreads = forces_of(mark, weights, here, there)
        spreads = jnp.concatenate(spreads, 0)
        ahead = spreads * mark[4:5, :]
        first, second = sums_of(spreads - ahead, ahead, jnp.concatenate([spot, side], 0))
        force = force + (first[:, 0:LANES] + roll(second[:, 0:LANES], 1, 1))
        of_rim = of_rim + jnp.where(rim_left, second[:, LANES:], first[:, LANES:])
    twin_ref[...] = of_rim

    further = jnp.where((lane >= FIRST_SPARE) & (lane < FIRST_Z), 1.0, 0.0)
    most = got_ref[0]
    for source in range(1, sources):
        most = jnp.maximum(most, got_ref[source])

    @pl.when(jnp.max(most * further) > 0.5)
    def _():
        near, far = twins(lane < SPARE, lane >= SPARE)
        side = sides(lambda member: member < SPARE, lambda member: member >= SPARE, LANES)

        def one(source, carry):
            mark = roll(got_ref[source], -FIRST_SPARE, 1)
            mark = jnp.where(lane < 2 * SPARE, mark, 0.0)
            _, spreads = forces_of(mark, block_weights(mark), near, far)
            spreads = jnp.concatenate(spreads, 0)
            ahead = spreads * mark[4:5, :]
            first, second = sums_of(spreads - ahead, ahead, side)
            twin_ref[...] = twin_ref[...] + jnp.where(rim_left, second, first)
            return carry

        lax.fori_loop(0, sources, one, 0)

    sums = twin_ref[...]
    pulls = []
    for axis_no in range(3):
        total = None
        for plane in range(PLANES):
            at = axis_no * 32 + plane * 8
            value = sums[at : at + 8, :]
            total = value if total is None else jnp.where(lane % PLANES == plane, value, total)
        pulls.append(total)
    density, speeds, relax = rim[0], rim[1:4], rim[4]
    pull = relax / density
    shifted = [speeds[a] + pull * pulls[a] for a in range(3)]
    shifted_sq = shifted[0] * shifted[0] + shifted[1] * shifted[1] + shifted[2] * shifted[2]
    rate = 1.0 / relax
    sign = jnp.where(lane < 64, 1.0, -1.0)
    rim_post = []
    for number, member in enumerate(ahead_z):
        along = sign * along_of(member, shifted)
        weight = 1.0 / 18.0 if number == 0 else 1.0 / 36.0
        target = weight * density * (1.0 + 3.0 * along + 4.5 * along * along - 1.5 * shifted_sq)
        rim_post.append((1.0 - rate) * rim[5 + number] + rate * target)

    for plane in range(PLANES):
        ats = [a * 32 + plane * 8 for a in range(3)]
        results = relaxed(
            [pops_ref[member, plane] for member in range(19)],
            density_ref[plane],
            [field_ref[at : at + 8, :] for at in ats],
            relax_ref[plane],
            [force[at : at + 8, :] for at in ats],
        )
        for member in range(19):
            post_ref[member, plane] = results[member]

    for plane in range(PLANES):
        pops = []
        for member in range(19):
            shift_x, shift_y, shift_z = velocity_table[member]
            source = (plane - shift_x) % PLANES
            value = post_ref[member, source]
            if shift_z == 1:
                edge = roll(rim_post[ahead_z.index(member)], -source, 1)
                value = jnp.where(lane == 0, edge, roll(value, 1, 1))
            if shift_z == -1:
                edge = roll(rim_post[back_z.index(member)], 63 - source, 1)
                value = jnp.where(lane == LANES - 1, edge, roll(value, -1, 1))
            if shift_y == 1:
                at = AT_NEXT + rising.index(member) * PLANES + plane
                up_ref[at : at + 1, :] = value[ROWS - 1 : ROWS, :]
                value = jnp.where(row == 0, post_ref[opposite[member], plane], roll(value, 1, 0))
            if shift_y == -1:
                at = AT_NEXT + falling.index(member) * PLANES + plane
                down_ref[at : at + 1, :] = value[0:1, :]
                value = jnp.where(
                    row == ROWS - 1, post_ref[opposite[member], plane], roll(value, -1, 0)
                )
            next_ref[member, plane] = value
            pops.append(value)
        _, speeds = moments_of(pops)
        for axis_no in range(3):
            at = AT_SPEED + axis_no * PLANES + plane
            up_ref[at : at + 1, :] = speeds[axis_no][ROWS - 2 : ROWS - 1, :]
            down_ref[at : at + 1, :] = speeds[axis_no][1:2, :]
        for number, member in enumerate(level + rising):
            at = AT_POPS + number * PLANES + plane
            up_ref[at : at + 1, :] = pops[member][ROWS - 1 : ROWS, :]
        for number, member in enumerate(level + falling):
            at = AT_POPS + number * PLANES + plane
            down_ref[at : at + 1, :] = pops[member][0:1, :]


def third_kernel(
    info_ref, next_ref, up_ref, down_ref, below_ref, above_ref,
    moved_ref, back_ref,
    wide_ref, field_ref, density_ref, post_ref, outer_ref,
):
    left, right, first_open, last_open, first_wall, last_wall = [info_ref[i] for i in range(6)]
    lane = iota((ROWS, LANES), 1)
    row = iota((ROWS, LANES), 0)
    sources = back_ref.shape[0]

    def four(ref, at):
        return ref[at : at + PLANES, :]

    for plane in range(PLANES):
        pops = []
        for member in range(19):
            value = next_ref[member, plane]
            if member in rising:
                at = AT_NEXT + rising.index(member) * PLANES + plane
                value = jnp.where(row == first_open, below_ref[at : at + 1, :], value)
            if member in falling:
                at = AT_NEXT + falling.index(member) * PLANES + plane
                value = jnp.where(row == last_open, above_ref[at : at + 1, :], value)
            wide_ref[member, plane] = value
            pops.append(value)
        density, speeds = moments_of(pops)
        density_ref[plane] = density
        for axis_no in range(3):
            at = axis_no * 32 + plane * 8
            field_ref[at : at + 8, :] = speeds[axis_no]

    outer = []
    for member in range(19):
        if member in falling:
            low = four(down_ref, AT_NEXT + falling.index(member) * PLANES)
        else:
            low = four(below_ref, AT_POPS + (level + rising).index(member) * PLANES)
        if member in rising:
            top = four(up_ref, AT_NEXT + rising.index(member) * PLANES)
        else:
            top = four(above_ref, AT_POPS + (level + falling).index(member) * PLANES)
        outer.append(jnp.concatenate([low, top], 0))
    outer_density, outer_speeds = moments_of(outer)
    lows, tops = [], []
    for axis_no in range(3):
        at = AT_SPEED + axis_no * PLANES
        second = jnp.concatenate([four(above_ref, at), four(below_ref, at)], 0)
        lows.append(jnp.where(row < PLANES, outer_speeds[axis_no], second))
        tops.append(jnp.where(row < PLANES, second, outer_speeds[axis_no]))

    def beyond(ref, field, base_y):
        pairs = pairs_of(jnp.concatenate(field, 0))
        total = jnp.zeros((24, LANES), f32)
        for block in range(sources // 8):
            tile = AT_MARKS + 16 * block
            mark = jnp.concatenate([ref[tile : tile + 8, :], ref[tile + 8 : tile + 16, :]], 1)
            at = AT_Z + 2 * block
            base = jnp.concatenate([ref[at : at + 1, :], ref[at + 1 : at + 2, :]], 1)
            spot = spots(base)
            found = gathered(pairs, spot)
            place = iota((ROWS, 2 * LANES), 0)
            frac = mark[3:4, :]
            weight = along_x(mark, (place % PLANES).astype(f32))
            weight = weight * jnp.where(place < PLANES, frac, 1.0 - frac)
            weight = jnp.where(mark[1:2, :] == base_y, weight, 0.0)
            frac = mark[4:5, :]
            spreads = []
            for axis_no in range(3):
                here = found[axis_no * 8 : axis_no * 8 + 8]
                there = found[24 + axis_no * 8 : 32 + axis_no * 8]
                value = weight * (here + frac * (there - here))
                force = mark[5 + axis_no : 6 + axis_no, :] - jnp.sum(value, 0, keepdims=True)
                spreads.append(weight * force)
            spreads = jnp.concatenate(spreads, 0)
            ahead = spreads * frac
            total = total + scattered(spreads - ahead, ahead, spot)
        return total

    from_below = beyond(below_ref, lows, float(ROWS - 2))
    from_above = beyond(above_ref, tops, 0.0)
    outer_pulls = [
        jnp.where(row < PLANES, from_below[a * 8 : a * 8 + 8], from_above[a * 8 : a * 8 + 8])
        for a in range(3)
    ]
    relax = relax_of(outer, outer_density, outer_speeds)
    outer_post = relaxed(outer, outer_density, outer_speeds, relax, outer_pulls)
    for number in range(5):
        outer_ref[number] = jnp.where(
            row < PLANES, outer_post[rising[number]], outer_post[falling[number]]
        )

    pairs = pairs_of(field_ref[...])
    total = jnp.zeros((96, LANES), f32)
    kept = [jnp.zeros((ROWS, LANES), f32) for axis_no in range(3)]
    for block in range(sources // 8):
        tile = AT_MARKS + 16 * block
        mark = jnp.concatenate([up_ref[tile : tile + 8, :], up_ref[tile + 8 : tile + 16, :]], 1)
        at = AT_Z + 2 * block
        spot = spots(jnp.concatenate([up_ref[at : at + 1, :], up_ref[at + 1 : at + 2, :]], 1))
        found = gathered(pairs, spot)
        forces, spreads = forces_of(
            mark,
            block_weights(mark),
            [found[at * 8 : at * 8 + 8] for at in range(12)],
            [found[96 + at * 8 : 104 + at * 8] for at in range(12)],
        )
        spreads = jnp.concatenate(spreads, 0)
        ahead = spreads * mark[4:5, :]
        total = total + scattered(spreads - ahead, ahead, spot)
        for half in range(2):
            lanes = slice(half * LANES, (half + 1) * LANES)
            for axis_no in range(3):
                kept[axis_no] = jnp.where(
                    row == 2 * block + half, forces[axis_no][:, lanes], kept[axis_no]
                )
    back_ref[...] = jnp.zeros(back_ref.shape, f32)
    for part in range(4):
        value = roll(kept[0], -SHARE * part, 1)
        for axis_no in range(1, 3):
            moved = roll(kept[axis_no], SHARE * (axis_no - part), 1)
            value = jnp.where(lane // SHARE == axis_no, moved, value)
        for tile in range(sources // 4):
            back_ref[4 * tile + part, 0:1, :] = value[tile : tile + 1, :]

    for plane in range(PLANES):
        ats = [a * 32 + plane * 8 for a in range(3)]
        pops = [wide_ref[member, plane] for member in range(19)]
        speeds = [field_ref[at : at + 8, :] for at in ats]
        density = density_ref[plane]
        relax = relax_of(pops, density, speeds)
        results = relaxed(pops, density, speeds, relax, [total[at : at + 8, :] for at in ats])
        for member in range(19):
            post_ref[member, plane] = results[member]

    to_right, to_left = jnp.zeros((ROWS, LANES), f32), jnp.zeros((ROWS, LANES), f32)
    for plane in range(PLANES):
        for member in range(19):
            shift_x, shift_y, shift_z = velocity_table[member]
            source = (plane - shift_x) % PLANES
            value = post_ref[member, source]
            if shift_y == 1:
                edge = outer_ref[rising.index(member), source : source + 1, :]
                value = jnp.where(row == 0, edge, roll(value, 1, 0))
            if shift_y == -1:
                at = PLANES + source
                edge = outer_ref[falling.index(member), at : at + 1, :]
                value = jnp.where(row == ROWS - 1, edge, roll(value, -1, 0))
            if shift_z:
                value = roll(value, shift_z, 1)
            if shift_z == 1:
                place = ahead_z.index(member) * PLANES + plane
                to_right = jnp.where(lane == place, roll(value, place, 1), to_right)
            if shift_z == -1:
                place = back_z.index(member) * PLANES + plane
                to_left = jnp.where(lane == place, roll(value, place + 1, 1), to_left)
            if shift_y == 1:
                value = jnp.where(row == first_wall, post_ref[opposite[member], plane], value)
            if shift_y == -1:
                value = jnp.where(row == last_wall, post_ref[opposite[member], plane], value)
            moved_ref[member, plane] = value
    for target, face in ((left, to_left), (right, to_right)):
        early, late = jnp.zeros((ROWS, LANES), f32), jnp.zeros((ROWS, LANES), f32)
        for number in range(ROWS):
            early = jnp.where(row == number, roll(face, EARLY * number, 1), early)
            late = jnp.where(row == number, roll(face, LATE_FACE - EARLY + 4 * number, 1), late)
        early = jnp.where(lane // EARLY == row, early, 0.0)
        late = jnp.where((lane - LATE_FACE) // 4 == row, late, 0.0)
        late = jnp.where(lane >= LATE_FACE, late, 0.0)
        mine = jnp.where(iota((1, LANES), 1) < LATE_FACE, back_ref[target, 0:1, :], 0.0)
        back_ref[target, 0:1, :] = mine + jnp.sum(late, 0, keepdims=True)
        back_ref[target, 1:2, :] = jnp.sum(early, 0, keepdims=True)


def last_kernel(info_ref, count_ref, moved_ref, got_ref, owner_ref, rank_ref, pops_ref, force_ref):
    left, right, _, _, first_wall, last_wall = [info_ref[i] for i in range(6)]
    lane = iota((ROWS, LANES), 1)
    row = iota((ROWS, LANES), 0)

    def face_of(source):
        late = jnp.broadcast_to(got_ref[source, 0:1, :], (ROWS, LANES))
        early = jnp.broadcast_to(got_ref[source, 1:2, :], (ROWS, LANES))
        face = jnp.zeros((ROWS, LANES), f32)
        for number in range(ROWS):
            value = roll(late, EARLY - LATE_FACE - 4 * number, 1)
            value = jnp.where(lane < EARLY, roll(early, -EARLY * number, 1), value)
            face = jnp.where(row == number, value, face)
        return face

    from_left, from_right = face_of(left), face_of(right)
    for member in range(19):
        _, shift_y, shift_z = velocity_table[member]
        for plane in range(PLANES):
            value = moved_ref[member, plane]
            if shift_z:
                if shift_z == 1:
                    place = ahead_z.index(member) * PLANES + plane
                    edge, here = roll(from_left, -place, 1), lane == 0
                else:
                    place = back_z.index(member) * PLANES + plane
                    edge, here = roll(from_right, LANES - 1 - place, 1), lane == LANES - 1
                if shift_y == 1:
                    here = here & (row != first_wall)
                if shift_y == -1:
                    here = here & (row != last_wall)
                value = jnp.where(here, edge, value)
            pops_ref[member, plane] = value
    owners, markers = got_ref.shape[0], owner_ref.shape[1]
    live = iota((1, markers), 1) < count_ref[0]
    owner = jnp.where(live, owner_ref[...], -1)
    spot = (iota((LANES, markers), 0).astype(f32) == rank_ref[...]).astype(bf16)
    rows = got_ref[:, 0, :]
    high, low = split_two(
        jnp.concatenate([roll(rows, -SHARE * axis_no, 1) for axis_no in range(3)], 0)
    )
    found = jnp.dot(
        jnp.concatenate([high, low], 1),
        jnp.concatenate([spot, spot], 0),
        preferred_element_type=f32,
    )
    hit = iota((owners, markers), 0) == owner
    for axis_no in range(3):
        value = jnp.where(hit, found[axis_no * owners : (axis_no + 1) * owners], 0.0)
        force_ref[axis_no : axis_no + 1, :] = jnp.sum(value, 0, keepdims=True) / ref_speed


def body(populations, marker_owner, marker_cell, marker_frac, marker_speed, marker_count):
    count_gy, count_gz = lax.axis_size("gy"), lax.axis_size("gz")
    markers = marker_owner.shape[0]
    smem = pl.BlockSpec(memory_space=pltpu.SMEM)
    vmem = pl.BlockSpec(memory_space=pltpu.VMEM)
    hbm = pl.BlockSpec(memory_space=pltpu.HBM)
    shape = jax.ShapeDtypeStruct
    row, column = lax.axis_index("gy"), lax.axis_index("gz")
    first, last = row == 0, row == count_gy - 1
    info = jnp.stack(
        [
            (column + count_gz - 1) % count_gz,
            (column + 1) % count_gz,
            jnp.where(first, -1, 0),
            jnp.where(last, -1, ROWS - 1),
            jnp.where(first, 0, -1),
            jnp.where(last, ROWS - 1, -1),
        ]
    ).astype(jnp.int32)
    owner = marker_owner.reshape(1, markers)
    tiles = shape((count_gz, 8, LANES), f32)
    field = shape((96, LANES), f32)
    cells = shape((PLANES, ROWS, LANES), f32)
    lattice = shape(populations.shape, f32)
    send, rank, speeds, density, relax = call(
        first_kernel,
        [tiles, shape((1, markers), f32), field, cells, cells],
        [info, marker_count, owner, marker_cell, marker_frac, marker_speed, populations],
        [smem] * 2 + [hbm] * 5,
        scratch=[
            pltpu.VMEM((1, markers), jnp.int32),
            pltpu.VMEM((3, markers), jnp.int32),
            pltpu.VMEM((3, markers), f32),
            pltpu.VMEM((3, markers), f32),
            pltpu.VMEM(populations.shape, f32),
            pltpu.SemaphoreType.DMA((5,)),
        ],
    )
    got = lax.all_to_all(send, "gz", split_axis=0, concat_axis=0, tiled=True)
    face = shape((FACE_ROWS, LANES), f32)
    next_pops, up, down = call(
        second_kernel,
        [lattice, face, face],
        [info, populations, got, speeds, density, relax],
        [smem] + [vmem] * 5,
        scratch=[
            pltpu.VMEM(populations.shape, f32),
            pltpu.VMEM((24, ROWS, LANES), f32),
            pltpu.VMEM((24, ROWS, LANES), f32),
            pltpu.VMEM((96, LANES), f32),
        ],
    )
    below = lax.ppermute(up, "gy", [(i, (i + 1) % count_gy) for i in range(count_gy)])
    above = lax.ppermute(down, "gy", [((i + 1) % count_gy, i) for i in range(count_gy)])
    moved, back = call(
        third_kernel,
        [lattice, shape((count_gz, 2, LANES), f32)],
        [info, next_pops, up, down, below, above],
        [smem] + [vmem] * 5,
        scratch=[
            pltpu.VMEM(populations.shape, f32),
            pltpu.VMEM((96, LANES), f32),
            pltpu.VMEM((PLANES, ROWS, LANES), f32),
            pltpu.VMEM(populations.shape, f32),
            pltpu.VMEM((5, ROWS, LANES), f32),
        ],
    )
    back = lax.all_to_all(back, "gz", split_axis=0, concat_axis=0, tiled=True)
    pops, force = call(
        last_kernel,
        [lattice, shape((3, markers), f32)],
        [info, marker_count, moved, back, owner, rank],
        [smem] * 2 + [vmem] * 4,
    )
    return pops, force


def solution(mesh):
    return jax.shard_map(
        body,
        mesh=mesh,
        in_specs=(
            P(None, None, "gy", "gz"),
            P(("gy", "gz"), None),
            P(None, ("gy", "gz")),
            P(None, ("gy", "gz")),
            P(None, ("gy", "gz")),
            P(("gy", "gz")),
        ),
        out_specs=(P(None, None, "gy", "gz"), P(None, ("gy", "gz"))),
        check_vma=False,
    )
```

```python
import math

import jax
import jax.numpy as jnp
from jax import lax
from jax.experimental import pallas as pl
from jax.experimental.pallas import tpu as pltpu
from jax.sharding import PartitionSpec as P

INTERPRET = False

velocity_table = (
    (0, 0, 0),
    (1, 0, 0),
    (-1, 0, 0),
    (0, 1, 0),
    (0, -1, 0),
    (0, 0, 1),
    (0, 0, -1),
    (1, 1, 0),
    (-1, -1, 0),
    (1, -1, 0),
    (-1, 1, 0),
    (1, 0, 1),
    (-1, 0, -1),
    (1, 0, -1),
    (-1, 0, 1),
    (0, 1, 1),
    (0, -1, -1),
    (0, 1, -1),
    (0, -1, 1),
)
opposite = (0, 2, 1, 4, 3, 6, 5, 8, 7, 10, 9, 12, 11, 14, 13, 16, 15, 18, 17)
rising = tuple(i for i in range(19) if velocity_table[i][1] == 1)
falling = tuple(opposite[i] for i in rising)
level = tuple(i for i in range(19) if velocity_table[i][1] == 0)
ahead_z = tuple(i for i in range(19) if velocity_table[i][2] == 1)
back_z = tuple(opposite[i] for i in ahead_z)
tau_base = 0.52
smag_const = 0.17
ref_speed = 0.05

PLANES = 4
ROWS = 8
LANES = 128
SLOTS = 24
SHARE = 32
FEW = 4
SPARE = SLOTS - FEW
FIRST_SPARE = SHARE
FIRST_Z = SHARE + 2 * SPARE
FIRST_RIM = 76
LATE_FACE = 3 * SHARE
EARLY = 16
RIM_WORDS = 13
AT_SPEED, AT_POPS, AT_NEXT, AT_MARKS, AT_Z, FACE_ROWS = 0, 12, 68, 88, 152, 160

f32 = jnp.float32
bf16 = jnp.bfloat16


def iota(shape, dim):
    return lax.broadcasted_iota(jnp.int32, shape, dim)


def roll(value, shift, axis):
    shift = shift % value.shape[axis]
    return pltpu.roll(value, shift, axis) if shift else value


def split_two(value):
    high = value.astype(bf16)
    return high, (value - high.astype(f32)).astype(bf16)


def call(kernel, out_shape, args, in_specs, scratch=(), out_specs=None, aliases=()):
    vmem = pl.BlockSpec(memory_space=pltpu.VMEM)
    return pl.pallas_call(
        kernel,
        out_shape=out_shape,
        in_specs=in_specs,
        out_specs=out_specs or [vmem] * len(out_shape),
        input_output_aliases=dict(aliases),
        scratch_shapes=list(scratch),
        compiler_params=pltpu.CompilerParams(vmem_limit_bytes=32 * 1024 * 1024),
        interpret=INTERPRET,
    )(*args)


def z_neighbours():
    column, size = lax.axis_index("gz"), lax.axis_size("gz")
    return (column + size - 1) % size, (column + 1) % size


def y_ends():
    place, size = lax.axis_index("gy"), lax.axis_size("gy")
    first, last = place == 0, place == size - 1
    return (
        jnp.where(first, -1, 0),
        jnp.where(last, -1, ROWS - 1),
        jnp.where(first, 0, -1),
        jnp.where(last, ROWS - 1, -1),
    )


def moments_of(pops):
    density = pops[0]
    for member in range(1, 19):
        density = density + pops[member]
    parts = []
    for axis_no in range(3):
        total = None
        for member in range(19):
            if velocity_table[member][axis_no] == 1:
                total = pops[member] if total is None else total + pops[member]
        for member in range(19):
            if velocity_table[member][axis_no] == -1:
                total = total - pops[member]
        parts.append(total)
    inverse = 1.0 / density
    return density, [part * inverse for part in parts]


def relax_of(pops, density, speeds):
    factor = 18.0 * math.sqrt(2.0) * smag_const * smag_const
    moved = [density * part for part in speeds]
    pair = [pops[2 * k + 1] + pops[2 * k + 2] for k in range(9)]
    third = density * (1.0 / 3.0)
    xx = pair[0] + pair[3] + pair[4] + pair[5] + pair[6] - third - moved[0] * speeds[0]
    yy = pair[1] + pair[3] + pair[4] + pair[7] + pair[8] - third - moved[1] * speeds[1]
    zz = pair[2] + pair[5] + pair[6] + pair[7] + pair[8] - third - moved[2] * speeds[2]
    xy = pair[3] - pair[4] - moved[0] * speeds[1]
    xz = pair[5] - pair[6] - moved[0] * speeds[2]
    yz = pair[7] - pair[8] - moved[1] * speeds[2]
    norm_sq = xx * xx + yy * yy + zz * zz + 2.0 * (xy * xy + xz * xz + yz * yz)
    return 0.5 * (tau_base + jnp.sqrt(tau_base * tau_base + factor * jnp.sqrt(norm_sq) / density))


def along_of(member, speeds):
    total = None
    for axis_no in range(3):
        if velocity_table[member][axis_no] == 1:
            total = speeds[axis_no] if total is None else total + speeds[axis_no]
    for axis_no in range(3):
        if velocity_table[member][axis_no] == -1:
            total = total - speeds[axis_no]
    return total


def relaxed(pops, density, speeds, relax, pulls):
    pull = relax / density
    shifted = [speeds[a] + pull * pulls[a] for a in range(3)]
    shifted_sq = shifted[0] * shifted[0] + shifted[1] * shifted[1] + shifted[2] * shifted[2]
    rate = 1.0 / relax
    keep = 1.0 - rate
    scale = rate * density
    base = scale * (1.0 - 1.5 * shifted_sq)
    quad = 4.5 * scale
    results = [keep * pops[0] + base * (1.0 / 3.0)]
    for pair in range(9):
        plus = 2 * pair + 1
        along = along_of(plus, shifted)
        weight = 1.0 / 18.0 if pair < 3 else 1.0 / 36.0
        even = weight * (base + quad * along * along)
        odd = (3.0 * weight) * (scale * along)
        results.append(keep * pops[plus] + (even + odd))
        results.append(keep * pops[plus + 1] + (even - odd))
    return results


def along_x(mark, plane):
    base, frac = mark[0:1, :], mark[2:3, :]
    following = jnp.where(base == float(PLANES), 0.0, base)
    weight = jnp.where(base - 1.0 == plane, 1.0 - frac, 0.0)
    return jnp.where((base > 0.5) & (following == plane), frac, weight)


def block_weights(mark):
    base, frac = mark[1:2, :], mark[3:4, :]
    row = iota((ROWS, mark.shape[1]), 0).astype(f32)
    along_y = jnp.where(row == base, 1.0 - frac, jnp.where(row == base + 1.0, frac, 0.0))
    return [along_y * along_x(mark, float(plane)) for plane in range(PLANES)]


def spots(base_z):
    count = base_z.shape[1]
    return jnp.where(iota((LANES, count), 0).astype(f32) == base_z, 1.0, 0.0).astype(bf16)


def pairs_of(field):
    high, low = split_two(field)
    next_high, next_low = split_two(roll(field, -1, 1))
    return jnp.concatenate(
        [jnp.concatenate([high, low], 1), jnp.concatenate([next_high, next_low], 1)], 0
    )


def gathered(pairs, spot):
    return jnp.dot(pairs, jnp.concatenate([spot, spot], 0), preferred_element_type=f32)


def sums_of(here, there, spot):
    size = here.shape[0]
    high, low = split_two(here)
    next_high, next_low = split_two(there)
    sums = lax.dot_general(
        jnp.concatenate([high, low, next_high, next_low], 0),
        spot,
        (((1,), (1,)), ((), ())),
        preferred_element_type=f32,
    )
    first = sums[0:size] + sums[size : 2 * size]
    second = sums[2 * size : 3 * size] + sums[3 * size :]
    return first, second


def scattered(here, there, spot):
    first, second = sums_of(here, there, spot)
    return first + roll(second, 1, 1)


def forces_of(mark, weights, here, there):
    frac = mark[4:5, :]
    forces, spreads = [], []
    for axis_no in range(3):
        total = None
        for plane in range(PLANES):
            at = axis_no * PLANES + plane
            value = weights[plane] * (here[at] + frac * (there[at] - here[at]))
            total = value if total is None else total + value
        force = mark[5 + axis_no : 6 + axis_no, :] - jnp.sum(total, 0, keepdims=True)
        forces.append(force)
        for plane in range(PLANES):
            spreads.append(weights[plane] * force)
    return forces, spreads


def first_kernel(
    count_ref, owner_hbm, cell_hbm, frac_hbm, speed_hbm, pops_hbm,
    send_ref, rank_ref, live_ref, field_ref, density_ref, relax_ref,
    owner_ref, cell_ref, frac_ref, speed_ref, pops_ref, sems,
):
    copies = [
        pltpu.make_async_copy(source, target, sems.at[number])
        for number, (source, target) in enumerate(
            [
                (owner_hbm, owner_ref),
                (cell_hbm, cell_ref),
                (frac_hbm, frac_ref),
                (speed_hbm, speed_ref),
                (pops_hbm, pops_ref),
            ]
        )
    ]
    for copy in copies:
        copy.start()
    for copy in copies[0:4]:
        copy.wait()
    owners, markers = send_ref.shape[0], owner_ref.shape[1]
    live = iota((1, markers), 1) < count_ref[...]
    owner = jnp.where(live, owner_ref[...], -1)
    live_ref[...] = owner
    base_z = cell_ref[2:3, :]
    upper, lower = base_z == LANES - 2, base_z == 0
    twin = jnp.where(
        upper,
        jnp.where(owner == owners - 1, 0, owner + 1),
        jnp.where(owner == 0, owners - 1, owner - 1),
    )
    twin = jnp.where(live & (upper | lower), twin, -1)
    hit = iota((owners, markers), 0) == owner
    hits = jnp.concatenate(
        [hit.astype(f32), (hit & upper).astype(f32), (hit & lower).astype(f32)], 0
    )
    blocks = markers // LANES
    parts = [hits[:, block * LANES : (block + 1) * LANES] for block in range(blocks)]
    earlier = iota((LANES, 2 * LANES), 0) < iota((LANES, 2 * LANES), 1)
    counts = jnp.dot(
        jnp.concatenate(parts, 0).astype(bf16), earlier.astype(bf16), preferred_element_type=f32
    )
    before = None
    ranks = [[], [], []]
    for block in range(blocks):
        inner = counts[block * 3 * owners : (block + 1) * 3 * owners]
        place = inner[:, 0:LANES] if before is None else inner[:, 0:LANES] + before
        before = inner[:, LANES:] if before is None else inner[:, LANES:] + before
        picked = parts[block] * place
        for kind in range(3):
            ranks[kind].append(
                jnp.sum(picked[kind * owners : (kind + 1) * owners], 0, keepdims=True)
            )
    rank, rank_up, rank_low = [jnp.concatenate(kind, 1) for kind in ranks]
    rank_ref[...] = rank
    lane_up = jnp.where(rank_up < FEW, SLOTS + rank_up, FIRST_SPARE - FEW + rank_up)
    lane_low = jnp.where(
        rank_low < FEW, SLOTS + FEW + rank_low, FIRST_SPARE + SPARE - FEW + rank_low
    )
    lane_twin = jnp.where(upper, lane_up, lane_low)
    lane_z = FIRST_Z + jnp.where(rank >= 16.0, 2.0, jnp.where(rank >= 8.0, 1.0, 0.0))
    slot_z = rank - 8.0 * (lane_z - FIRST_Z)
    lane = iota((LANES, markers), 0).astype(f32)
    spot_own = (lane == rank).astype(bf16)
    spot_twin = (lane == lane_twin).astype(bf16)
    spot_z = (lane == lane_z).astype(bf16)
    row = iota((8, markers), 0)
    words = jnp.where(row == 0, cell_ref[0:1, :] + 1, cell_ref[1:2, :]).astype(f32)
    for number in range(3):
        words = jnp.where(row == 2 + number, frac_ref[number : number + 1, :], words)
        words = jnp.where(row == 5 + number, speed_ref[number : number + 1, :], words)
    high, low = split_two(words)
    high, low = high.astype(f32), low.astype(f32)
    words_z = jnp.where(row.astype(f32) == slot_z, base_z.astype(f32), 0.0)

    def to_owners(value, target):
        rows = [jnp.where(target == number, value, 0.0) for number in range(owners)]
        return jnp.concatenate(rows, 0).astype(bf16)

    def placed(left, spot):
        return lax.dot_general(left, spot, (((1,), (1,)), ((), ())), preferred_element_type=f32)

    tiles = placed(to_owners(high, owner), spot_own) + placed(to_owners(low, owner), spot_own)
    tiles = tiles + placed(to_owners(high, twin), spot_twin)
    tiles = tiles + placed(to_owners(low, twin), spot_twin)
    tiles = tiles + placed(to_owners(words_z, owner), spot_z)
    send_ref[...] = tiles.reshape(owners, 8, LANES)

    copies[4].wait()

    lane = iota((ROWS, LANES), 1)
    to_right, to_left = jnp.zeros((ROWS, LANES), f32), jnp.zeros((ROWS, LANES), f32)
    for plane in range(PLANES):
        pops = [pops_ref[member, plane] for member in range(19)]
        density, speeds = moments_of(pops)
        relax = relax_of(pops, density, speeds)
        density_ref[plane] = density
        relax_ref[plane] = relax
        for axis_no in range(3):
            at = axis_no * 32 + plane * 8
            field_ref[at : at + 8, :] = speeds[axis_no]
        common = [density, *speeds, relax]
        for word in range(RIM_WORDS):
            place = FIRST_RIM + word * PLANES + plane
            if word < 5:
                right, left, shift = common[word], common[word], 0
            elif word < 10:
                right, left, shift = pops[ahead_z[word - 5]], pops[back_z[word - 5]], 0
            else:
                right, left, shift = speeds[word - 10], speeds[word - 10], 1
            here = lane == place
            to_right = jnp.where(here, roll(right, place - (LANES - 1) + shift, 1), to_right)
            to_left = jnp.where(here, roll(left, place - shift, 1), to_left)
    left, right = z_neighbours()
    send_ref[left] = send_ref[left] + to_left
    send_ref[right] = send_ref[right] + to_right


def second_kernel(
    pops_ref, got_ref, field_ref, density_ref, relax_ref,
    next_ref, up_ref, down_ref,
    post_ref, near_ref, far_ref, twin_ref,
):
    left, right = z_neighbours()
    lane = iota((ROWS, LANES), 1)
    row = iota((ROWS, LANES), 0)
    sources = got_ref.shape[0]

    chosen = iota((LANES, LANES), 1) % SHARE
    chosen = (iota((LANES, LANES), 0) == FIRST_Z + chosen // 8) & (chosen < SLOTS)
    every_z = jnp.dot(
        got_ref[...].reshape(sources * 8, LANES).astype(bf16),
        chosen.astype(bf16),
        preferred_element_type=f32,
    )
    marks, bases = [], []
    for tile in range(sources // 4):
        words, place = None, None
        for part in range(4):
            source = tile * 4 + part
            value = roll(got_ref[source], SHARE * part, 1)
            spot = every_z[source * 8 : source * 8 + 8, :]
            if part:
                words = jnp.where(lane // SHARE == part, value, words)
                place = jnp.where(lane // SHARE == part, spot, place)
            else:
                words, place = value, spot
        place = jnp.sum(jnp.where(lane % 8 == row, place, 0.0), 0, keepdims=True)
        place = jnp.where(iota((1, LANES), 1) % SHARE < SLOTS, place, -5.0)
        marks.append(words)
        bases.append(place)
        for ref in (up_ref, down_ref):
            ref[AT_MARKS + tile * 8 : AT_MARKS + tile * 8 + 8, :] = words
            ref[AT_Z + tile : AT_Z + tile + 1, :] = place

    ends = jnp.where(lane >= FIRST_RIM, got_ref[left], roll(got_ref[right], 64, 1))
    rim = [roll(ends, -(FIRST_RIM + PLANES * word), 1) for word in range(RIM_WORDS)]

    def spread_lane(value, at):
        return jnp.broadcast_to(value[:, at : at + 1], (ROWS, LANES))

    for axis_no in range(3):
        for plane in range(PLANES):
            at = axis_no * PLANES + plane
            near_ref[at] = spread_lane(rim[10 + axis_no], plane)
            near_ref[12 + at] = spread_lane(rim[1 + axis_no], 64 + plane)
            far_ref[at] = spread_lane(rim[1 + axis_no], plane)
            far_ref[12 + at] = spread_lane(rim[10 + axis_no], 64 + plane)

    def twins(of_left, of_right):
        def both(ref):
            return [
                jnp.where(of_left, ref[at], jnp.where(of_right, ref[12 + at], 0.0))
                for at in range(12)
            ]

        return both(near_ref), both(far_ref)

    def sides(lefts, rights, count):
        place, member = iota((LANES, count), 0), iota((LANES, count), 1)
        chosen = jnp.where(place < 64, lefts(member).astype(f32), rights(member).astype(f32))
        return chosen.astype(bf16)

    of_left = (lane % SHARE >= SLOTS) & (lane % SHARE < SLOTS + FEW)
    of_right = lane % SHARE >= SLOTS + FEW
    near, far = twins(of_left, of_right)
    side = sides(
        lambda member: (member % SHARE >= SLOTS) & (member % SHARE < SLOTS + FEW),
        lambda member: member % SHARE >= SLOTS + FEW,
        2 * LANES,
    )
    of_rim = jnp.zeros((96, LANES), f32)
    rim_left = iota((96, LANES), 1) < 64
    pairs = pairs_of(field_ref[...])
    force = jnp.zeros((96, LANES), f32)
    for block in range(sources // 8):
        mark = jnp.concatenate(marks[2 * block : 2 * block + 2], 1)
        spot = spots(jnp.concatenate(bases[2 * block : 2 * block + 2], 1))
        found = gathered(pairs, spot)
        weights = block_weights(mark)
        here = [found[at * 8 : at * 8 + 8] + jnp.concatenate([near[at]] * 2, 1) for at in range(12)]
        there = [
            found[96 + at * 8 : 104 + at * 8] + jnp.concatenate([far[at]] * 2, 1) for at in range(12)
        ]
        _, spreads = forces_of(mark, weights, here, there)
        spreads = jnp.concatenate(spreads, 0)
        ahead = spreads * mark[4:5, :]
        first, second = sums_of(spreads - ahead, ahead, jnp.concatenate([spot, side], 0))
        force = force + (first[:, 0:LANES] + roll(second[:, 0:LANES], 1, 1))
        of_rim = of_rim + jnp.where(rim_left, second[:, LANES:], first[:, LANES:])
    twin_ref[...] = of_rim

    further = jnp.where((lane >= FIRST_SPARE) & (lane < FIRST_Z), 1.0, 0.0)
    most = got_ref[0]
    for source in range(1, sources):
        most = jnp.maximum(most, got_ref[source])

    @pl.when(jnp.max(most * further) > 0.5)
    def _():
        near, far = twins(lane < SPARE, lane >= SPARE)
        side = sides(lambda member: member < SPARE, lambda member: member >= SPARE, LANES)

        def one(source, carry):
            mark = roll(got_ref[source], -FIRST_SPARE, 1)
            mark = jnp.where(lane < 2 * SPARE, mark, 0.0)
            _, spreads = forces_of(mark, block_weights(mark), near, far)
            spreads = jnp.concatenate(spreads, 0)
            ahead = spreads * mark[4:5, :]
            first, second = sums_of(spreads - ahead, ahead, side)
            twin_ref[...] = twin_ref[...] + jnp.where(rim_left, second, first)
            return carry

        lax.fori_loop(0, sources, one, 0)

    sums = twin_ref[...]
    pulls = []
    for axis_no in range(3):
        total = None
        for plane in range(PLANES):
            at = axis_no * 32 + plane * 8
            value = sums[at : at + 8, :]
            total = value if total is None else jnp.where(lane % PLANES == plane, value, total)
        pulls.append(total)
    density, speeds, relax = rim[0], rim[1:4], rim[4]
    pull = relax / density
    shifted = [speeds[a] + pull * pulls[a] for a in range(3)]
    shifted_sq = shifted[0] * shifted[0] + shifted[1] * shifted[1] + shifted[2] * shifted[2]
    rate = 1.0 / relax
    sign = jnp.where(lane < 64, 1.0, -1.0)
    rim_post = []
    for number, member in enumerate(ahead_z):
        along = sign * along_of(member, shifted)
        weight = 1.0 / 18.0 if number == 0 else 1.0 / 36.0
        target = weight * density * (1.0 + 3.0 * along + 4.5 * along * along - 1.5 * shifted_sq)
        rim_post.append((1.0 - rate) * rim[5 + number] + rate * target)

    for plane in range(PLANES):
        ats = [a * 32 + plane * 8 for a in range(3)]
        results = relaxed(
            [pops_ref[member, plane] for member in range(19)],
            density_ref[plane],
            [field_ref[at : at + 8, :] for at in ats],
            relax_ref[plane],
            [force[at : at + 8, :] for at in ats],
        )
        for member in range(19):
            post_ref[member, plane] = results[member]

    for plane in range(PLANES):
        pops = []
        for member in range(19):
            shift_x, shift_y, shift_z = velocity_table[member]
            source = (plane - shift_x) % PLANES
            value = post_ref[member, source]
            if shift_z == 1:
                edge = roll(rim_post[ahead_z.index(member)], -source, 1)
                value = jnp.where(lane == 0, edge, roll(value, 1, 1))
            if shift_z == -1:
                edge = roll(rim_post[back_z.index(member)], 63 - source, 1)
                value = jnp.where(lane == LANES - 1, edge, roll(value, -1, 1))
            if shift_y == 1:
                at = AT_NEXT + rising.index(member) * PLANES + plane
                up_ref[at : at + 1, :] = value[ROWS - 1 : ROWS, :]
                value = jnp.where(row == 0, post_ref[opposite[member], plane], roll(value, 1, 0))
            if shift_y == -1:
                at = AT_NEXT + falling.index(member) * PLANES + plane
                down_ref[at : at + 1, :] = value[0:1, :]
                value = jnp.where(
                    row == ROWS - 1, post_ref[opposite[member], plane], roll(value, -1, 0)
                )
            next_ref[member, plane] = value
            pops.append(value)
        _, speeds = moments_of(pops)
        for axis_no in range(3):
            at = AT_SPEED + axis_no * PLANES + plane
            up_ref[at : at + 1, :] = speeds[axis_no][ROWS - 2 : ROWS - 1, :]
            down_ref[at : at + 1, :] = speeds[axis_no][1:2, :]
        for number, member in enumerate(level + rising):
            at = AT_POPS + number * PLANES + plane
            up_ref[at : at + 1, :] = pops[member][ROWS - 1 : ROWS, :]
        for number, member in enumerate(level + falling):
            at = AT_POPS + number * PLANES + plane
            down_ref[at : at + 1, :] = pops[member][0:1, :]


def third_kernel(
    next_ref, up_ref, down_ref, below_ref, above_ref,
    moved_ref, back_ref,
    wide_ref, field_ref, density_ref, post_ref, outer_ref,
):
    left, right = z_neighbours()
    first_open, last_open, first_wall, last_wall = y_ends()
    lane = iota((ROWS, LANES), 1)
    row = iota((ROWS, LANES), 0)
    sources = back_ref.shape[0]

    def four(ref, at):
        return ref[at : at + PLANES, :]

    for plane in range(PLANES):
        pops = []
        for member in range(19):
            value = next_ref[member, plane]
            if member in rising:
                at = AT_NEXT + rising.index(member) * PLANES + plane
                value = jnp.where(row == first_open, below_ref[at : at + 1, :], value)
            if member in falling:
                at = AT_NEXT + falling.index(member) * PLANES + plane
                value = jnp.where(row == last_open, above_ref[at : at + 1, :], value)
            wide_ref[member, plane] = value
            pops.append(value)
        density, speeds = moments_of(pops)
        density_ref[plane] = density
        for axis_no in range(3):
            at = axis_no * 32 + plane * 8
            field_ref[at : at + 8, :] = speeds[axis_no]

    outer = []
    for member in range(19):
        if member in falling:
            low = four(down_ref, AT_NEXT + falling.index(member) * PLANES)
        else:
            low = four(below_ref, AT_POPS + (level + rising).index(member) * PLANES)
        if member in rising:
            top = four(up_ref, AT_NEXT + rising.index(member) * PLANES)
        else:
            top = four(above_ref, AT_POPS + (level + falling).index(member) * PLANES)
        outer.append(jnp.concatenate([low, top], 0))
    outer_density, outer_speeds = moments_of(outer)
    lows, tops = [], []
    for axis_no in range(3):
        at = AT_SPEED + axis_no * PLANES
        second = jnp.concatenate([four(above_ref, at), four(below_ref, at)], 0)
        lows.append(jnp.where(row < PLANES, outer_speeds[axis_no], second))
        tops.append(jnp.where(row < PLANES, second, outer_speeds[axis_no]))

    def beyond(ref, field, base_y):
        pairs = pairs_of(jnp.concatenate(field, 0))
        total = jnp.zeros((24, LANES), f32)
        for block in range(sources // 8):
            tile = AT_MARKS + 16 * block
            mark = jnp.concatenate([ref[tile : tile + 8, :], ref[tile + 8 : tile + 16, :]], 1)
            at = AT_Z + 2 * block
            base = jnp.concatenate([ref[at : at + 1, :], ref[at + 1 : at + 2, :]], 1)
            spot = spots(base)
            found = gathered(pairs, spot)
            place = iota((ROWS, 2 * LANES), 0)
            frac = mark[3:4, :]
            weight = along_x(mark, (place % PLANES).astype(f32))
            weight = weight * jnp.where(place < PLANES, frac, 1.0 - frac)
            weight = jnp.where(mark[1:2, :] == base_y, weight, 0.0)
            frac = mark[4:5, :]
            spreads = []
            for axis_no in range(3):
                here = found[axis_no * 8 : axis_no * 8 + 8]
                there = found[24 + axis_no * 8 : 32 + axis_no * 8]
                value = weight * (here + frac * (there - here))
                force = mark[5 + axis_no : 6 + axis_no, :] - jnp.sum(value, 0, keepdims=True)
                spreads.append(weight * force)
            spreads = jnp.concatenate(spreads, 0)
            ahead = spreads * frac
            total = total + scattered(spreads - ahead, ahead, spot)
        return total

    from_below = beyond(below_ref, lows, float(ROWS - 2))
    from_above = beyond(above_ref, tops, 0.0)
    outer_pulls = [
        jnp.where(row < PLANES, from_below[a * 8 : a * 8 + 8], from_above[a * 8 : a * 8 + 8])
        for a in range(3)
    ]
    relax = relax_of(outer, outer_density, outer_speeds)
    outer_post = relaxed(outer, outer_density, outer_speeds, relax, outer_pulls)
    for number in range(5):
        outer_ref[number] = jnp.where(
            row < PLANES, outer_post[rising[number]], outer_post[falling[number]]
        )

    pairs = pairs_of(field_ref[...])
    total = jnp.zeros((96, LANES), f32)
    kept = [jnp.zeros((ROWS, LANES), f32) for axis_no in range(3)]
    for block in range(sources // 8):
        tile = AT_MARKS + 16 * block
        mark = jnp.concatenate([up_ref[tile : tile + 8, :], up_ref[tile + 8 : tile + 16, :]], 1)
        at = AT_Z + 2 * block
        spot = spots(jnp.concatenate([up_ref[at : at + 1, :], up_ref[at + 1 : at + 2, :]], 1))
        found = gathered(pairs, spot)
        forces, spreads = forces_of(
            mark,
            block_weights(mark),
            [found[at * 8 : at * 8 + 8] for at in range(12)],
            [found[96 + at * 8 : 104 + at * 8] for at in range(12)],
        )
        spreads = jnp.concatenate(spreads, 0)
        ahead = spreads * mark[4:5, :]
        total = total + scattered(spreads - ahead, ahead, spot)
        for half in range(2):
            lanes = slice(half * LANES, (half + 1) * LANES)
            for axis_no in range(3):
                kept[axis_no] = jnp.where(
                    row == 2 * block + half, forces[axis_no][:, lanes], kept[axis_no]
                )
    back_ref[...] = jnp.zeros(back_ref.shape, f32)
    for part in range(4):
        value = roll(kept[0], -SHARE * part, 1)
        for axis_no in range(1, 3):
            moved = roll(kept[axis_no], SHARE * (axis_no - part), 1)
            value = jnp.where(lane // SHARE == axis_no, moved, value)
        for tile in range(sources // 4):
            back_ref[4 * tile + part, 0:1, :] = value[tile : tile + 1, :]

    for plane in range(PLANES):
        ats = [a * 32 + plane * 8 for a in range(3)]
        pops = [wide_ref[member, plane] for member in range(19)]
        speeds = [field_ref[at : at + 8, :] for at in ats]
        density = density_ref[plane]
        relax = relax_of(pops, density, speeds)
        results = relaxed(pops, density, speeds, relax, [total[at : at + 8, :] for at in ats])
        for member in range(19):
            post_ref[member, plane] = results[member]

    to_right, to_left = jnp.zeros((ROWS, LANES), f32), jnp.zeros((ROWS, LANES), f32)
    for plane in range(PLANES):
        for member in range(19):
            shift_x, shift_y, shift_z = velocity_table[member]
            source = (plane - shift_x) % PLANES
            value = post_ref[member, source]
            if shift_y == 1:
                edge = outer_ref[rising.index(member), source : source + 1, :]
                value = jnp.where(row == 0, edge, roll(value, 1, 0))
            if shift_y == -1:
                at = PLANES + source
                edge = outer_ref[falling.index(member), at : at + 1, :]
                value = jnp.where(row == ROWS - 1, edge, roll(value, -1, 0))
            if shift_z:
                value = roll(value, shift_z, 1)
            if shift_z == 1:
                place = ahead_z.index(member) * PLANES + plane
                to_right = jnp.where(lane == place, roll(value, place, 1), to_right)
            if shift_z == -1:
                place = back_z.index(member) * PLANES + plane
                to_left = jnp.where(lane == place, roll(value, place + 1, 1), to_left)
            if shift_y == 1:
                value = jnp.where(row == first_wall, post_ref[opposite[member], plane], value)
            if shift_y == -1:
                value = jnp.where(row == last_wall, post_ref[opposite[member], plane], value)
            moved_ref[member, plane] = value
    for target, face in ((left, to_left), (right, to_right)):
        early, late = jnp.zeros((ROWS, LANES), f32), jnp.zeros((ROWS, LANES), f32)
        for number in range(ROWS):
            early = jnp.where(row == number, roll(face, EARLY * number, 1), early)
            late = jnp.where(row == number, roll(face, LATE_FACE - EARLY + 4 * number, 1), late)
        early = jnp.where(lane // EARLY == row, early, 0.0)
        late = jnp.where((lane - LATE_FACE) // 4 == row, late, 0.0)
        late = jnp.where(lane >= LATE_FACE, late, 0.0)
        mine = jnp.where(iota((1, LANES), 1) < LATE_FACE, back_ref[target, 0:1, :], 0.0)
        back_ref[target, 0:1, :] = mine + jnp.sum(late, 0, keepdims=True)
        back_ref[target, 1:2, :] = jnp.sum(early, 0, keepdims=True)


def last_kernel(
    moved_ref, got_ref, owner_ref, rank_ref, pops_ref, force_ref
):
    left, right = z_neighbours()
    _, _, first_wall, last_wall = y_ends()
    lane = iota((ROWS, LANES), 1)
    row = iota((ROWS, LANES), 0)

    def face_of(source):
        late = jnp.broadcast_to(got_ref[source, 0:1, :], (ROWS, LANES))
        early = jnp.broadcast_to(got_ref[source, 1:2, :], (ROWS, LANES))
        face = jnp.zeros((ROWS, LANES), f32)
        for number in range(ROWS):
            value = roll(late, EARLY - LATE_FACE - 4 * number, 1)
            value = jnp.where(lane < EARLY, roll(early, -EARLY * number, 1), value)
            face = jnp.where(row == number, value, face)
        return face

    from_left, from_right = face_of(left), face_of(right)
    changed = [i for i in range(19) if velocity_table[i][2]]
    for member in range(19):
        if member not in changed:
            pops_ref[member] = moved_ref[member]
    for number, member in enumerate(changed):
        _, shift_y, shift_z = velocity_table[member]
        for plane in range(PLANES):
            if shift_z == 1:
                place = ahead_z.index(member) * PLANES + plane
                edge, here = roll(from_left, -place, 1), lane == 0
            else:
                place = back_z.index(member) * PLANES + plane
                edge, here = roll(from_right, LANES - 1 - place, 1), lane == LANES - 1
            if shift_y == 1:
                here = here & (row != first_wall)
            if shift_y == -1:
                here = here & (row != last_wall)
            pops_ref[member, plane] = jnp.where(here, edge, moved_ref[member, plane])
    owners, markers = got_ref.shape[0], owner_ref.shape[1]
    owner = owner_ref[...]
    spot = (iota((LANES, markers), 0).astype(f32) == rank_ref[...]).astype(bf16)
    rows = got_ref[:, 0, :]
    high, low = split_two(
        jnp.concatenate([roll(rows, -SHARE * axis_no, 1) for axis_no in range(3)], 0)
    )
    found = jnp.dot(
        jnp.concatenate([high, low], 1),
        jnp.concatenate([spot, spot], 0),
        preferred_element_type=f32,
    )
    hit = iota((owners, markers), 0) == owner
    for axis_no in range(3):
        value = jnp.where(hit, found[axis_no * owners : (axis_no + 1) * owners], 0.0)
        force_ref[axis_no : axis_no + 1, :] = jnp.sum(value, 0, keepdims=True) / ref_speed


def body(populations, marker_owner, marker_cell, marker_frac, marker_speed, marker_count):
    count_gy, count_gz = lax.axis_size("gy"), lax.axis_size("gz")
    markers = marker_owner.shape[0]
    vmem = pl.BlockSpec(memory_space=pltpu.VMEM)
    shape = jax.ShapeDtypeStruct
    tiles = shape((count_gz, 8, LANES), f32)
    field = shape((96, LANES), f32)
    cells = shape((PLANES, ROWS, LANES), f32)
    lattice = shape(populations.shape, f32)
    inputs = [
        marker_owner.reshape(1, markers),
        marker_cell,
        marker_frac,
        marker_speed,
        populations,
    ]
    send, rank, live, speeds, density, relax = call(
        first_kernel,
        [tiles, shape((1, markers), f32), shape((1, markers), jnp.int32), field, cells, cells],
        [marker_count.reshape(1, 1)]
        + [pltpu.with_memory_space_constraint(value, pltpu.HBM) for value in inputs],
        [vmem] + [pl.BlockSpec(memory_space=pltpu.HBM)] * 5,
        scratch=[pltpu.VMEM(value.shape, value.dtype) for value in inputs]
        + [pltpu.SemaphoreType.DMA((5,))],
    )
    got = lax.all_to_all(send, "gz", split_axis=0, concat_axis=0, tiled=True)
    face = shape((FACE_ROWS, LANES), f32)
    next_pops, up, down = call(
        second_kernel,
        [lattice, face, face],
        [populations, got, speeds, density, relax],
        [vmem] * 5,
        scratch=[
            pltpu.VMEM(populations.shape, f32),
            pltpu.VMEM((24, ROWS, LANES), f32),
            pltpu.VMEM((24, ROWS, LANES), f32),
            pltpu.VMEM((96, LANES), f32),
        ],
    )
    below = lax.ppermute(up, "gy", [(i, (i + 1) % count_gy) for i in range(count_gy)])
    above = lax.ppermute(down, "gy", [((i + 1) % count_gy, i) for i in range(count_gy)])
    moved, back = call(
        third_kernel,
        [lattice, shape((count_gz, 2, LANES), f32)],
        [next_pops, up, down, below, above],
        [vmem] * 5,
        scratch=[
            pltpu.VMEM(populations.shape, f32),
            pltpu.VMEM((96, LANES), f32),
            pltpu.VMEM((PLANES, ROWS, LANES), f32),
            pltpu.VMEM(populations.shape, f32),
            pltpu.VMEM((5, ROWS, LANES), f32),
        ],
    )
    back = lax.all_to_all(back, "gz", split_axis=0, concat_axis=0, tiled=True)
    pops, force = call(
        last_kernel,
        [lattice, shape((3, markers), f32)],
        [moved, back, live, rank],
        [vmem] * 4,
    )
    return pops, force


def solution(mesh):
    return jax.shard_map(
        body,
        mesh=mesh,
        in_specs=(
            P(None, None, "gy", "gz"),
            P(("gy", "gz"), None),
            P(None, ("gy", "gz")),
            P(None, ("gy", "gz")),
            P(None, ("gy", "gz")),
            P(("gy", "gz")),
        ),
        out_specs=(P(None, None, "gy", "gz"), P(None, ("gy", "gz"))),
        check_vma=False,
    )
```

```python
import math

import jax
import jax.numpy as jnp
from jax import lax
from jax.experimental import pallas as pl
from jax.experimental.pallas import tpu as pltpu
from jax.sharding import PartitionSpec as P

INTERPRET = False

velocity_table = (
    (0, 0, 0),
    (1, 0, 0),
    (-1, 0, 0),
    (0, 1, 0),
    (0, -1, 0),
    (0, 0, 1),
    (0, 0, -1),
    (1, 1, 0),
    (-1, -1, 0),
    (1, -1, 0),
    (-1, 1, 0),
    (1, 0, 1),
    (-1, 0, -1),
    (1, 0, -1),
    (-1, 0, 1),
    (0, 1, 1),
    (0, -1, -1),
    (0, 1, -1),
    (0, -1, 1),
)
opposite = (0, 2, 1, 4, 3, 6, 5, 8, 7, 10, 9, 12, 11, 14, 13, 16, 15, 18, 17)
rising = tuple(i for i in range(19) if velocity_table[i][1] == 1)
falling = tuple(opposite[i] for i in rising)
level = tuple(i for i in range(19) if velocity_table[i][1] == 0)
ahead_z = tuple(i for i in range(19) if velocity_table[i][2] == 1)
back_z = tuple(opposite[i] for i in ahead_z)
tau_base = 0.52
smag_const = 0.17
ref_speed = 0.05

PLANES = 4
ROWS = 8
LANES = 128
SLOTS = 24
SHARE = 32
FEW = 4
SPARE = SLOTS - FEW
FIRST_SPARE = SHARE
FIRST_Z = SHARE + 2 * SPARE
FIRST_RIM = 76
LATE_FACE = 3 * SHARE
EARLY = 16
RIM_WORDS = 13
AT_SPEED, AT_POPS, AT_NEXT, AT_MARKS, AT_Z, FACE_ROWS = 0, 12, 68, 88, 152, 160

f32 = jnp.float32
bf16 = jnp.bfloat16


def iota(shape, dim):
    return lax.broadcasted_iota(jnp.int32, shape, dim)


def roll(value, shift, axis):
    shift = shift % value.shape[axis]
    return pltpu.roll(value, shift, axis) if shift else value


def split_two(value):
    high = value.astype(bf16)
    return high, (value - high.astype(f32)).astype(bf16)


def call(kernel, out_shape, args, in_specs, scratch=(), out_specs=None, aliases=()):
    vmem = pl.BlockSpec(memory_space=pltpu.VMEM)
    return pl.pallas_call(
        kernel,
        out_shape=out_shape,
        in_specs=in_specs,
        out_specs=out_specs or [vmem] * len(out_shape),
        input_output_aliases=dict(aliases),
        scratch_shapes=list(scratch),
        compiler_params=pltpu.CompilerParams(vmem_limit_bytes=32 * 1024 * 1024),
        interpret=INTERPRET,
    )(*args)


def z_neighbours():
    column, size = lax.axis_index("gz"), lax.axis_size("gz")
    return (column + size - 1) % size, (column + 1) % size


def y_ends():
    place, size = lax.axis_index("gy"), lax.axis_size("gy")
    first, last = place == 0, place == size - 1
    return (
        jnp.where(first, -1, 0),
        jnp.where(last, -1, ROWS - 1),
        jnp.where(first, 0, -1),
        jnp.where(last, ROWS - 1, -1),
    )


def moments_of(pops):
    density = pops[0]
    for member in range(1, 19):
        density = density + pops[member]
    parts = []
    for axis_no in range(3):
        total = None
        for member in range(19):
            if velocity_table[member][axis_no] == 1:
                total = pops[member] if total is None else total + pops[member]
        for member in range(19):
            if velocity_table[member][axis_no] == -1:
                total = total - pops[member]
        parts.append(total)
    inverse = 1.0 / density
    return density, [part * inverse for part in parts]


def relax_of(pops, density, speeds):
    factor = 18.0 * math.sqrt(2.0) * smag_const * smag_const
    moved = [density * part for part in speeds]
    pair = [pops[2 * k + 1] + pops[2 * k + 2] for k in range(9)]
    third = density * (1.0 / 3.0)
    xx = pair[0] + pair[3] + pair[4] + pair[5] + pair[6] - third - moved[0] * speeds[0]
    yy = pair[1] + pair[3] + pair[4] + pair[7] + pair[8] - third - moved[1] * speeds[1]
    zz = pair[2] + pair[5] + pair[6] + pair[7] + pair[8] - third - moved[2] * speeds[2]
    xy = pair[3] - pair[4] - moved[0] * speeds[1]
    xz = pair[5] - pair[6] - moved[0] * speeds[2]
    yz = pair[7] - pair[8] - moved[1] * speeds[2]
    norm_sq = xx * xx + yy * yy + zz * zz + 2.0 * (xy * xy + xz * xz + yz * yz)
    return 0.5 * (tau_base + jnp.sqrt(tau_base * tau_base + factor * jnp.sqrt(norm_sq) / density))


def along_of(member, speeds):
    total = None
    for axis_no in range(3):
        if velocity_table[member][axis_no] == 1:
            total = speeds[axis_no] if total is None else total + speeds[axis_no]
    for axis_no in range(3):
        if velocity_table[member][axis_no] == -1:
            total = total - speeds[axis_no]
    return total


def relaxed(pops, density, speeds, relax, pulls):
    pull = relax / density
    shifted = [speeds[a] + pull * pulls[a] for a in range(3)]
    shifted_sq = shifted[0] * shifted[0] + shifted[1] * shifted[1] + shifted[2] * shifted[2]
    rate = 1.0 / relax
    keep = 1.0 - rate
    scale = rate * density
    base = scale * (1.0 - 1.5 * shifted_sq)
    quad = 4.5 * scale
    results = [keep * pops[0] + base * (1.0 / 3.0)]
    for pair in range(9):
        plus = 2 * pair + 1
        along = along_of(plus, shifted)
        weight = 1.0 / 18.0 if pair < 3 else 1.0 / 36.0
        even = weight * (base + quad * along * along)
        odd = (3.0 * weight) * (scale * along)
        results.append(keep * pops[plus] + (even + odd))
        results.append(keep * pops[plus + 1] + (even - odd))
    return results


def along_x(mark, plane):
    base, frac = mark[0:1, :], mark[2:3, :]
    following = jnp.where(base == float(PLANES), 0.0, base)
    weight = jnp.where(base - 1.0 == plane, 1.0 - frac, 0.0)
    return jnp.where((base > 0.5) & (following == plane), frac, weight)


def block_weights(mark):
    base, frac = mark[1:2, :], mark[3:4, :]
    row = iota((ROWS, mark.shape[1]), 0).astype(f32)
    along_y = jnp.where(row == base, 1.0 - frac, jnp.where(row == base + 1.0, frac, 0.0))
    return [along_y * along_x(mark, float(plane)) for plane in range(PLANES)]


def spots(base_z):
    count = base_z.shape[1]
    return jnp.where(iota((LANES, count), 0).astype(f32) == base_z, 1.0, 0.0).astype(bf16)


def pairs_of(field):
    high, low = split_two(field)
    next_high, next_low = split_two(roll(field, -1, 1))
    return jnp.concatenate(
        [jnp.concatenate([high, low], 1), jnp.concatenate([next_high, next_low], 1)], 0
    )


def gathered(pairs, spot):
    return jnp.dot(pairs, jnp.concatenate([spot, spot], 0), preferred_element_type=f32)


def sums_of(here, there, spot):
    size = here.shape[0]
    high, low = split_two(here)
    next_high, next_low = split_two(there)
    sums = lax.dot_general(
        jnp.concatenate([high, low, next_high, next_low], 0),
        spot,
        (((1,), (1,)), ((), ())),
        preferred_element_type=f32,
    )
    first = sums[0:size] + sums[size : 2 * size]
    second = sums[2 * size : 3 * size] + sums[3 * size :]
    return first, second


def scattered(here, there, spot):
    first, second = sums_of(here, there, spot)
    return first + roll(second, 1, 1)


def forces_of(mark, weights, here, there):
    frac = mark[4:5, :]
    forces, spreads = [], []
    for axis_no in range(3):
        total = None
        for plane in range(PLANES):
            at = axis_no * PLANES + plane
            value = weights[plane] * (here[at] + frac * (there[at] - here[at]))
            total = value if total is None else total + value
        force = mark[5 + axis_no : 6 + axis_no, :] - jnp.sum(total, 0, keepdims=True)
        forces.append(force)
        for plane in range(PLANES):
            spreads.append(weights[plane] * force)
    return forces, spreads


def first_kernel(
    count_ref, owner_hbm, cell_hbm, frac_hbm, speed_hbm, pops_hbm,
    send_ref, rank_ref, live_ref, field_ref, density_ref, relax_ref,
    owner_ref, cell_ref, frac_ref, speed_ref, pops_ref, sems,
):
    copies = [
        pltpu.make_async_copy(source, target, sems.at[number])
        for number, (source, target) in enumerate(
            [
                (owner_hbm, owner_ref),
                (cell_hbm, cell_ref),
                (frac_hbm, frac_ref),
                (speed_hbm, speed_ref),
                (pops_hbm, pops_ref),
            ]
        )
    ]
    for copy in copies:
        copy.start()
    for copy in copies[0:4]:
        copy.wait()
    owners, markers = send_ref.shape[0], owner_ref.shape[1]
    live = iota((1, markers), 1) < count_ref[...]
    owner = jnp.where(live, owner_ref[...], -1)
    live_ref[...] = owner
    base_z = cell_ref[2:3, :]
    upper, lower = base_z == LANES - 2, base_z == 0
    twin = jnp.where(
        upper,
        jnp.where(owner == owners - 1, 0, owner + 1),
        jnp.where(owner == 0, owners - 1, owner - 1),
    )
    twin = jnp.where(live & (upper | lower), twin, -1)
    hit = iota((owners, markers), 0) == owner
    hits = jnp.concatenate(
        [hit.astype(f32), (hit & upper).astype(f32), (hit & lower).astype(f32)], 0
    )
    blocks = markers // LANES
    parts = [hits[:, block * LANES : (block + 1) * LANES] for block in range(blocks)]
    earlier = iota((LANES, 2 * LANES), 0) < iota((LANES, 2 * LANES), 1)
    counts = jnp.dot(
        jnp.concatenate(parts, 0).astype(bf16), earlier.astype(bf16), preferred_element_type=f32
    )
    before = None
    ranks = [[], [], []]
    for block in range(blocks):
        inner = counts[block * 3 * owners : (block + 1) * 3 * owners]
        place = inner[:, 0:LANES] if before is None else inner[:, 0:LANES] + before
        before = inner[:, LANES:] if before is None else inner[:, LANES:] + before
        picked = parts[block] * place
        for kind in range(3):
            ranks[kind].append(
                jnp.sum(picked[kind * owners : (kind + 1) * owners], 0, keepdims=True)
            )
    rank, rank_up, rank_low = [jnp.concatenate(kind, 1) for kind in ranks]
    rank_ref[...] = rank
    lane_up = jnp.where(rank_up < FEW, SLOTS + rank_up, FIRST_SPARE - FEW + rank_up)
    lane_low = jnp.where(
        rank_low < FEW, SLOTS + FEW + rank_low, FIRST_SPARE + SPARE - FEW + rank_low
    )
    lane_twin = jnp.where(upper, lane_up, lane_low)
    lane_z = FIRST_Z + jnp.where(rank >= 16.0, 2.0, jnp.where(rank >= 8.0, 1.0, 0.0))
    slot_z = rank - 8.0 * (lane_z - FIRST_Z)
    lane = iota((LANES, markers), 0).astype(f32)
    spot_own = (lane == rank).astype(bf16)
    spot_twin = (lane == lane_twin).astype(bf16)
    spot_z = (lane == lane_z).astype(bf16)
    row = iota((8, markers), 0)
    words = jnp.where(row == 0, cell_ref[0:1, :] + 1, cell_ref[1:2, :]).astype(f32)
    for number in range(3):
        words = jnp.where(row == 2 + number, frac_ref[number : number + 1, :], words)
        words = jnp.where(row == 5 + number, speed_ref[number : number + 1, :], words)
    high, low = split_two(words)
    high, low = high.astype(f32), low.astype(f32)
    words_z = jnp.where(row.astype(f32) == slot_z, base_z.astype(f32), 0.0)

    def to_owners(value, target):
        rows = [jnp.where(target == number, value, 0.0) for number in range(owners)]
        return jnp.concatenate(rows, 0).astype(bf16)

    def placed(left, spot):
        return lax.dot_general(left, spot, (((1,), (1,)), ((), ())), preferred_element_type=f32)

    tiles = placed(to_owners(high, owner), spot_own) + placed(to_owners(low, owner), spot_own)
    tiles = tiles + placed(to_owners(high, twin), spot_twin)
    tiles = tiles + placed(to_owners(low, twin), spot_twin)
    tiles = tiles + placed(to_owners(words_z, owner), spot_z)
    send_ref[...] = tiles.reshape(owners, 8, LANES)

    copies[4].wait()

    lane = iota((ROWS, LANES), 1)
    to_right, to_left = jnp.zeros((ROWS, LANES), f32), jnp.zeros((ROWS, LANES), f32)
    for plane in range(PLANES):
        pops = [pops_ref[member, plane] for member in range(19)]
        density, speeds = moments_of(pops)
        relax = relax_of(pops, density, speeds)
        density_ref[plane] = density
        relax_ref[plane] = relax
        for axis_no in range(3):
            at = axis_no * 32 + plane * 8
            field_ref[at : at + 8, :] = speeds[axis_no]
        common = [density, *speeds, relax]
        for word in range(RIM_WORDS):
            place = FIRST_RIM + word * PLANES + plane
            if word < 5:
                right, left, shift = common[word], common[word], 0
            elif word < 10:
                right, left, shift = pops[ahead_z[word - 5]], pops[back_z[word - 5]], 0
            else:
                right, left, shift = speeds[word - 10], speeds[word - 10], 1
            here = lane == place
            to_right = jnp.where(here, roll(right, place - (LANES - 1) + shift, 1), to_right)
            to_left = jnp.where(here, roll(left, place - shift, 1), to_left)
    left, right = z_neighbours()
    send_ref[left] = send_ref[left] + to_left
    send_ref[right] = send_ref[right] + to_right


def second_kernel(
    pops_ref, got_ref, field_ref, density_ref, relax_ref,
    next_ref, up_ref, down_ref,
    post_ref, near_ref, far_ref, twin_ref,
):
    left, right = z_neighbours()
    lane = iota((ROWS, LANES), 1)
    row = iota((ROWS, LANES), 0)
    sources = got_ref.shape[0]

    chosen = iota((LANES, LANES), 1) % SHARE
    chosen = (iota((LANES, LANES), 0) == FIRST_Z + chosen // 8) & (chosen < SLOTS)
    every_z = jnp.dot(
        got_ref[...].reshape(sources * 8, LANES).astype(bf16),
        chosen.astype(bf16),
        preferred_element_type=f32,
    )
    marks, bases = [], []
    for tile in range(sources // 4):
        words, place = None, None
        for part in range(4):
            source = tile * 4 + part
            value = roll(got_ref[source], SHARE * part, 1)
            spot = every_z[source * 8 : source * 8 + 8, :]
            if part:
                words = jnp.where(lane // SHARE == part, value, words)
                place = jnp.where(lane // SHARE == part, spot, place)
            else:
                words, place = value, spot
        place = jnp.sum(jnp.where(lane % 8 == row, place, 0.0), 0, keepdims=True)
        place = jnp.where(iota((1, LANES), 1) % SHARE < SLOTS, place, -5.0)
        marks.append(words)
        bases.append(place)
        for ref in (up_ref, down_ref):
            ref[AT_MARKS + tile * 8 : AT_MARKS + tile * 8 + 8, :] = words
            ref[AT_Z + tile : AT_Z + tile + 1, :] = place

    ends = jnp.where(lane >= FIRST_RIM, got_ref[left], roll(got_ref[right], 64, 1))
    rim = [roll(ends, -(FIRST_RIM + PLANES * word), 1) for word in range(RIM_WORDS)]

    def spread_lane(value, at):
        return jnp.broadcast_to(value[:, at : at + 1], (ROWS, LANES))

    for axis_no in range(3):
        for plane in range(PLANES):
            at = axis_no * PLANES + plane
            near_ref[at] = spread_lane(rim[10 + axis_no], plane)
            near_ref[12 + at] = spread_lane(rim[1 + axis_no], 64 + plane)
            far_ref[at] = spread_lane(rim[1 + axis_no], plane)
            far_ref[12 + at] = spread_lane(rim[10 + axis_no], 64 + plane)

    def twins(of_left, of_right):
        def both(ref):
            return [
                jnp.where(of_left, ref[at], jnp.where(of_right, ref[12 + at], 0.0))
                for at in range(12)
            ]

        return both(near_ref), both(far_ref)

    def sides(lefts, rights, count):
        place, member = iota((LANES, count), 0), iota((LANES, count), 1)
        chosen = jnp.where(place < 64, lefts(member).astype(f32), rights(member).astype(f32))
        return chosen.astype(bf16)

    of_left = (lane % SHARE >= SLOTS) & (lane % SHARE < SLOTS + FEW)
    of_right = lane % SHARE >= SLOTS + FEW
    near, far = twins(of_left, of_right)
    side = sides(
        lambda member: (member % SHARE >= SLOTS) & (member % SHARE < SLOTS + FEW),
        lambda member: member % SHARE >= SLOTS + FEW,
        2 * LANES,
    )
    of_rim = jnp.zeros((96, LANES), f32)
    rim_left = iota((96, LANES), 1) < 64
    pairs = pairs_of(field_ref[...])
    force = jnp.zeros((96, LANES), f32)
    for block in range(sources // 8):
        mark = jnp.concatenate(marks[2 * block : 2 * block + 2], 1)
        spot = spots(jnp.concatenate(bases[2 * block : 2 * block + 2], 1))
        found = gathered(pairs, spot)
        weights = block_weights(mark)
        here = [found[at * 8 : at * 8 + 8] + jnp.concatenate([near[at]] * 2, 1) for at in range(12)]
        there = [
            found[96 + at * 8 : 104 + at * 8] + jnp.concatenate([far[at]] * 2, 1) for at in range(12)
        ]
        _, spreads = forces_of(mark, weights, here, there)
        spreads = jnp.concatenate(spreads, 0)
        ahead = spreads * mark[4:5, :]
        first, second = sums_of(spreads - ahead, ahead, jnp.concatenate([spot, side], 0))
        force = force + (first[:, 0:LANES] + roll(second[:, 0:LANES], 1, 1))
        of_rim = of_rim + jnp.where(rim_left, second[:, LANES:], first[:, LANES:])
    twin_ref[...] = of_rim

    further = jnp.where((lane >= FIRST_SPARE) & (lane < FIRST_Z), 1.0, 0.0)
    most = got_ref[0]
    for source in range(1, sources):
        most = jnp.maximum(most, got_ref[source])

    @pl.when(jnp.max(most * further) > 0.5)
    def _():
        near, far = twins(lane < SPARE, lane >= SPARE)
        side = sides(lambda member: member < SPARE, lambda member: member >= SPARE, LANES)

        def one(source, carry):
            mark = roll(got_ref[source], -FIRST_SPARE, 1)
            mark = jnp.where(lane < 2 * SPARE, mark, 0.0)
            _, spreads = forces_of(mark, block_weights(mark), near, far)
            spreads = jnp.concatenate(spreads, 0)
            ahead = spreads * mark[4:5, :]
            first, second = sums_of(spreads - ahead, ahead, side)
            twin_ref[...] = twin_ref[...] + jnp.where(rim_left, second, first)
            return carry

        lax.fori_loop(0, sources, one, 0)

    sums = twin_ref[...]
    pulls = []
    for axis_no in range(3):
        total = None
        for plane in range(PLANES):
            at = axis_no * 32 + plane * 8
            value = sums[at : at + 8, :]
            total = value if total is None else jnp.where(lane % PLANES == plane, value, total)
        pulls.append(total)
    density, speeds, relax = rim[0], rim[1:4], rim[4]
    pull = relax / density
    shifted = [speeds[a] + pull * pulls[a] for a in range(3)]
    shifted_sq = shifted[0] * shifted[0] + shifted[1] * shifted[1] + shifted[2] * shifted[2]
    rate = 1.0 / relax
    sign = jnp.where(lane < 64, 1.0, -1.0)
    rim_post = []
    for number, member in enumerate(ahead_z):
        along = sign * along_of(member, shifted)
        weight = 1.0 / 18.0 if number == 0 else 1.0 / 36.0
        target = weight * density * (1.0 + 3.0 * along + 4.5 * along * along - 1.5 * shifted_sq)
        rim_post.append((1.0 - rate) * rim[5 + number] + rate * target)

    for plane in range(PLANES):
        ats = [a * 32 + plane * 8 for a in range(3)]
        results = relaxed(
            [pops_ref[member, plane] for member in range(19)],
            density_ref[plane],
            [field_ref[at : at + 8, :] for at in ats],
            relax_ref[plane],
            [force[at : at + 8, :] for at in ats],
        )
        for member in range(19):
            post_ref[member, plane] = results[member]

    for plane in range(PLANES):
        pops = []
        for member in range(19):
            shift_x, shift_y, shift_z = velocity_table[member]
            source = (plane - shift_x) % PLANES
            value = post_ref[member, source]
            if shift_z == 1:
                edge = roll(rim_post[ahead_z.index(member)], -source, 1)
                value = jnp.where(lane == 0, edge, roll(value, 1, 1))
            if shift_z == -1:
                edge = roll(rim_post[back_z.index(member)], 63 - source, 1)
                value = jnp.where(lane == LANES - 1, edge, roll(value, -1, 1))
            if shift_y == 1:
                at = AT_NEXT + rising.index(member) * PLANES + plane
                up_ref[at : at + 1, :] = value[ROWS - 1 : ROWS, :]
                value = jnp.where(row == 0, post_ref[opposite[member], plane], roll(value, 1, 0))
            if shift_y == -1:
                at = AT_NEXT + falling.index(member) * PLANES + plane
                down_ref[at : at + 1, :] = value[0:1, :]
                value = jnp.where(
                    row == ROWS - 1, post_ref[opposite[member], plane], roll(value, -1, 0)
                )
            next_ref[member, plane] = value
            pops.append(value)
        _, speeds = moments_of(pops)
        for axis_no in range(3):
            at = AT_SPEED + axis_no * PLANES + plane
            up_ref[at : at + 1, :] = speeds[axis_no][ROWS - 2 : ROWS - 1, :]
            down_ref[at : at + 1, :] = speeds[axis_no][1:2, :]
        for number, member in enumerate(level + rising):
            at = AT_POPS + number * PLANES + plane
            up_ref[at : at + 1, :] = pops[member][ROWS - 1 : ROWS, :]
        for number, member in enumerate(level + falling):
            at = AT_POPS + number * PLANES + plane
            down_ref[at : at + 1, :] = pops[member][0:1, :]


def third_kernel(
    next_ref, up_ref, down_ref, below_ref, above_ref,
    moved_ref, back_ref,
    wide_ref, field_ref, density_ref, post_ref, outer_ref,
):
    left, right = z_neighbours()
    first_open, last_open, first_wall, last_wall = y_ends()
    lane = iota((ROWS, LANES), 1)
    row = iota((ROWS, LANES), 0)
    sources = back_ref.shape[0]

    def four(ref, at):
        return ref[at : at + PLANES, :]

    for plane in range(PLANES):
        pops = []
        for member in range(19):
            value = next_ref[member, plane]
            if member in rising:
                at = AT_NEXT + rising.index(member) * PLANES + plane
                value = jnp.where(row == first_open, below_ref[at : at + 1, :], value)
            if member in falling:
                at = AT_NEXT + falling.index(member) * PLANES + plane
                value = jnp.where(row == last_open, above_ref[at : at + 1, :], value)
            wide_ref[member, plane] = value
            pops.append(value)
        density, speeds = moments_of(pops)
        density_ref[plane] = density
        for axis_no in range(3):
            at = axis_no * 32 + plane * 8
            field_ref[at : at + 8, :] = speeds[axis_no]

    outside = ((row < PLANES) & (first_wall == 0)) | ((row >= PLANES) & (last_wall > 0))
    outer = []
    for member in range(19):
        if member in falling:
            low = four(down_ref, AT_NEXT + falling.index(member) * PLANES)
        else:
            low = four(below_ref, AT_POPS + (level + rising).index(member) * PLANES)
        if member in rising:
            top = four(up_ref, AT_NEXT + rising.index(member) * PLANES)
        else:
            top = four(above_ref, AT_POPS + (level + falling).index(member) * PLANES)
        value = jnp.concatenate([low, top], 0)
        outer.append(jnp.where(outside, 0.0 if member else 1.0, value))
    outer_density, outer_speeds = moments_of(outer)
    lows, tops = [], []
    for axis_no in range(3):
        at = AT_SPEED + axis_no * PLANES
        second = jnp.concatenate([four(above_ref, at), four(below_ref, at)], 0)
        lows.append(jnp.where(row < PLANES, outer_speeds[axis_no], second))
        tops.append(jnp.where(row < PLANES, second, outer_speeds[axis_no]))

    def beyond(ref, field, base_y):
        pairs = pairs_of(jnp.concatenate(field, 0))
        total = jnp.zeros((24, LANES), f32)
        for block in range(sources // 8):
            tile = AT_MARKS + 16 * block
            mark = jnp.concatenate([ref[tile : tile + 8, :], ref[tile + 8 : tile + 16, :]], 1)
            at = AT_Z + 2 * block
            base = jnp.concatenate([ref[at : at + 1, :], ref[at + 1 : at + 2, :]], 1)
            spot = spots(base)
            found = gathered(pairs, spot)
            place = iota((ROWS, 2 * LANES), 0)
            frac = mark[3:4, :]
            weight = along_x(mark, (place % PLANES).astype(f32))
            weight = weight * jnp.where(place < PLANES, frac, 1.0 - frac)
            weight = jnp.where(mark[1:2, :] == base_y, weight, 0.0)
            frac = mark[4:5, :]
            spreads = []
            for axis_no in range(3):
                here = found[axis_no * 8 : axis_no * 8 + 8]
                there = found[24 + axis_no * 8 : 32 + axis_no * 8]
                value = weight * (here + frac * (there - here))
                force = mark[5 + axis_no : 6 + axis_no, :] - jnp.sum(value, 0, keepdims=True)
                spreads.append(weight * force)
            spreads = jnp.concatenate(spreads, 0)
            ahead = spreads * frac
            total = total + scattered(spreads - ahead, ahead, spot)
        return total

    from_below = beyond(below_ref, lows, float(ROWS - 2))
    from_above = beyond(above_ref, tops, 0.0)
    outer_pulls = [
        jnp.where(row < PLANES, from_below[a * 8 : a * 8 + 8], from_above[a * 8 : a * 8 + 8])
        for a in range(3)
    ]
    relax = relax_of(outer, outer_density, outer_speeds)
    outer_post = relaxed(outer, outer_density, outer_speeds, relax, outer_pulls)
    for number in range(5):
        outer_ref[number] = jnp.where(
            row < PLANES, outer_post[rising[number]], outer_post[falling[number]]
        )

    pairs = pairs_of(field_ref[...])
    total = jnp.zeros((96, LANES), f32)
    kept = [jnp.zeros((ROWS, LANES), f32) for axis_no in range(3)]
    for block in range(sources // 8):
        tile = AT_MARKS + 16 * block
        mark = jnp.concatenate([up_ref[tile : tile + 8, :], up_ref[tile + 8 : tile + 16, :]], 1)
        at = AT_Z + 2 * block
        spot = spots(jnp.concatenate([up_ref[at : at + 1, :], up_ref[at + 1 : at + 2, :]], 1))
        found = gathered(pairs, spot)
        forces, spreads = forces_of(
            mark,
            block_weights(mark),
            [found[at * 8 : at * 8 + 8] for at in range(12)],
            [found[96 + at * 8 : 104 + at * 8] for at in range(12)],
        )
        spreads = jnp.concatenate(spreads, 0)
        ahead = spreads * mark[4:5, :]
        total = total + scattered(spreads - ahead, ahead, spot)
        for half in range(2):
            lanes = slice(half * LANES, (half + 1) * LANES)
            for axis_no in range(3):
                kept[axis_no] = jnp.where(
                    row == 2 * block + half, forces[axis_no][:, lanes], kept[axis_no]
                )
    back_ref[...] = jnp.zeros(back_ref.shape, f32)
    for part in range(4):
        value = roll(kept[0], -SHARE * part, 1)
        for axis_no in range(1, 3):
            moved = roll(kept[axis_no], SHARE * (axis_no - part), 1)
            value = jnp.where(lane // SHARE == axis_no, moved, value)
        for tile in range(sources // 4):
            back_ref[4 * tile + part, 0:1, :] = value[tile : tile + 1, :]

    for plane in range(PLANES):
        ats = [a * 32 + plane * 8 for a in range(3)]
        pops = [wide_ref[member, plane] for member in range(19)]
        speeds = [field_ref[at : at + 8, :] for at in ats]
        density = density_ref[plane]
        relax = relax_of(pops, density, speeds)
        results = relaxed(pops, density, speeds, relax, [total[at : at + 8, :] for at in ats])
        for member in range(19):
            post_ref[member, plane] = results[member]

    to_right, to_left = jnp.zeros((ROWS, LANES), f32), jnp.zeros((ROWS, LANES), f32)
    for plane in range(PLANES):
        for member in range(19):
            shift_x, shift_y, shift_z = velocity_table[member]
            source = (plane - shift_x) % PLANES
            value = post_ref[member, source]
            if shift_y == 1:
                edge = outer_ref[rising.index(member), source : source + 1, :]
                value = jnp.where(row == 0, edge, roll(value, 1, 0))
            if shift_y == -1:
                at = PLANES + source
                edge = outer_ref[falling.index(member), at : at + 1, :]
                value = jnp.where(row == ROWS - 1, edge, roll(value, -1, 0))
            if shift_z:
                value = roll(value, shift_z, 1)
            if shift_z == 1:
                place = ahead_z.index(member) * PLANES + plane
                to_right = jnp.where(lane == place, roll(value, place, 1), to_right)
            if shift_z == -1:
                place = back_z.index(member) * PLANES + plane
                to_left = jnp.where(lane == place, roll(value, place + 1, 1), to_left)
            if shift_y == 1:
                value = jnp.where(row == first_wall, post_ref[opposite[member], plane], value)
            if shift_y == -1:
                value = jnp.where(row == last_wall, post_ref[opposite[member], plane], value)
            moved_ref[member, plane] = value
    for target, face in ((left, to_left), (right, to_right)):
        early, late = jnp.zeros((ROWS, LANES), f32), jnp.zeros((ROWS, LANES), f32)
        for number in range(ROWS):
            early = jnp.where(row == number, roll(face, EARLY * number, 1), early)
            late = jnp.where(row == number, roll(face, LATE_FACE - EARLY + 4 * number, 1), late)
        early = jnp.where(lane // EARLY == row, early, 0.0)
        late = jnp.where((lane - LATE_FACE) // 4 == row, late, 0.0)
        late = jnp.where(lane >= LATE_FACE, late, 0.0)
        mine = jnp.where(iota((1, LANES), 1) < LATE_FACE, back_ref[target, 0:1, :], 0.0)
        back_ref[target, 0:1, :] = mine + jnp.sum(late, 0, keepdims=True)
        back_ref[target, 1:2, :] = jnp.sum(early, 0, keepdims=True)


def last_kernel(
    moved_ref, got_ref, owner_ref, rank_ref, pops_ref, force_ref
):
    left, right = z_neighbours()
    _, _, first_wall, last_wall = y_ends()
    lane = iota((ROWS, LANES), 1)
    row = iota((ROWS, LANES), 0)

    def face_of(source):
        late = jnp.broadcast_to(got_ref[source, 0:1, :], (ROWS, LANES))
        early = jnp.broadcast_to(got_ref[source, 1:2, :], (ROWS, LANES))
        face = jnp.zeros((ROWS, LANES), f32)
        for number in range(ROWS):
            value = roll(late, EARLY - LATE_FACE - 4 * number, 1)
            value = jnp.where(lane < EARLY, roll(early, -EARLY * number, 1), value)
            face = jnp.where(row == number, value, face)
        return face

    from_left, from_right = face_of(left), face_of(right)
    changed = [i for i in range(19) if velocity_table[i][2]]
    for member in range(19):
        if member not in changed:
            pops_ref[member] = moved_ref[member]
    for number, member in enumerate(changed):
        _, shift_y, shift_z = velocity_table[member]
        for plane in range(PLANES):
            if shift_z == 1:
                place = ahead_z.index(member) * PLANES + plane
                edge, here = roll(from_left, -place, 1), lane == 0
            else:
                place = back_z.index(member) * PLANES + plane
                edge, here = roll(from_right, LANES - 1 - place, 1), lane == LANES - 1
            if shift_y == 1:
                here = here & (row != first_wall)
            if shift_y == -1:
                here = here & (row != last_wall)
            pops_ref[member, plane] = jnp.where(here, edge, moved_ref[member, plane])
    owners, markers = got_ref.shape[0], owner_ref.shape[1]
    owner = owner_ref[...]
    spot = (iota((LANES, markers), 0).astype(f32) == rank_ref[...]).astype(bf16)
    rows = got_ref[:, 0, :]
    high, low = split_two(
        jnp.concatenate([roll(rows, -SHARE * axis_no, 1) for axis_no in range(3)], 0)
    )
    found = jnp.dot(
        jnp.concatenate([high, low], 1),
        jnp.concatenate([spot, spot], 0),
        preferred_element_type=f32,
    )
    hit = iota((owners, markers), 0) == owner
    for axis_no in range(3):
        value = jnp.where(hit, found[axis_no * owners : (axis_no + 1) * owners], 0.0)
        force_ref[axis_no : axis_no + 1, :] = jnp.sum(value, 0, keepdims=True) / ref_speed


def body(populations, marker_owner, marker_cell, marker_frac, marker_speed, marker_count):
    count_gy, count_gz = lax.axis_size("gy"), lax.axis_size("gz")
    markers = marker_owner.shape[0]
    vmem = pl.BlockSpec(memory_space=pltpu.VMEM)
    shape = jax.ShapeDtypeStruct
    tiles = shape((count_gz, 8, LANES), f32)
    field = shape((96, LANES), f32)
    cells = shape((PLANES, ROWS, LANES), f32)
    lattice = shape(populations.shape, f32)
    inputs = [
        marker_owner.reshape(1, markers),
        marker_cell,
        marker_frac,
        marker_speed,
        populations,
    ]
    send, rank, live, speeds, density, relax = call(
        first_kernel,
        [tiles, shape((1, markers), f32), shape((1, markers), jnp.int32), field, cells, cells],
        [marker_count.reshape(1, 1)]
        + [pltpu.with_memory_space_constraint(value, pltpu.HBM) for value in inputs],
        [vmem] + [pl.BlockSpec(memory_space=pltpu.HBM)] * 5,
        scratch=[pltpu.VMEM(value.shape, value.dtype) for value in inputs]
        + [pltpu.SemaphoreType.DMA((5,))],
    )
    got = lax.all_to_all(send, "gz", split_axis=0, concat_axis=0, tiled=True)
    face = shape((FACE_ROWS, LANES), f32)
    next_pops, up, down = call(
        second_kernel,
        [lattice, face, face],
        [populations, got, speeds, density, relax],
        [vmem] * 5,
        scratch=[
            pltpu.VMEM(populations.shape, f32),
            pltpu.VMEM((24, ROWS, LANES), f32),
            pltpu.VMEM((24, ROWS, LANES), f32),
            pltpu.VMEM((96, LANES), f32),
        ],
    )
    below = lax.ppermute(up, "gy", [(i, i + 1) for i in range(count_gy - 1)])
    above = lax.ppermute(down, "gy", [(i + 1, i) for i in range(count_gy - 1)])
    moved, back = call(
        third_kernel,
        [lattice, shape((count_gz, 2, LANES), f32)],
        [next_pops, up, down, below, above],
        [vmem] * 5,
        scratch=[
            pltpu.VMEM(populations.shape, f32),
            pltpu.VMEM((96, LANES), f32),
            pltpu.VMEM((PLANES, ROWS, LANES), f32),
            pltpu.VMEM(populations.shape, f32),
            pltpu.VMEM((5, ROWS, LANES), f32),
        ],
    )
    back = lax.all_to_all(back, "gz", split_axis=0, concat_axis=0, tiled=True)
    pops, force = call(
        last_kernel,
        [lattice, shape((3, markers), f32)],
        [moved, back, live, rank],
        [vmem] * 4,
    )
    return pops, force


def solution(mesh):
    return jax.shard_map(
        body,
        mesh=mesh,
        in_specs=(
            P(None, None, "gy", "gz"),
            P(("gy", "gz"), None),
            P(None, ("gy", "gz")),
            P(None, ("gy", "gz")),
            P(None, ("gy", "gz")),
            P(("gy", "gz")),
        ),
        out_specs=(P(None, None, "gy", "gz"), P(None, ("gy", "gz"))),
        check_vma=False,
    )
```

```python
import math

import jax
import jax.numpy as jnp
from jax import lax
from jax.experimental import pallas as pl
from jax.experimental.pallas import tpu as pltpu
from jax.sharding import PartitionSpec as P

INTERPRET = False

velocity_table = (
    (0, 0, 0),
    (1, 0, 0),
    (-1, 0, 0),
    (0, 1, 0),
    (0, -1, 0),
    (0, 0, 1),
    (0, 0, -1),
    (1, 1, 0),
    (-1, -1, 0),
    (1, -1, 0),
    (-1, 1, 0),
    (1, 0, 1),
    (-1, 0, -1),
    (1, 0, -1),
    (-1, 0, 1),
    (0, 1, 1),
    (0, -1, -1),
    (0, 1, -1),
    (0, -1, 1),
)
opposite = (0, 2, 1, 4, 3, 6, 5, 8, 7, 10, 9, 12, 11, 14, 13, 16, 15, 18, 17)
rising = tuple(i for i in range(19) if velocity_table[i][1] == 1)
falling = tuple(opposite[i] for i in rising)
level = tuple(i for i in range(19) if velocity_table[i][1] == 0)
ahead_z = tuple(i for i in range(19) if velocity_table[i][2] == 1)
back_z = tuple(opposite[i] for i in ahead_z)
tau_base = 0.52
smag_const = 0.17
ref_speed = 0.05

PLANES = 4
ROWS = 8
LANES = 128
SLOTS = 24
SHARE = 32
FEW = 4
SPARE = SLOTS - FEW
FIRST_SPARE = SHARE
FIRST_Z = SHARE + 2 * SPARE
FIRST_RIM = 76
LATE_FACE = 3 * SHARE
EARLY = 16
RIM_WORDS = 13
AT_SPEED, AT_POPS, AT_NEXT, AT_MARKS, AT_Z, FACE_ROWS = 0, 12, 68, 88, 136, 144

f32 = jnp.float32
bf16 = jnp.bfloat16


def iota(shape, dim):
    return lax.broadcasted_iota(jnp.int32, shape, dim)


def roll(value, shift, axis):
    shift = shift % value.shape[axis]
    return pltpu.roll(value, shift, axis) if shift else value


def split_two(value):
    high = value.astype(bf16)
    return high, (value - high.astype(f32)).astype(bf16)


def call(kernel, out_shape, args, in_specs, scratch=(), out_specs=None, aliases=()):
    vmem = pl.BlockSpec(memory_space=pltpu.VMEM)
    return pl.pallas_call(
        kernel,
        out_shape=out_shape,
        in_specs=in_specs,
        out_specs=out_specs or [vmem] * len(out_shape),
        input_output_aliases=dict(aliases),
        scratch_shapes=list(scratch),
        compiler_params=pltpu.CompilerParams(vmem_limit_bytes=32 * 1024 * 1024),
        interpret=INTERPRET,
    )(*args)


def z_neighbours():
    column, size = lax.axis_index("gz"), lax.axis_size("gz")
    return (column + size - 1) % size, (column + 1) % size


def y_ends():
    place, size = lax.axis_index("gy"), lax.axis_size("gy")
    first, last = place == 0, place == size - 1
    return (
        jnp.where(first, -1, 0),
        jnp.where(last, -1, ROWS - 1),
        jnp.where(first, 0, -1),
        jnp.where(last, ROWS - 1, -1),
    )


def moments_of(pops):
    density = pops[0]
    for member in range(1, 19):
        density = density + pops[member]
    parts = []
    for axis_no in range(3):
        total = None
        for member in range(19):
            if velocity_table[member][axis_no] == 1:
                total = pops[member] if total is None else total + pops[member]
        for member in range(19):
            if velocity_table[member][axis_no] == -1:
                total = total - pops[member]
        parts.append(total)
    inverse = 1.0 / density
    return density, [part * inverse for part in parts]


def relax_of(pops, density, speeds):
    factor = 18.0 * math.sqrt(2.0) * smag_const * smag_const
    moved = [density * part for part in speeds]
    pair = [pops[2 * k + 1] + pops[2 * k + 2] for k in range(9)]
    third = density * (1.0 / 3.0)
    xx = pair[0] + pair[3] + pair[4] + pair[5] + pair[6] - third - moved[0] * speeds[0]
    yy = pair[1] + pair[3] + pair[4] + pair[7] + pair[8] - third - moved[1] * speeds[1]
    zz = pair[2] + pair[5] + pair[6] + pair[7] + pair[8] - third - moved[2] * speeds[2]
    xy = pair[3] - pair[4] - moved[0] * speeds[1]
    xz = pair[5] - pair[6] - moved[0] * speeds[2]
    yz = pair[7] - pair[8] - moved[1] * speeds[2]
    norm_sq = xx * xx + yy * yy + zz * zz + 2.0 * (xy * xy + xz * xz + yz * yz)
    return 0.5 * (tau_base + jnp.sqrt(tau_base * tau_base + factor * jnp.sqrt(norm_sq) / density))


def along_of(member, speeds):
    total = None
    for axis_no in range(3):
        if velocity_table[member][axis_no] == 1:
            total = speeds[axis_no] if total is None else total + speeds[axis_no]
    for axis_no in range(3):
        if velocity_table[member][axis_no] == -1:
            total = total - speeds[axis_no]
    return total


def relaxed(pops, density, speeds, relax, pulls):
    pull = relax / density
    shifted = [speeds[a] + pull * pulls[a] for a in range(3)]
    shifted_sq = shifted[0] * shifted[0] + shifted[1] * shifted[1] + shifted[2] * shifted[2]
    rate = 1.0 / relax
    keep = 1.0 - rate
    scale = rate * density
    base = scale * (1.0 - 1.5 * shifted_sq)
    quad = 4.5 * scale
    results = [keep * pops[0] + base * (1.0 / 3.0)]
    for pair in range(9):
        plus = 2 * pair + 1
        along = along_of(plus, shifted)
        weight = 1.0 / 18.0 if pair < 3 else 1.0 / 36.0
        even = weight * (base + quad * along * along)
        odd = (3.0 * weight) * (scale * along)
        results.append(keep * pops[plus] + (even + odd))
        results.append(keep * pops[plus + 1] + (even - odd))
    return results


def along_x(mark, plane):
    base, frac = mark[0:1, :], mark[2:3, :]
    following = jnp.where(base == float(PLANES), 0.0, base)
    weight = jnp.where(base - 1.0 == plane, 1.0 - frac, 0.0)
    return jnp.where((base > 0.5) & (following == plane), frac, weight)


def block_weights(mark):
    base, frac = mark[1:2, :], mark[3:4, :]
    row = iota((ROWS, mark.shape[1]), 0).astype(f32)
    along_y = jnp.where(row == base, 1.0 - frac, jnp.where(row == base + 1.0, frac, 0.0))
    return [along_y * along_x(mark, float(plane)) for plane in range(PLANES)]


def spots(base_z):
    count = base_z.shape[1]
    one, none = jnp.ones((), bf16), jnp.zeros((), bf16)
    return jnp.where(iota((LANES, count), 0).astype(bf16) == base_z.astype(bf16), one, none)


def pairs_of(field):
    high, low = split_two(field)
    next_high, next_low = split_two(roll(field, -1, 1))
    return jnp.concatenate(
        [jnp.concatenate([high, low], 1), jnp.concatenate([next_high, next_low], 1)], 0
    )


def gathered(pairs, spot):
    return jnp.dot(pairs, jnp.concatenate([spot, spot], 0), preferred_element_type=f32)


def sums_of(here, there, spot):
    size = here.shape[0]
    high, low = split_two(here)
    next_high, next_low = split_two(there)
    sums = lax.dot_general(
        jnp.concatenate([high, low, next_high, next_low], 0),
        spot,
        (((1,), (1,)), ((), ())),
        preferred_element_type=f32,
    )
    first = sums[0:size] + sums[size : 2 * size]
    second = sums[2 * size : 3 * size] + sums[3 * size :]
    return first, second


def scattered(here, there, spot):
    first, second = sums_of(here, there, spot)
    return first + roll(second, 1, 1)


def forces_of(mark, weights, here, there):
    frac = mark[4:5, :]
    forces, spreads = [], []
    for axis_no in range(3):
        total = None
        for plane in range(PLANES):
            at = axis_no * PLANES + plane
            value = weights[plane] * (here[at] + frac * (there[at] - here[at]))
            total = value if total is None else total + value
        force = mark[5 + axis_no : 6 + axis_no, :] - jnp.sum(total, 0, keepdims=True)
        forces.append(force)
        for plane in range(PLANES):
            spreads.append(weights[plane] * force)
    return forces, spreads


def first_kernel(
    count_ref, owner_hbm, cell_hbm, frac_hbm, speed_hbm, pops_hbm,
    send_ref, rank_ref, live_ref, field_ref, density_ref, relax_ref,
    owner_ref, cell_ref, frac_ref, speed_ref, pops_ref, sems,
):
    copies = [
        pltpu.make_async_copy(source, target, sems.at[number])
        for number, (source, target) in enumerate(
            [
                (owner_hbm, owner_ref),
                (cell_hbm, cell_ref),
                (frac_hbm, frac_ref),
                (speed_hbm, speed_ref),
                (pops_hbm, pops_ref),
            ]
        )
    ]
    for copy in copies:
        copy.start()
    for copy in copies[0:4]:
        copy.wait()
    owners, markers = send_ref.shape[0], owner_ref.shape[1]
    live = iota((1, markers), 1) < count_ref[...]
    owner = jnp.where(live, owner_ref[...], -1)
    live_ref[...] = owner
    base_z = cell_ref[2:3, :]
    upper, lower = base_z == LANES - 2, base_z == 0
    twin = jnp.where(
        upper,
        jnp.where(owner == owners - 1, 0, owner + 1),
        jnp.where(owner == 0, owners - 1, owner - 1),
    )
    twin = jnp.where(live & (upper | lower), twin, -1)
    hit = iota((owners, markers), 0) == owner
    hits = jnp.concatenate(
        [hit.astype(f32), (hit & upper).astype(f32), (hit & lower).astype(f32)], 0
    )
    blocks = markers // LANES
    parts = [hits[:, block * LANES : (block + 1) * LANES] for block in range(blocks)]
    earlier = iota((LANES, 2 * LANES), 0) < iota((LANES, 2 * LANES), 1)
    counts = jnp.dot(
        jnp.concatenate(parts, 0).astype(bf16), earlier.astype(bf16), preferred_element_type=f32
    )
    before = None
    ranks = [[], [], []]
    for block in range(blocks):
        inner = counts[block * 3 * owners : (block + 1) * 3 * owners]
        place = inner[:, 0:LANES] if before is None else inner[:, 0:LANES] + before
        before = inner[:, LANES:] if before is None else inner[:, LANES:] + before
        picked = parts[block] * place
        for kind in range(3):
            ranks[kind].append(
                jnp.sum(picked[kind * owners : (kind + 1) * owners], 0, keepdims=True)
            )
    rank, rank_up, rank_low = [jnp.concatenate(kind, 1) for kind in ranks]
    rank_ref[...] = rank
    copies[4].wait()
    lane_up = jnp.where(rank_up < FEW, SLOTS + rank_up, FIRST_SPARE - FEW + rank_up)
    lane_low = jnp.where(
        rank_low < FEW, SLOTS + FEW + rank_low, FIRST_SPARE + SPARE - FEW + rank_low
    )
    lane_twin = jnp.where(upper, lane_up, lane_low)
    lane_z = FIRST_Z + jnp.where(rank >= 16.0, 2.0, jnp.where(rank >= 8.0, 1.0, 0.0))
    slot_z = rank - 8.0 * (lane_z - FIRST_Z)
    lane = iota((LANES, markers), 0).astype(f32)
    spot_own = (lane == rank).astype(bf16)
    spot_twin = (lane == lane_twin).astype(bf16)
    spot_z = (lane == lane_z).astype(bf16)
    row = iota((8, markers), 0)
    words = jnp.where(row == 0, cell_ref[0:1, :] + 1, cell_ref[1:2, :]).astype(f32)
    for number in range(3):
        words = jnp.where(row == 2 + number, frac_ref[number : number + 1, :], words)
        words = jnp.where(row == 5 + number, speed_ref[number : number + 1, :], words)
    high, low = split_two(words)
    high, low = high.astype(f32), low.astype(f32)
    words_z = jnp.where(row.astype(f32) == slot_z, base_z.astype(f32), 0.0)

    def to_owners(value, target):
        value = jnp.concatenate([value, value], 0).astype(bf16)
        target = jnp.broadcast_to(target.astype(f32), (16, markers)).astype(bf16)
        first = jnp.where(iota((16, markers), 0) < 8, 0.0, 1.0).astype(bf16)
        rows = []
        for number in range(0, owners, 2):
            rows.append(jnp.where(target == first + float(number), value, jnp.zeros((), bf16)))
        return jnp.concatenate(rows, 0)

    def placed(left, spot):
        return lax.dot_general(left, spot, (((1,), (1,)), ((), ())), preferred_element_type=f32)

    tiles = placed(to_owners(high, owner), spot_own) + placed(to_owners(low, owner), spot_own)
    tiles = tiles + placed(to_owners(high, twin), spot_twin)
    tiles = tiles + placed(to_owners(low, twin), spot_twin)
    tiles = tiles + placed(to_owners(words_z, owner), spot_z)
    send_ref[...] = tiles.reshape(owners, 8, LANES)


    lane = iota((ROWS, LANES), 1)
    to_right, to_left = jnp.zeros((ROWS, LANES), f32), jnp.zeros((ROWS, LANES), f32)
    for plane in range(PLANES):
        pops = [pops_ref[member, plane] for member in range(19)]
        density, speeds = moments_of(pops)
        relax = relax_of(pops, density, speeds)
        density_ref[plane] = density
        relax_ref[plane] = relax
        for axis_no in range(3):
            at = axis_no * 32 + plane * 8
            field_ref[at : at + 8, :] = speeds[axis_no]
        common = [density, *speeds, relax]
        for word in range(RIM_WORDS):
            place = FIRST_RIM + word * PLANES + plane
            if word < 5:
                right, left, shift = common[word], common[word], 0
            elif word < 10:
                right, left, shift = pops[ahead_z[word - 5]], pops[back_z[word - 5]], 0
            else:
                right, left, shift = speeds[word - 10], speeds[word - 10], 1
            here = lane == place
            to_right = jnp.where(here, roll(right, place - (LANES - 1) + shift, 1), to_right)
            to_left = jnp.where(here, roll(left, place - shift, 1), to_left)
    left, right = z_neighbours()
    send_ref[left] = send_ref[left] + to_left
    send_ref[right] = send_ref[right] + to_right


def second_kernel(
    pops_ref, got_ref, field_ref, density_ref, relax_ref,
    next_ref, up_ref, down_ref,
    post_ref, near_ref, far_ref, twin_ref,
):
    left, right = z_neighbours()
    lane = iota((ROWS, LANES), 1)
    row = iota((ROWS, LANES), 0)
    sources = got_ref.shape[0]

    tiles = sources * SLOTS // LANES
    marks = [None] * tiles
    twin_marks = [None] * (sources * 2 * FEW // LANES)
    for source in range(sources):
        tile, first = divmod(source * SLOTS, LANES)
        words = roll(got_ref[source], first, 1)
        marks[tile] = words if marks[tile] is None else jnp.where(lane >= first, words, marks[tile])
        if first + SLOTS > LANES:
            marks[tile + 1] = words
        tile, first = divmod(source * 2 * FEW, LANES)
        words = roll(got_ref[source], first - SLOTS, 1)
        old = twin_marks[tile]
        twin_marks[tile] = words if old is None else jnp.where(lane >= first, words, old)
    bases = []
    for tile in range(tiles):
        first, last = tile * LANES // SLOTS, ((tile + 1) * LANES - 1) // SLOTS
        rows = jnp.concatenate([got_ref[source] for source in range(first, last + 1)], 0)

        def slot_of(shape):
            member = iota(shape, 1) + tile * LANES
            source = (member * 2731) >> 16
            return source, member - SLOTS * source

        _, slot = slot_of((LANES, LANES))
        chosen = (iota((LANES, LANES), 0) == FIRST_Z + (slot >> 3)).astype(bf16)
        value = jnp.dot(rows.astype(bf16), chosen, preferred_element_type=f32)
        source, slot = slot_of(value.shape)
        here = iota(value.shape, 0) == (source - first) * 8 + (slot & 7)
        bases.append(jnp.sum(jnp.where(here, value, 0.0), 0, keepdims=True))
    for ref in (up_ref, down_ref):
        for tile in range(tiles):
            ref[AT_MARKS + tile * 8 : AT_MARKS + tile * 8 + 8, :] = marks[tile]
            ref[AT_Z + tile : AT_Z + tile + 1, :] = bases[tile]
        ref[AT_Z + tiles : FACE_ROWS, :] = jnp.zeros((FACE_ROWS - AT_Z - tiles, LANES), f32)

    ends = jnp.where(lane >= FIRST_RIM, got_ref[left], roll(got_ref[right], 64, 1))
    rim = [roll(ends, -(FIRST_RIM + PLANES * word), 1) for word in range(RIM_WORDS)]

    def spread_lane(value, at):
        return jnp.broadcast_to(value[:, at : at + 1], (ROWS, LANES))

    for axis_no in range(3):
        for plane in range(PLANES):
            at = axis_no * PLANES + plane
            near_ref[at] = spread_lane(rim[10 + axis_no], plane)
            near_ref[12 + at] = spread_lane(rim[1 + axis_no], 64 + plane)
            far_ref[at] = spread_lane(rim[1 + axis_no], plane)
            far_ref[12 + at] = spread_lane(rim[10 + axis_no], 64 + plane)

    def twins(of_left, of_right):
        def both(ref):
            return [
                jnp.where(of_left, ref[at], jnp.where(of_right, ref[12 + at], 0.0))
                for at in range(12)
            ]

        return both(near_ref), both(far_ref)

    def sides(lefts, rights, count):
        place, member = iota((LANES, count), 0), iota((LANES, count), 1)
        chosen = jnp.where(place < 64, lefts(member).astype(f32), rights(member).astype(f32))
        return chosen.astype(bf16)

    near, far = twins(lane % (2 * FEW) < FEW, lane % (2 * FEW) >= FEW)
    side = sides(
        lambda member: member % (2 * FEW) < FEW,
        lambda member: member % (2 * FEW) >= FEW,
        2 * LANES,
    )
    rim_left = iota((96, LANES), 1) < 64
    pairs = pairs_of(field_ref[...])
    force = jnp.zeros((96, LANES), f32)
    for block in range(tiles // 2):
        mark = jnp.concatenate(marks[2 * block : 2 * block + 2], 1)
        spot = spots(jnp.concatenate(bases[2 * block : 2 * block + 2], 1))
        found = gathered(pairs, spot)
        _, spreads = forces_of(
            mark,
            block_weights(mark),
            [found[at * 8 : at * 8 + 8] for at in range(12)],
            [found[96 + at * 8 : 104 + at * 8] for at in range(12)],
        )
        spreads = jnp.concatenate(spreads, 0)
        ahead = spreads * mark[4:5, :]
        force = force + scattered(spreads - ahead, ahead, spot)
    mark = jnp.concatenate(twin_marks, 1)
    _, spreads = forces_of(
        mark,
        block_weights(mark),
        [jnp.concatenate([value] * 2, 1) for value in near],
        [jnp.concatenate([value] * 2, 1) for value in far],
    )
    spreads = jnp.concatenate(spreads, 0)
    ahead = spreads * mark[4:5, :]
    first, second = sums_of(spreads - ahead, ahead, side)
    twin_ref[...] = jnp.where(rim_left, second, first)

    further = jnp.where((lane >= FIRST_SPARE) & (lane < FIRST_Z), 1.0, 0.0)
    most = got_ref[0]
    for source in range(1, sources):
        most = jnp.maximum(most, got_ref[source])

    @pl.when(jnp.max(most * further) > 0.5)
    def _():
        near, far = twins(lane < SPARE, lane >= SPARE)
        side = sides(lambda member: member < SPARE, lambda member: member >= SPARE, LANES)

        def one(source, carry):
            mark = roll(got_ref[source], -FIRST_SPARE, 1)
            mark = jnp.where(lane < 2 * SPARE, mark, 0.0)
            _, spreads = forces_of(mark, block_weights(mark), near, far)
            spreads = jnp.concatenate(spreads, 0)
            ahead = spreads * mark[4:5, :]
            first, second = sums_of(spreads - ahead, ahead, side)
            twin_ref[...] = twin_ref[...] + jnp.where(rim_left, second, first)
            return carry

        lax.fori_loop(0, sources, one, 0)

    sums = twin_ref[...]
    pulls = []
    for axis_no in range(3):
        total = None
        for plane in range(PLANES):
            at = axis_no * 32 + plane * 8
            value = sums[at : at + 8, :]
            total = value if total is None else jnp.where(lane % PLANES == plane, value, total)
        pulls.append(total)
    density, speeds, relax = rim[0], rim[1:4], rim[4]
    pull = relax / density
    shifted = [speeds[a] + pull * pulls[a] for a in range(3)]
    shifted_sq = shifted[0] * shifted[0] + shifted[1] * shifted[1] + shifted[2] * shifted[2]
    rate = 1.0 / relax
    sign = jnp.where(lane < 64, 1.0, -1.0)
    rim_post = []
    for number, member in enumerate(ahead_z):
        along = sign * along_of(member, shifted)
        weight = 1.0 / 18.0 if number == 0 else 1.0 / 36.0
        target = weight * density * (1.0 + 3.0 * along + 4.5 * along * along - 1.5 * shifted_sq)
        rim_post.append((1.0 - rate) * rim[5 + number] + rate * target)

    for plane in range(PLANES):
        ats = [a * 32 + plane * 8 for a in range(3)]
        results = relaxed(
            [pops_ref[member, plane] for member in range(19)],
            density_ref[plane],
            [field_ref[at : at + 8, :] for at in ats],
            relax_ref[plane],
            [force[at : at + 8, :] for at in ats],
        )
        for member in range(19):
            post_ref[member, plane] = results[member]

    for plane in range(PLANES):
        pops = []
        for member in range(19):
            shift_x, shift_y, shift_z = velocity_table[member]
            source = (plane - shift_x) % PLANES
            value = post_ref[member, source]
            if shift_z == 1:
                edge = roll(rim_post[ahead_z.index(member)], -source, 1)
                value = jnp.where(lane == 0, edge, roll(value, 1, 1))
            if shift_z == -1:
                edge = roll(rim_post[back_z.index(member)], 63 - source, 1)
                value = jnp.where(lane == LANES - 1, edge, roll(value, -1, 1))
            if shift_y == 1:
                at = AT_NEXT + rising.index(member) * PLANES + plane
                up_ref[at : at + 1, :] = value[ROWS - 1 : ROWS, :]
                value = jnp.where(row == 0, post_ref[opposite[member], plane], roll(value, 1, 0))
            if shift_y == -1:
                at = AT_NEXT + falling.index(member) * PLANES + plane
                down_ref[at : at + 1, :] = value[0:1, :]
                value = jnp.where(
                    row == ROWS - 1, post_ref[opposite[member], plane], roll(value, -1, 0)
                )
            next_ref[member, plane] = value
            pops.append(value)
        _, speeds = moments_of(pops)
        for axis_no in range(3):
            at = AT_SPEED + axis_no * PLANES + plane
            up_ref[at : at + 1, :] = speeds[axis_no][ROWS - 2 : ROWS - 1, :]
            down_ref[at : at + 1, :] = speeds[axis_no][1:2, :]
        for number, member in enumerate(level + rising):
            at = AT_POPS + number * PLANES + plane
            up_ref[at : at + 1, :] = pops[member][ROWS - 1 : ROWS, :]
        for number, member in enumerate(level + falling):
            at = AT_POPS + number * PLANES + plane
            down_ref[at : at + 1, :] = pops[member][0:1, :]


def third_kernel(
    next_ref, up_ref, down_ref, below_ref, above_ref,
    moved_ref, back_ref,
    wide_ref, field_ref, density_ref, post_ref, outer_ref,
):
    left, right = z_neighbours()
    first_open, last_open, first_wall, last_wall = y_ends()
    lane = iota((ROWS, LANES), 1)
    row = iota((ROWS, LANES), 0)
    sources = back_ref.shape[0]
    tiles = sources * SLOTS // LANES

    def four(ref, at):
        return ref[at : at + PLANES, :]

    for plane in range(PLANES):
        pops = []
        for member in range(19):
            value = next_ref[member, plane]
            if member in rising:
                at = AT_NEXT + rising.index(member) * PLANES + plane
                value = jnp.where(row == first_open, below_ref[at : at + 1, :], value)
            if member in falling:
                at = AT_NEXT + falling.index(member) * PLANES + plane
                value = jnp.where(row == last_open, above_ref[at : at + 1, :], value)
            wide_ref[member, plane] = value
            pops.append(value)
        density, speeds = moments_of(pops)
        density_ref[plane] = density
        for axis_no in range(3):
            at = axis_no * 32 + plane * 8
            field_ref[at : at + 8, :] = speeds[axis_no]

    outside = ((row < PLANES) & (first_wall == 0)) | ((row >= PLANES) & (last_wall > 0))
    outer = []
    for member in range(19):
        if member in falling:
            low = four(down_ref, AT_NEXT + falling.index(member) * PLANES)
        else:
            low = four(below_ref, AT_POPS + (level + rising).index(member) * PLANES)
        if member in rising:
            top = four(up_ref, AT_NEXT + rising.index(member) * PLANES)
        else:
            top = four(above_ref, AT_POPS + (level + falling).index(member) * PLANES)
        value = jnp.concatenate([low, top], 0)
        outer.append(jnp.where(outside, 0.0 if member else 1.0, value))
    outer_density, outer_speeds = moments_of(outer)
    lows, tops = [], []
    for axis_no in range(3):
        at = AT_SPEED + axis_no * PLANES
        second = jnp.concatenate([four(above_ref, at), four(below_ref, at)], 0)
        lows.append(jnp.where(row < PLANES, outer_speeds[axis_no], second))
        tops.append(jnp.where(row < PLANES, second, outer_speeds[axis_no]))

    def beyond(ref, field, base_y):
        pairs = pairs_of(jnp.concatenate(field, 0))
        total = jnp.zeros((24, LANES), f32)
        for block in range(tiles // 2):
            tile = AT_MARKS + 16 * block
            mark = jnp.concatenate([ref[tile : tile + 8, :], ref[tile + 8 : tile + 16, :]], 1)
            at = AT_Z + 2 * block
            base = jnp.concatenate([ref[at : at + 1, :], ref[at + 1 : at + 2, :]], 1)
            spot = spots(base)
            found = gathered(pairs, spot)
            place = iota((ROWS, 2 * LANES), 0)
            frac = mark[3:4, :]
            weight = along_x(mark, (place % PLANES).astype(f32))
            weight = weight * jnp.where(place < PLANES, frac, 1.0 - frac)
            weight = jnp.where(mark[1:2, :] == base_y, weight, 0.0)
            frac = mark[4:5, :]
            spreads = []
            for axis_no in range(3):
                here = found[axis_no * 8 : axis_no * 8 + 8]
                there = found[24 + axis_no * 8 : 32 + axis_no * 8]
                value = weight * (here + frac * (there - here))
                force = mark[5 + axis_no : 6 + axis_no, :] - jnp.sum(value, 0, keepdims=True)
                spreads.append(weight * force)
            spreads = jnp.concatenate(spreads, 0)
            ahead = spreads * frac
            total = total + scattered(spreads - ahead, ahead, spot)
        return total

    from_below = beyond(below_ref, lows, float(ROWS - 2))
    from_above = beyond(above_ref, tops, 0.0)
    outer_pulls = [
        jnp.where(row < PLANES, from_below[a * 8 : a * 8 + 8], from_above[a * 8 : a * 8 + 8])
        for a in range(3)
    ]
    relax = relax_of(outer, outer_density, outer_speeds)
    outer_post = relaxed(outer, outer_density, outer_speeds, relax, outer_pulls)
    for number in range(5):
        outer_ref[number] = jnp.where(
            row < PLANES, outer_post[rising[number]], outer_post[falling[number]]
        )

    pairs = pairs_of(field_ref[...])
    total = jnp.zeros((96, LANES), f32)
    kept = [jnp.zeros((ROWS, LANES), f32) for axis_no in range(3)]
    for block in range(tiles // 2):
        tile = AT_MARKS + 16 * block
        mark = jnp.concatenate([up_ref[tile : tile + 8, :], up_ref[tile + 8 : tile + 16, :]], 1)
        at = AT_Z + 2 * block
        spot = spots(jnp.concatenate([up_ref[at : at + 1, :], up_ref[at + 1 : at + 2, :]], 1))
        found = gathered(pairs, spot)
        forces, spreads = forces_of(
            mark,
            block_weights(mark),
            [found[at * 8 : at * 8 + 8] for at in range(12)],
            [found[96 + at * 8 : 104 + at * 8] for at in range(12)],
        )
        spreads = jnp.concatenate(spreads, 0)
        ahead = spreads * mark[4:5, :]
        total = total + scattered(spreads - ahead, ahead, spot)
        for half in range(2):
            lanes = slice(half * LANES, (half + 1) * LANES)
            for axis_no in range(3):
                kept[axis_no] = jnp.where(
                    row == 2 * block + half, forces[axis_no][:, lanes], kept[axis_no]
                )
    back_ref[...] = jnp.zeros(back_ref.shape, f32)
    following = [roll(value, -1, 0) for value in kept]
    for part in range(sources // 2):
        tile, first = divmod(part * SLOTS, LANES)
        value = None
        for axis_no in range(3):
            moved = jnp.where(lane >= first, kept[axis_no], following[axis_no])
            moved = roll(moved, SHARE * axis_no - first, 1)
            value = moved if axis_no == 0 else jnp.where(lane // SHARE >= axis_no, moved, value)
        for source, at in ((part, tile), (part + sources // 2, tile + tiles // 2)):
            back_ref[source, 0:1, :] = value[at : at + 1, :]
    for plane in range(PLANES):
        ats = [a * 32 + plane * 8 for a in range(3)]
        pops = [wide_ref[member, plane] for member in range(19)]
        speeds = [field_ref[at : at + 8, :] for at in ats]
        density = density_ref[plane]
        relax = relax_of(pops, density, speeds)
        results = relaxed(pops, density, speeds, relax, [total[at : at + 8, :] for at in ats])
        for member in range(19):
            post_ref[member, plane] = results[member]

    to_right, to_left = jnp.zeros((ROWS, LANES), f32), jnp.zeros((ROWS, LANES), f32)
    for plane in range(PLANES):
        for member in range(19):
            shift_x, shift_y, shift_z = velocity_table[member]
            source = (plane - shift_x) % PLANES
            value = post_ref[member, source]
            if shift_y == 1:
                edge = outer_ref[rising.index(member), source : source + 1, :]
                value = jnp.where(row == 0, edge, roll(value, 1, 0))
            if shift_y == -1:
                at = PLANES + source
                edge = outer_ref[falling.index(member), at : at + 1, :]
                value = jnp.where(row == ROWS - 1, edge, roll(value, -1, 0))
            if shift_z:
                value = roll(value, shift_z, 1)
            if shift_z == 1:
                place = ahead_z.index(member) * PLANES + plane
                to_right = jnp.where(lane == place, roll(value, place, 1), to_right)
            if shift_z == -1:
                place = back_z.index(member) * PLANES + plane
                to_left = jnp.where(lane == place, roll(value, place + 1, 1), to_left)
            if shift_y == 1:
                value = jnp.where(row == first_wall, post_ref[opposite[member], plane], value)
            if shift_y == -1:
                value = jnp.where(row == last_wall, post_ref[opposite[member], plane], value)
            moved_ref[member, plane] = value
    for target, face in ((left, to_left), (right, to_right)):
        early, late = jnp.zeros((ROWS, LANES), f32), jnp.zeros((ROWS, LANES), f32)
        for number in range(ROWS):
            early = jnp.where(row == number, roll(face, EARLY * number, 1), early)
            late = jnp.where(row == number, roll(face, LATE_FACE - EARLY + 4 * number, 1), late)
        early = jnp.where(lane // EARLY == row, early, 0.0)
        late = jnp.where((lane - LATE_FACE) // 4 == row, late, 0.0)
        late = jnp.where(lane >= LATE_FACE, late, 0.0)
        mine = jnp.where(iota((1, LANES), 1) < LATE_FACE, back_ref[target, 0:1, :], 0.0)
        back_ref[target, 0:1, :] = mine + jnp.sum(late, 0, keepdims=True)
        back_ref[target, 1:2, :] = jnp.sum(early, 0, keepdims=True)


def last_kernel(
    moved_ref, got_ref, owner_ref, rank_ref, pops_ref, force_ref
):
    left, right = z_neighbours()
    _, _, first_wall, last_wall = y_ends()
    lane = iota((ROWS, LANES), 1)
    row = iota((ROWS, LANES), 0)

    def face_of(source):
        late = jnp.broadcast_to(got_ref[source, 0:1, :], (ROWS, LANES))
        early = jnp.broadcast_to(got_ref[source, 1:2, :], (ROWS, LANES))
        face = jnp.zeros((ROWS, LANES), f32)
        for number in range(ROWS):
            value = roll(late, EARLY - LATE_FACE - 4 * number, 1)
            value = jnp.where(lane < EARLY, roll(early, -EARLY * number, 1), value)
            face = jnp.where(row == number, value, face)
        return face

    from_left, from_right = face_of(left), face_of(right)
    changed = [i for i in range(19) if velocity_table[i][2]]
    for member in range(19):
        if member not in changed:
            pops_ref[member] = moved_ref[member]
    for number, member in enumerate(changed):
        _, shift_y, shift_z = velocity_table[member]
        for plane in range(PLANES):
            if shift_z == 1:
                place = ahead_z.index(member) * PLANES + plane
                edge, here = roll(from_left, -place, 1), lane == 0
            else:
                place = back_z.index(member) * PLANES + plane
                edge, here = roll(from_right, LANES - 1 - place, 1), lane == LANES - 1
            if shift_y == 1:
                here = here & (row != first_wall)
            if shift_y == -1:
                here = here & (row != last_wall)
            pops_ref[member, plane] = jnp.where(here, edge, moved_ref[member, plane])
    owners, markers = got_ref.shape[0], owner_ref.shape[1]
    owner = owner_ref[...]
    spot = (iota((LANES, markers), 0).astype(f32) == rank_ref[...]).astype(bf16)
    rows = got_ref[:, 0, :]
    high, low = split_two(
        jnp.concatenate([roll(rows, -SHARE * axis_no, 1) for axis_no in range(3)], 0)
    )
    found = jnp.dot(
        jnp.concatenate([high, low], 1),
        jnp.concatenate([spot, spot], 0),
        preferred_element_type=f32,
    )
    hit = iota((owners, markers), 0) == owner
    for axis_no in range(3):
        value = jnp.where(hit, found[axis_no * owners : (axis_no + 1) * owners], 0.0)
        force_ref[axis_no : axis_no + 1, :] = jnp.sum(value, 0, keepdims=True) / ref_speed


def body(populations, marker_owner, marker_cell, marker_frac, marker_speed, marker_count):
    count_gy, count_gz = lax.axis_size("gy"), lax.axis_size("gz")
    markers = marker_owner.shape[0]
    vmem = pl.BlockSpec(memory_space=pltpu.VMEM)
    shape = jax.ShapeDtypeStruct
    tiles = shape((count_gz, 8, LANES), f32)
    field = shape((96, LANES), f32)
    cells = shape((PLANES, ROWS, LANES), f32)
    lattice = shape(populations.shape, f32)
    inputs = [
        marker_owner.reshape(1, markers),
        marker_cell,
        marker_frac,
        marker_speed,
        populations,
    ]
    send, rank, live, speeds, density, relax = call(
        first_kernel,
        [tiles, shape((1, markers), f32), shape((1, markers), jnp.int32), field, cells, cells],
        [marker_count.reshape(1, 1)]
        + [pltpu.with_memory_space_constraint(value, pltpu.HBM) for value in inputs],
        [vmem] + [pl.BlockSpec(memory_space=pltpu.HBM)] * 5,
        scratch=[pltpu.VMEM(value.shape, value.dtype) for value in inputs]
        + [pltpu.SemaphoreType.DMA((5,))],
    )
    got = lax.all_to_all(send, "gz", split_axis=0, concat_axis=0, tiled=True)
    face = shape((FACE_ROWS, LANES), f32)
    next_pops, up, down = call(
        second_kernel,
        [lattice, face, face],
        [populations, got, speeds, density, relax],
        [vmem] * 5,
        scratch=[
            pltpu.VMEM(populations.shape, f32),
            pltpu.VMEM((24, ROWS, LANES), f32),
            pltpu.VMEM((24, ROWS, LANES), f32),
            pltpu.VMEM((96, LANES), f32),
        ],
    )
    below = lax.ppermute(up, "gy", [(i, i + 1) for i in range(count_gy - 1)])
    above = lax.ppermute(down, "gy", [(i + 1, i) for i in range(count_gy - 1)])
    moved, back = call(
        third_kernel,
        [lattice, shape((count_gz, 2, LANES), f32)],
        [next_pops, up, down, below, above],
        [vmem] * 5,
        scratch=[
            pltpu.VMEM(populations.shape, f32),
            pltpu.VMEM((96, LANES), f32),
            pltpu.VMEM((PLANES, ROWS, LANES), f32),
            pltpu.VMEM(populations.shape, f32),
            pltpu.VMEM((5, ROWS, LANES), f32),
        ],
    )
    back = lax.all_to_all(back, "gz", split_axis=0, concat_axis=0, tiled=True)
    pops, force = call(
        last_kernel,
        [lattice, shape((3, markers), f32)],
        [moved, back, live, rank],
        [vmem] * 4,
    )
    return pops, force


def solution(mesh):
    return jax.shard_map(
        body,
        mesh=mesh,
        in_specs=(
            P(None, None, "gy", "gz"),
            P(("gy", "gz"), None),
            P(None, ("gy", "gz")),
            P(None, ("gy", "gz")),
            P(None, ("gy", "gz")),
            P(("gy", "gz")),
        ),
        out_specs=(P(None, None, "gy", "gz"), P(None, ("gy", "gz"))),
        check_vma=False,
    )
```

```python
import math

import jax
import jax.numpy as jnp
from jax import lax
from jax.experimental import pallas as pl
from jax.experimental.pallas import tpu as pltpu
from jax.sharding import PartitionSpec as P

INTERPRET = False

velocity_table = (
    (0, 0, 0),
    (1, 0, 0),
    (-1, 0, 0),
    (0, 1, 0),
    (0, -1, 0),
    (0, 0, 1),
    (0, 0, -1),
    (1, 1, 0),
    (-1, -1, 0),
    (1, -1, 0),
    (-1, 1, 0),
    (1, 0, 1),
    (-1, 0, -1),
    (1, 0, -1),
    (-1, 0, 1),
    (0, 1, 1),
    (0, -1, -1),
    (0, 1, -1),
    (0, -1, 1),
)
opposite = (0, 2, 1, 4, 3, 6, 5, 8, 7, 10, 9, 12, 11, 14, 13, 16, 15, 18, 17)
rising = tuple(i for i in range(19) if velocity_table[i][1] == 1)
falling = tuple(opposite[i] for i in rising)
level = tuple(i for i in range(19) if velocity_table[i][1] == 0)
ahead_z = tuple(i for i in range(19) if velocity_table[i][2] == 1)
back_z = tuple(opposite[i] for i in ahead_z)
tau_base = 0.52
smag_const = 0.17
ref_speed = 0.05

PLANES = 4
ROWS = 8
LANES = 128
SLOTS = 24
SHARE = 32
FEW = 4
SPARE = SLOTS - FEW
FIRST_SPARE = SHARE
FIRST_Z = SHARE + 2 * SPARE
FIRST_RIM = 76
LATE_FACE = 3 * SHARE
EARLY = 16
RIM_WORDS = 13
AT_SPEED, AT_SUMS, AT_POPS, AT_NEXT, AT_MARKS, FACE_ROWS = 0, 12, 36, 56, 80, 128
AT_Z, MARK_ROWS = 48, 56

f32 = jnp.float32
bf16 = jnp.bfloat16


def iota(shape, dim):
    return lax.broadcasted_iota(jnp.int32, shape, dim)


def roll(value, shift, axis):
    shift = shift % value.shape[axis]
    return pltpu.roll(value, shift, axis) if shift else value


def split_two(value):
    high = value.astype(bf16)
    return high, (value - high.astype(f32)).astype(bf16)


def call(kernel, out_shape, args, in_specs, scratch=(), out_specs=None, aliases=()):
    vmem = pl.BlockSpec(memory_space=pltpu.VMEM)
    return pl.pallas_call(
        kernel,
        out_shape=out_shape,
        in_specs=in_specs,
        out_specs=out_specs or [vmem] * len(out_shape),
        input_output_aliases=dict(aliases),
        scratch_shapes=list(scratch),
        compiler_params=pltpu.CompilerParams(vmem_limit_bytes=32 * 1024 * 1024),
        interpret=INTERPRET,
    )(*args)


def z_neighbours():
    column, size = lax.axis_index("gz"), lax.axis_size("gz")
    return (column + size - 1) % size, (column + 1) % size


def y_ends():
    place, size = lax.axis_index("gy"), lax.axis_size("gy")
    first, last = place == 0, place == size - 1
    return (
        jnp.where(first, -1, 0),
        jnp.where(last, -1, ROWS - 1),
        jnp.where(first, 0, -1),
        jnp.where(last, ROWS - 1, -1),
    )


def moments_of(pops):
    density = pops[0]
    for member in range(1, 19):
        density = density + pops[member]
    parts = []
    for axis_no in range(3):
        total = None
        for member in range(19):
            if velocity_table[member][axis_no] == 1:
                total = pops[member] if total is None else total + pops[member]
        for member in range(19):
            if velocity_table[member][axis_no] == -1:
                total = total - pops[member]
        parts.append(total)
    inverse = 1.0 / density
    return density, [part * inverse for part in parts]


def relax_of(pops, density, speeds):
    factor = 18.0 * math.sqrt(2.0) * smag_const * smag_const
    moved = [density * part for part in speeds]
    pair = [pops[2 * k + 1] + pops[2 * k + 2] for k in range(9)]
    third = density * (1.0 / 3.0)
    xx = pair[0] + pair[3] + pair[4] + pair[5] + pair[6] - third - moved[0] * speeds[0]
    yy = pair[1] + pair[3] + pair[4] + pair[7] + pair[8] - third - moved[1] * speeds[1]
    zz = pair[2] + pair[5] + pair[6] + pair[7] + pair[8] - third - moved[2] * speeds[2]
    xy = pair[3] - pair[4] - moved[0] * speeds[1]
    xz = pair[5] - pair[6] - moved[0] * speeds[2]
    yz = pair[7] - pair[8] - moved[1] * speeds[2]
    norm_sq = xx * xx + yy * yy + zz * zz + 2.0 * (xy * xy + xz * xz + yz * yz)
    return 0.5 * (tau_base + jnp.sqrt(tau_base * tau_base + factor * jnp.sqrt(norm_sq) / density))


def along_of(member, speeds):
    total = None
    for axis_no in range(3):
        if velocity_table[member][axis_no] == 1:
            total = speeds[axis_no] if total is None else total + speeds[axis_no]
    for axis_no in range(3):
        if velocity_table[member][axis_no] == -1:
            total = total - speeds[axis_no]
    return total


def relaxed(pops, density, speeds, relax, pulls):
    pull = relax / density
    shifted = [speeds[a] + pull * pulls[a] for a in range(3)]
    shifted_sq = shifted[0] * shifted[0] + shifted[1] * shifted[1] + shifted[2] * shifted[2]
    rate = 1.0 / relax
    keep = 1.0 - rate
    scale = rate * density
    base = scale * (1.0 - 1.5 * shifted_sq)
    quad = 4.5 * scale
    results = [keep * pops[0] + base * (1.0 / 3.0)]
    for pair in range(9):
        plus = 2 * pair + 1
        along = along_of(plus, shifted)
        weight = 1.0 / 18.0 if pair < 3 else 1.0 / 36.0
        even = weight * (base + quad * along * along)
        odd = (3.0 * weight) * (scale * along)
        results.append(keep * pops[plus] + (even + odd))
        results.append(keep * pops[plus + 1] + (even - odd))
    return results


def along_x(mark, plane):
    base, frac = mark[0:1, :], mark[2:3, :]
    following = jnp.where(base == float(PLANES), 0.0, base)
    weight = jnp.where(base - 1.0 == plane, 1.0 - frac, 0.0)
    return jnp.where((base > 0.5) & (following == plane), frac, weight)


def block_weights(mark):
    base, frac = mark[1:2, :], mark[3:4, :]
    row = iota((ROWS, mark.shape[1]), 0).astype(f32)
    along_y = jnp.where(row == base, 1.0 - frac, jnp.where(row == base + 1.0, frac, 0.0))
    return [along_y * along_x(mark, float(plane)) for plane in range(PLANES)]


def spots(base_z):
    count = base_z.shape[1]
    one, none = jnp.ones((), bf16), jnp.zeros((), bf16)
    return jnp.where(iota((LANES, count), 0).astype(bf16) == base_z.astype(bf16), one, none)


def pairs_of(field):
    high, low = split_two(field)
    next_high, next_low = split_two(roll(field, -1, 1))
    return jnp.concatenate(
        [jnp.concatenate([high, low], 1), jnp.concatenate([next_high, next_low], 1)], 0
    )


def gathered(pairs, spot):
    return jnp.dot(pairs, jnp.concatenate([spot, spot], 0), preferred_element_type=f32)


def sums_of(here, there, spot):
    size = here.shape[0]
    high, low = split_two(here)
    next_high, next_low = split_two(there)
    sums = lax.dot_general(
        jnp.concatenate([high, low, next_high, next_low], 0),
        spot,
        (((1,), (1,)), ((), ())),
        preferred_element_type=f32,
    )
    first = sums[0:size] + sums[size : 2 * size]
    second = sums[2 * size : 3 * size] + sums[3 * size :]
    return first, second


def scattered(here, there, spot):
    first, second = sums_of(here, there, spot)
    return first + roll(second, 1, 1)


def forces_of(mark, weights, here, there):
    frac = mark[4:5, :]
    forces, spreads = [], []
    for axis_no in range(3):
        total = None
        for plane in range(PLANES):
            at = axis_no * PLANES + plane
            value = weights[plane] * (here[at] + frac * (there[at] - here[at]))
            total = value if total is None else total + value
        force = mark[5 + axis_no : 6 + axis_no, :] - jnp.sum(total, 0, keepdims=True)
        forces.append(force)
        for plane in range(PLANES):
            spreads.append(weights[plane] * force)
    return forces, spreads


def first_kernel(
    count_ref, owner_hbm, cell_hbm, frac_hbm, speed_hbm, pops_hbm,
    send_ref, rank_ref, live_ref, field_ref, density_ref, relax_ref,
    owner_ref, cell_ref, frac_ref, speed_ref, pops_ref, sems,
):
    copies = [
        pltpu.make_async_copy(source, target, sems.at[number])
        for number, (source, target) in enumerate(
            [
                (owner_hbm, owner_ref),
                (cell_hbm, cell_ref),
                (frac_hbm, frac_ref),
                (speed_hbm, speed_ref),
                (pops_hbm, pops_ref),
            ]
        )
    ]
    for copy in copies:
        copy.start()
    for copy in copies[0:4]:
        copy.wait()
    owners, markers = send_ref.shape[0], owner_ref.shape[1]
    live = iota((1, markers), 1) < count_ref[...]
    owner = jnp.where(live, owner_ref[...], -1)
    live_ref[...] = owner
    base_z = cell_ref[2:3, :]
    upper, lower = base_z == LANES - 2, base_z == 0
    twin = jnp.where(
        upper,
        jnp.where(owner == owners - 1, 0, owner + 1),
        jnp.where(owner == 0, owners - 1, owner - 1),
    )
    twin = jnp.where(live & (upper | lower), twin, -1)
    hit = iota((owners, markers), 0) == owner
    hits = jnp.concatenate(
        [hit.astype(f32), (hit & upper).astype(f32), (hit & lower).astype(f32)], 0
    )
    blocks = markers // LANES
    parts = [hits[:, block * LANES : (block + 1) * LANES] for block in range(blocks)]
    earlier = iota((LANES, 2 * LANES), 0) < iota((LANES, 2 * LANES), 1)
    counts = jnp.dot(
        jnp.concatenate(parts, 0).astype(bf16), earlier.astype(bf16), preferred_element_type=f32
    )
    before = None
    ranks = [[], [], []]
    for block in range(blocks):
        inner = counts[block * 3 * owners : (block + 1) * 3 * owners]
        place = inner[:, 0:LANES] if before is None else inner[:, 0:LANES] + before
        before = inner[:, LANES:] if before is None else inner[:, LANES:] + before
        picked = parts[block] * place
        for kind in range(3):
            ranks[kind].append(
                jnp.sum(picked[kind * owners : (kind + 1) * owners], 0, keepdims=True)
            )
    rank, rank_up, rank_low = [jnp.concatenate(kind, 1) for kind in ranks]
    rank_ref[...] = rank
    copies[4].wait()
    lane_up = jnp.where(rank_up < FEW, SLOTS + rank_up, FIRST_SPARE - FEW + rank_up)
    lane_low = jnp.where(
        rank_low < FEW, SLOTS + FEW + rank_low, FIRST_SPARE + SPARE - FEW + rank_low
    )
    lane_twin = jnp.where(upper, lane_up, lane_low)
    lane_z = FIRST_Z + jnp.where(rank >= 16.0, 2.0, jnp.where(rank >= 8.0, 1.0, 0.0))
    slot_z = rank - 8.0 * (lane_z - FIRST_Z)
    lane = iota((LANES, markers), 0).astype(f32)
    spot_own = (lane == rank).astype(bf16)
    spot_twin = (lane == lane_twin).astype(bf16)
    spot_z = (lane == lane_z).astype(bf16)
    row = iota((8, markers), 0)
    words = jnp.where(row == 0, cell_ref[0:1, :] + 1, cell_ref[1:2, :]).astype(f32)
    for number in range(3):
        words = jnp.where(row == 2 + number, frac_ref[number : number + 1, :], words)
        words = jnp.where(row == 5 + number, speed_ref[number : number + 1, :], words)
    high, low = split_two(words)
    high, low = high.astype(f32), low.astype(f32)
    words_z = jnp.where(row.astype(f32) == slot_z, base_z.astype(f32), 0.0)

    def to_owners(value, target):
        value = jnp.concatenate([value, value], 0).astype(bf16)
        target = jnp.broadcast_to(target.astype(f32), (16, markers)).astype(bf16)
        first = jnp.where(iota((16, markers), 0) < 8, 0.0, 1.0).astype(bf16)
        rows = []
        for number in range(0, owners, 2):
            rows.append(jnp.where(target == first + float(number), value, jnp.zeros((), bf16)))
        return jnp.concatenate(rows, 0)

    def placed(left, spot):
        return lax.dot_general(left, spot, (((1,), (1,)), ((), ())), preferred_element_type=f32)

    tiles = placed(to_owners(high, owner), spot_own) + placed(to_owners(low, owner), spot_own)
    tiles = tiles + placed(to_owners(high, twin), spot_twin)
    tiles = tiles + placed(to_owners(low, twin), spot_twin)
    tiles = tiles + placed(to_owners(words_z, owner), spot_z)
    send_ref[...] = tiles.reshape(owners, 8, LANES)


    lane = iota((ROWS, LANES), 1)
    to_right, to_left = jnp.zeros((ROWS, LANES), f32), jnp.zeros((ROWS, LANES), f32)
    for plane in range(PLANES):
        pops = [pops_ref[member, plane] for member in range(19)]
        density, speeds = moments_of(pops)
        relax = relax_of(pops, density, speeds)
        density_ref[plane] = density
        relax_ref[plane] = relax
        for axis_no in range(3):
            at = axis_no * 32 + plane * 8
            field_ref[at : at + 8, :] = speeds[axis_no]
        common = [density, *speeds, relax]
        for word in range(RIM_WORDS):
            place = FIRST_RIM + word * PLANES + plane
            if word < 5:
                right, left, shift = common[word], common[word], 0
            elif word < 10:
                right, left, shift = pops[ahead_z[word - 5]], pops[back_z[word - 5]], 0
            else:
                right, left, shift = speeds[word - 10], speeds[word - 10], 1
            here = lane == place
            to_right = jnp.where(here, roll(right, place - (LANES - 1) + shift, 1), to_right)
            to_left = jnp.where(here, roll(left, place - shift, 1), to_left)
    left, right = z_neighbours()
    send_ref[left] = send_ref[left] + to_left
    send_ref[right] = send_ref[right] + to_right


def second_kernel(
    pops_ref, got_ref, field_ref, density_ref, relax_ref,
    next_ref, up_ref, down_ref, marks_ref,
    post_ref, near_ref, far_ref, twin_ref,
):
    left, right = z_neighbours()
    lane = iota((ROWS, LANES), 1)
    row = iota((ROWS, LANES), 0)
    sources = got_ref.shape[0]

    tiles = sources * SLOTS // LANES
    marks = [None] * tiles
    twin_marks = [None] * (sources * 2 * FEW // LANES)
    for source in range(sources):
        tile, first = divmod(source * SLOTS, LANES)
        words = roll(got_ref[source], first, 1)
        marks[tile] = words if marks[tile] is None else jnp.where(lane >= first, words, marks[tile])
        if first + SLOTS > LANES:
            marks[tile + 1] = words
        tile, first = divmod(source * 2 * FEW, LANES)
        words = roll(got_ref[source], first - SLOTS, 1)
        old = twin_marks[tile]
        twin_marks[tile] = words if old is None else jnp.where(lane >= first, words, old)
    bases = []
    for tile in range(tiles):
        first, last = tile * LANES // SLOTS, ((tile + 1) * LANES - 1) // SLOTS
        rows = jnp.concatenate([got_ref[source] for source in range(first, last + 1)], 0)

        def slot_of(shape):
            member = iota(shape, 1) + tile * LANES
            source = (member * 2731) >> 16
            return source, member - SLOTS * source

        _, slot = slot_of((LANES, LANES))
        chosen = (iota((LANES, LANES), 0) == FIRST_Z + (slot >> 3)).astype(bf16)
        value = jnp.dot(rows.astype(bf16), chosen, preferred_element_type=f32)
        source, slot = slot_of(value.shape)
        here = iota(value.shape, 0) == (source - first) * 8 + (slot & 7)
        bases.append(jnp.sum(jnp.where(here, value, 0.0), 0, keepdims=True))
    for tile in range(tiles):
        marks_ref[tile * 8 : tile * 8 + 8, :] = marks[tile]
        marks_ref[AT_Z + tile : AT_Z + tile + 1, :] = bases[tile]
        for ref, base_y in ((up_ref, float(ROWS - 2)), (down_ref, 0.0)):
            words = jnp.where((row == 0) & (marks[tile][1:2, :] != base_y), 0.0, marks[tile])
            words = jnp.where(row == 1, bases[tile], words)
            ref[AT_MARKS + tile * 8 : AT_MARKS + tile * 8 + 8, :] = words
    for ref in (up_ref, down_ref):
        ref[AT_NEXT + 20 : AT_MARKS, :] = jnp.zeros((AT_MARKS - AT_NEXT - 20, LANES), f32)

    ends = jnp.where(lane >= FIRST_RIM, got_ref[left], roll(got_ref[right], 64, 1))
    rim = [roll(ends, -(FIRST_RIM + PLANES * word), 1) for word in range(RIM_WORDS)]

    def spread_lane(value, at):
        return jnp.broadcast_to(value[:, at : at + 1], (ROWS, LANES))

    for axis_no in range(3):
        for plane in range(PLANES):
            at = axis_no * PLANES + plane
            near_ref[at] = spread_lane(rim[10 + axis_no], plane)
            near_ref[12 + at] = spread_lane(rim[1 + axis_no], 64 + plane)
            far_ref[at] = spread_lane(rim[1 + axis_no], plane)
            far_ref[12 + at] = spread_lane(rim[10 + axis_no], 64 + plane)

    def twins(of_left, of_right):
        def both(ref):
            return [
                jnp.where(of_left, ref[at], jnp.where(of_right, ref[12 + at], 0.0))
                for at in range(12)
            ]

        return both(near_ref), both(far_ref)

    def sides(lefts, rights, count):
        place, member = iota((LANES, count), 0), iota((LANES, count), 1)
        chosen = jnp.where(place < 64, lefts(member).astype(f32), rights(member).astype(f32))
        return chosen.astype(bf16)

    near, far = twins(lane % (2 * FEW) < FEW, lane % (2 * FEW) >= FEW)
    side = sides(
        lambda member: member % (2 * FEW) < FEW,
        lambda member: member % (2 * FEW) >= FEW,
        2 * LANES,
    )
    rim_left = iota((96, LANES), 1) < 64
    pairs = pairs_of(field_ref[...])
    force = jnp.zeros((96, LANES), f32)
    for block in range(tiles // 2):
        mark = jnp.concatenate(marks[2 * block : 2 * block + 2], 1)
        spot = spots(jnp.concatenate(bases[2 * block : 2 * block + 2], 1))
        found = gathered(pairs, spot)
        _, spreads = forces_of(
            mark,
            block_weights(mark),
            [found[at * 8 : at * 8 + 8] for at in range(12)],
            [found[96 + at * 8 : 104 + at * 8] for at in range(12)],
        )
        spreads = jnp.concatenate(spreads, 0)
        ahead = spreads * mark[4:5, :]
        force = force + scattered(spreads - ahead, ahead, spot)
    mark = jnp.concatenate(twin_marks, 1)
    _, spreads = forces_of(
        mark,
        block_weights(mark),
        [jnp.concatenate([value] * 2, 1) for value in near],
        [jnp.concatenate([value] * 2, 1) for value in far],
    )
    spreads = jnp.concatenate(spreads, 0)
    ahead = spreads * mark[4:5, :]
    first, second = sums_of(spreads - ahead, ahead, side)
    twin_ref[...] = jnp.where(rim_left, second, first)

    further = jnp.where((lane >= FIRST_SPARE) & (lane < FIRST_Z), 1.0, 0.0)
    most = got_ref[0]
    for source in range(1, sources):
        most = jnp.maximum(most, got_ref[source])

    @pl.when(jnp.max(most * further) > 0.5)
    def _():
        near, far = twins(lane < SPARE, lane >= SPARE)
        side = sides(lambda member: member < SPARE, lambda member: member >= SPARE, LANES)

        def one(source, carry):
            mark = roll(got_ref[source], -FIRST_SPARE, 1)
            mark = jnp.where(lane < 2 * SPARE, mark, 0.0)
            _, spreads = forces_of(mark, block_weights(mark), near, far)
            spreads = jnp.concatenate(spreads, 0)
            ahead = spreads * mark[4:5, :]
            first, second = sums_of(spreads - ahead, ahead, side)
            twin_ref[...] = twin_ref[...] + jnp.where(rim_left, second, first)
            return carry

        lax.fori_loop(0, sources, one, 0)

    sums = twin_ref[...]
    pulls = []
    for axis_no in range(3):
        total = None
        for plane in range(PLANES):
            at = axis_no * 32 + plane * 8
            value = sums[at : at + 8, :]
            total = value if total is None else jnp.where(lane % PLANES == plane, value, total)
        pulls.append(total)
    density, speeds, relax = rim[0], rim[1:4], rim[4]
    pull = relax / density
    shifted = [speeds[a] + pull * pulls[a] for a in range(3)]
    shifted_sq = shifted[0] * shifted[0] + shifted[1] * shifted[1] + shifted[2] * shifted[2]
    rate = 1.0 / relax
    sign = jnp.where(lane < 64, 1.0, -1.0)
    rim_post = []
    for number, member in enumerate(ahead_z):
        along = sign * along_of(member, shifted)
        weight = 1.0 / 18.0 if number == 0 else 1.0 / 36.0
        target = weight * density * (1.0 + 3.0 * along + 4.5 * along * along - 1.5 * shifted_sq)
        rim_post.append((1.0 - rate) * rim[5 + number] + rate * target)

    for plane in range(PLANES):
        ats = [a * 32 + plane * 8 for a in range(3)]
        results = relaxed(
            [pops_ref[member, plane] for member in range(19)],
            density_ref[plane],
            [field_ref[at : at + 8, :] for at in ats],
            relax_ref[plane],
            [force[at : at + 8, :] for at in ats],
        )
        for member in range(19):
            post_ref[member, plane] = results[member]

    for plane in range(PLANES):
        pops = []
        for member in range(19):
            shift_x, shift_y, shift_z = velocity_table[member]
            source = (plane - shift_x) % PLANES
            value = post_ref[member, source]
            if shift_z == 1:
                edge = roll(rim_post[ahead_z.index(member)], -source, 1)
                value = jnp.where(lane == 0, edge, roll(value, 1, 1))
            if shift_z == -1:
                edge = roll(rim_post[back_z.index(member)], 63 - source, 1)
                value = jnp.where(lane == LANES - 1, edge, roll(value, -1, 1))
            if shift_y == 1:
                at = AT_NEXT + rising.index(member) * PLANES + plane
                up_ref[at : at + 1, :] = value[ROWS - 1 : ROWS, :]
                value = jnp.where(row == 0, post_ref[opposite[member], plane], roll(value, 1, 0))
            if shift_y == -1:
                at = AT_NEXT + falling.index(member) * PLANES + plane
                down_ref[at : at + 1, :] = value[0:1, :]
                value = jnp.where(
                    row == ROWS - 1, post_ref[opposite[member], plane], roll(value, -1, 0)
                )
            next_ref[member, plane] = value
            pops.append(value)
        _, speeds = moments_of(pops)
        for axis_no in range(3):
            at = AT_SPEED + axis_no * PLANES + plane
            up_ref[at : at + 1, :] = speeds[axis_no][ROWS - 2 : ROWS - 1, :]
            down_ref[at : at + 1, :] = speeds[axis_no][1:2, :]
        cross = pops[11] + pops[12]
        other = pops[13] + pops[14]
        across, along = pops[1] + pops[2], pops[5] + pops[6]
        lean = pops[11] - pops[12]
        tilt = pops[13] - pops[14]
        sums = [
            pops[0] + across + along + cross + other,
            pops[1] - pops[2] + lean + tilt,
            pops[5] - pops[6] + lean - tilt,
            across + cross + other,
            along + cross + other,
            cross - other,
        ]
        for number, value in enumerate(sums):
            at = AT_SUMS + number * PLANES + plane
            up_ref[at : at + 1, :] = value[ROWS - 1 : ROWS, :]
            down_ref[at : at + 1, :] = value[0:1, :]
        for number in range(5):
            at = AT_POPS + number * PLANES + plane
            up_ref[at : at + 1, :] = pops[rising[number]][ROWS - 1 : ROWS, :]
            down_ref[at : at + 1, :] = pops[falling[number]][0:1, :]


def third_kernel(
    next_ref, up_ref, down_ref, marks_ref, below_ref, above_ref,
    moved_ref, back_ref,
    wide_ref, field_ref, density_ref, post_ref, outer_ref,
):
    left, right = z_neighbours()
    first_open, last_open, first_wall, last_wall = y_ends()
    lane = iota((ROWS, LANES), 1)
    row = iota((ROWS, LANES), 0)
    sources = back_ref.shape[0]
    tiles = sources * SLOTS // LANES

    def four(ref, at):
        return ref[at : at + PLANES, :]

    for plane in range(PLANES):
        pops = []
        for member in range(19):
            value = next_ref[member, plane]
            if member in rising:
                at = AT_NEXT + rising.index(member) * PLANES + plane
                value = jnp.where(row == first_open, below_ref[at : at + 1, :], value)
            if member in falling:
                at = AT_NEXT + falling.index(member) * PLANES + plane
                value = jnp.where(row == last_open, above_ref[at : at + 1, :], value)
            wide_ref[member, plane] = value
            pops.append(value)
        density, speeds = moments_of(pops)
        density_ref[plane] = density
        for axis_no in range(3):
            at = axis_no * 32 + plane * 8
            field_ref[at : at + 8, :] = speeds[axis_no]

    outside = ((row < PLANES) & (first_wall == 0)) | ((row >= PLANES) & (last_wall > 0))
    sums = []
    for number in range(6):
        at = AT_SUMS + number * PLANES
        sums.append(jnp.concatenate([four(below_ref, at), four(above_ref, at)], 0))
    half_x, half_z = 0.5 * (sums[3] - sums[5]), 0.5 * (sums[4] - sums[5])
    nothing = jnp.zeros((ROWS, LANES), f32)
    outer = [nothing] * 19
    outer[0] = sums[0] - sums[3] - sums[4] + sums[5]
    outer[1], outer[2] = half_x + 0.5 * sums[1], half_x - 0.5 * sums[1]
    outer[5], outer[6] = half_z + 0.5 * sums[2], half_z - 0.5 * sums[2]
    outer[11] = outer[12] = 0.5 * sums[5]
    for number in range(5):
        known, mine = AT_POPS + number * PLANES, AT_NEXT + number * PLANES
        outer[rising[number]] = jnp.concatenate([four(below_ref, known), four(up_ref, mine)], 0)
        outer[falling[number]] = jnp.concatenate([four(down_ref, mine), four(above_ref, known)], 0)
    outer = [
        jnp.where(outside, 0.0 if member else 1.0, value) for member, value in enumerate(outer)
    ]
    outer_density, outer_speeds = moments_of(outer)
    lows, tops = [], []
    for axis_no in range(3):
        at = AT_SPEED + axis_no * PLANES
        second = jnp.concatenate([four(above_ref, at), four(below_ref, at)], 0)
        lows.append(jnp.where(row < PLANES, outer_speeds[axis_no], second))
        tops.append(jnp.where(row < PLANES, second, outer_speeds[axis_no]))

    def beyond(ref, field):
        pairs = pairs_of(jnp.concatenate(field, 0))
        total = jnp.zeros((24, LANES), f32)
        for block in range(tiles // 2):
            tile = AT_MARKS + 16 * block
            mark = jnp.concatenate([ref[tile : tile + 8, :], ref[tile + 8 : tile + 16, :]], 1)
            spot = spots(mark[1:2, :])
            found = gathered(pairs, spot)
            place = iota((ROWS, 2 * LANES), 0)
            frac = mark[3:4, :]
            weight = along_x(mark, (place % PLANES).astype(f32))
            weight = weight * jnp.where(place < PLANES, frac, 1.0 - frac)
            frac = mark[4:5, :]
            spreads = []
            for axis_no in range(3):
                here = found[axis_no * 8 : axis_no * 8 + 8]
                there = found[24 + axis_no * 8 : 32 + axis_no * 8]
                value = weight * (here + frac * (there - here))
                force = mark[5 + axis_no : 6 + axis_no, :] - jnp.sum(value, 0, keepdims=True)
                spreads.append(weight * force)
            spreads = jnp.concatenate(spreads, 0)
            ahead = spreads * frac
            total = total + scattered(spreads - ahead, ahead, spot)
        return total

    from_below = beyond(below_ref, lows)
    from_above = beyond(above_ref, tops)
    outer_pulls = [
        jnp.where(row < PLANES, from_below[a * 8 : a * 8 + 8], from_above[a * 8 : a * 8 + 8])
        for a in range(3)
    ]
    relax = relax_of(outer, outer_density, outer_speeds)
    outer_post = relaxed(outer, outer_density, outer_speeds, relax, outer_pulls)
    for number in range(5):
        outer_ref[number] = jnp.where(
            row < PLANES, outer_post[rising[number]], outer_post[falling[number]]
        )

    pairs = pairs_of(field_ref[...])
    total = jnp.zeros((96, LANES), f32)
    kept = [jnp.zeros((ROWS, LANES), f32) for axis_no in range(3)]
    for block in range(tiles // 2):
        tile = 16 * block
        mark = jnp.concatenate([marks_ref[tile : tile + 8, :], marks_ref[tile + 8 : tile + 16, :]], 1)
        at = AT_Z + 2 * block
        spot = spots(jnp.concatenate([marks_ref[at : at + 1, :], marks_ref[at + 1 : at + 2, :]], 1))
        found = gathered(pairs, spot)
        forces, spreads = forces_of(
            mark,
            block_weights(mark),
            [found[at * 8 : at * 8 + 8] for at in range(12)],
            [found[96 + at * 8 : 104 + at * 8] for at in range(12)],
        )
        spreads = jnp.concatenate(spreads, 0)
        ahead = spreads * mark[4:5, :]
        total = total + scattered(spreads - ahead, ahead, spot)
        for half in range(2):
            lanes = slice(half * LANES, (half + 1) * LANES)
            for axis_no in range(3):
                kept[axis_no] = jnp.where(
                    row == 2 * block + half, forces[axis_no][:, lanes], kept[axis_no]
                )
    back_ref[...] = jnp.zeros(back_ref.shape, f32)
    following = [roll(value, -1, 0) for value in kept]
    for part in range(sources // 2):
        tile, first = divmod(part * SLOTS, LANES)
        value = None
        for axis_no in range(3):
            moved = jnp.where(lane >= first, kept[axis_no], following[axis_no])
            moved = roll(moved, SHARE * axis_no - first, 1)
            value = moved if axis_no == 0 else jnp.where(lane // SHARE >= axis_no, moved, value)
        for source, at in ((part, tile), (part + sources // 2, tile + tiles // 2)):
            back_ref[source, 0:1, :] = value[at : at + 1, :]
    for plane in range(PLANES):
        ats = [a * 32 + plane * 8 for a in range(3)]
        pops = [wide_ref[member, plane] for member in range(19)]
        speeds = [field_ref[at : at + 8, :] for at in ats]
        density = density_ref[plane]
        relax = relax_of(pops, density, speeds)
        results = relaxed(pops, density, speeds, relax, [total[at : at + 8, :] for at in ats])
        for member in range(19):
            post_ref[member, plane] = results[member]

    to_right, to_left = jnp.zeros((ROWS, LANES), f32), jnp.zeros((ROWS, LANES), f32)
    for plane in range(PLANES):
        for member in range(19):
            shift_x, shift_y, shift_z = velocity_table[member]
            source = (plane - shift_x) % PLANES
            value = post_ref[member, source]
            if shift_y == 1:
                edge = outer_ref[rising.index(member), source : source + 1, :]
                value = jnp.where(row == 0, edge, roll(value, 1, 0))
            if shift_y == -1:
                at = PLANES + source
                edge = outer_ref[falling.index(member), at : at + 1, :]
                value = jnp.where(row == ROWS - 1, edge, roll(value, -1, 0))
            if shift_z:
                value = roll(value, shift_z, 1)
            if shift_z == 1:
                place = ahead_z.index(member) * PLANES + plane
                to_right = jnp.where(lane == place, roll(value, place, 1), to_right)
            if shift_z == -1:
                place = back_z.index(member) * PLANES + plane
                to_left = jnp.where(lane == place, roll(value, place + 1, 1), to_left)
            if shift_y == 1:
                value = jnp.where(row == first_wall, post_ref[opposite[member], plane], value)
            if shift_y == -1:
                value = jnp.where(row == last_wall, post_ref[opposite[member], plane], value)
            moved_ref[member, plane] = value
    for target, face in ((left, to_left), (right, to_right)):
        early, late = jnp.zeros((ROWS, LANES), f32), jnp.zeros((ROWS, LANES), f32)
        for number in range(ROWS):
            early = jnp.where(row == number, roll(face, EARLY * number, 1), early)
            late = jnp.where(row == number, roll(face, LATE_FACE - EARLY + 4 * number, 1), late)
        early = jnp.where(lane // EARLY == row, early, 0.0)
        late = jnp.where((lane - LATE_FACE) // 4 == row, late, 0.0)
        late = jnp.where(lane >= LATE_FACE, late, 0.0)
        mine = jnp.where(iota((1, LANES), 1) < LATE_FACE, back_ref[target, 0:1, :], 0.0)
        back_ref[target, 0:1, :] = mine + jnp.sum(late, 0, keepdims=True)
        back_ref[target, 1:2, :] = jnp.sum(early, 0, keepdims=True)


def last_kernel(
    moved_ref, got_ref, owner_ref, rank_ref, pops_ref, force_ref
):
    left, right = z_neighbours()
    _, _, first_wall, last_wall = y_ends()
    lane = iota((ROWS, LANES), 1)
    row = iota((ROWS, LANES), 0)

    def face_of(source):
        late = jnp.broadcast_to(got_ref[source, 0:1, :], (ROWS, LANES))
        early = jnp.broadcast_to(got_ref[source, 1:2, :], (ROWS, LANES))
        face = jnp.zeros((ROWS, LANES), f32)
        for number in range(ROWS):
            value = roll(late, EARLY - LATE_FACE - 4 * number, 1)
            value = jnp.where(lane < EARLY, roll(early, -EARLY * number, 1), value)
            face = jnp.where(row == number, value, face)
        return face

    from_left, from_right = face_of(left), face_of(right)
    changed = [i for i in range(19) if velocity_table[i][2]]
    for member in range(19):
        if member not in changed:
            pops_ref[member] = moved_ref[member]
    for number, member in enumerate(changed):
        _, shift_y, shift_z = velocity_table[member]
        for plane in range(PLANES):
            if shift_z == 1:
                place = ahead_z.index(member) * PLANES + plane
                edge, here = roll(from_left, -place, 1), lane == 0
            else:
                place = back_z.index(member) * PLANES + plane
                edge, here = roll(from_right, LANES - 1 - place, 1), lane == LANES - 1
            if shift_y == 1:
                here = here & (row != first_wall)
            if shift_y == -1:
                here = here & (row != last_wall)
            pops_ref[member, plane] = jnp.where(here, edge, moved_ref[member, plane])
    owners, markers = got_ref.shape[0], owner_ref.shape[1]
    owner = owner_ref[...]
    spot = (iota((LANES, markers), 0).astype(f32) == rank_ref[...]).astype(bf16)
    rows = got_ref[:, 0, :]
    high, low = split_two(
        jnp.concatenate([roll(rows, -SHARE * axis_no, 1) for axis_no in range(3)], 0)
    )
    found = jnp.dot(
        jnp.concatenate([high, low], 1),
        jnp.concatenate([spot, spot], 0),
        preferred_element_type=f32,
    )
    hit = iota((owners, markers), 0) == owner
    for axis_no in range(3):
        value = jnp.where(hit, found[axis_no * owners : (axis_no + 1) * owners], 0.0)
        force_ref[axis_no : axis_no + 1, :] = jnp.sum(value, 0, keepdims=True) / ref_speed


def body(populations, marker_owner, marker_cell, marker_frac, marker_speed, marker_count):
    count_gy, count_gz = lax.axis_size("gy"), lax.axis_size("gz")
    markers = marker_owner.shape[0]
    vmem = pl.BlockSpec(memory_space=pltpu.VMEM)
    shape = jax.ShapeDtypeStruct
    tiles = shape((count_gz, 8, LANES), f32)
    field = shape((96, LANES), f32)
    cells = shape((PLANES, ROWS, LANES), f32)
    lattice = shape(populations.shape, f32)
    inputs = [
        marker_owner.reshape(1, markers),
        marker_cell,
        marker_frac,
        marker_speed,
        populations,
    ]
    send, rank, live, speeds, density, relax = call(
        first_kernel,
        [tiles, shape((1, markers), f32), shape((1, markers), jnp.int32), field, cells, cells],
        [marker_count.reshape(1, 1)]
        + [pltpu.with_memory_space_constraint(value, pltpu.HBM) for value in inputs],
        [vmem] + [pl.BlockSpec(memory_space=pltpu.HBM)] * 5,
        scratch=[pltpu.VMEM(value.shape, value.dtype) for value in inputs]
        + [pltpu.SemaphoreType.DMA((5,))],
    )
    got = lax.all_to_all(send, "gz", split_axis=0, concat_axis=0, tiled=True)
    face = shape((FACE_ROWS, LANES), f32)
    next_pops, up, down, marks = call(
        second_kernel,
        [lattice, face, face, shape((MARK_ROWS, LANES), f32)],
        [populations, got, speeds, density, relax],
        [vmem] * 5,
        scratch=[
            pltpu.VMEM(populations.shape, f32),
            pltpu.VMEM((24, ROWS, LANES), f32),
            pltpu.VMEM((24, ROWS, LANES), f32),
            pltpu.VMEM((96, LANES), f32),
        ],
    )
    below = lax.ppermute(up, "gy", [(i, i + 1) for i in range(count_gy - 1)])
    above = lax.ppermute(down, "gy", [(i + 1, i) for i in range(count_gy - 1)])
    moved, back = call(
        third_kernel,
        [lattice, shape((count_gz, 2, LANES), f32)],
        [next_pops, up, down, marks, below, above],
        [vmem] * 6,
        scratch=[
            pltpu.VMEM(populations.shape, f32),
            pltpu.VMEM((96, LANES), f32),
            pltpu.VMEM((PLANES, ROWS, LANES), f32),
            pltpu.VMEM(populations.shape, f32),
            pltpu.VMEM((5, ROWS, LANES), f32),
        ],
    )
    back = lax.all_to_all(back, "gz", split_axis=0, concat_axis=0, tiled=True)
    pops, force = call(
        last_kernel,
        [lattice, shape((3, markers), f32)],
        [moved, back, live, rank],
        [vmem] * 4,
    )
    return pops, force


def solution(mesh):
    return jax.shard_map(
        body,
        mesh=mesh,
        in_specs=(
            P(None, None, "gy", "gz"),
            P(("gy", "gz"), None),
            P(None, ("gy", "gz")),
            P(None, ("gy", "gz")),
            P(None, ("gy", "gz")),
            P(("gy", "gz")),
        ),
        out_specs=(P(None, None, "gy", "gz"), P(None, ("gy", "gz"))),
        check_vma=False,
    )
```

```python
import math

import jax
import jax.numpy as jnp
from jax import lax
from jax.experimental import pallas as pl
from jax.experimental.pallas import tpu as pltpu
from jax.sharding import PartitionSpec as P

INTERPRET = False

velocity_table = (
    (0, 0, 0),
    (1, 0, 0),
    (-1, 0, 0),
    (0, 1, 0),
    (0, -1, 0),
    (0, 0, 1),
    (0, 0, -1),
    (1, 1, 0),
    (-1, -1, 0),
    (1, -1, 0),
    (-1, 1, 0),
    (1, 0, 1),
    (-1, 0, -1),
    (1, 0, -1),
    (-1, 0, 1),
    (0, 1, 1),
    (0, -1, -1),
    (0, 1, -1),
    (0, -1, 1),
)
opposite = (0, 2, 1, 4, 3, 6, 5, 8, 7, 10, 9, 12, 11, 14, 13, 16, 15, 18, 17)
rising = tuple(i for i in range(19) if velocity_table[i][1] == 1)
falling = tuple(opposite[i] for i in rising)
level = tuple(i for i in range(19) if velocity_table[i][1] == 0)
ahead_z = tuple(i for i in range(19) if velocity_table[i][2] == 1)
back_z = tuple(opposite[i] for i in ahead_z)
tau_base = 0.52
smag_const = 0.17
ref_speed = 0.05

PLANES = 4
ROWS = 8
LANES = 128
SLOTS = 24
SHARE = 32
FEW = 4
SPARE = SLOTS - FEW
FIRST_SPARE = SHARE
FIRST_Z = SHARE + 2 * SPARE
FIRST_RIM = 76
LATE_FACE = 3 * SHARE
EARLY = 16
RIM_WORDS = 13
AT_SPEED, AT_SUMS, AT_POPS, AT_NEXT, AT_MARKS, FACE_ROWS = 0, 12, 36, 56, 80, 128
AT_Z, MARK_ROWS = 48, 56

f32 = jnp.float32
bf16 = jnp.bfloat16


def iota(shape, dim):
    return lax.broadcasted_iota(jnp.int32, shape, dim)


def roll(value, shift, axis):
    shift = shift % value.shape[axis]
    return pltpu.roll(value, shift, axis) if shift else value


def split_two(value):
    high = value.astype(bf16)
    return high, (value - high.astype(f32)).astype(bf16)


def call(kernel, out_shape, args, in_specs, scratch=(), out_specs=None, aliases=()):
    vmem = pl.BlockSpec(memory_space=pltpu.VMEM)
    return pl.pallas_call(
        kernel,
        out_shape=out_shape,
        in_specs=in_specs,
        out_specs=out_specs or [vmem] * len(out_shape),
        input_output_aliases=dict(aliases),
        scratch_shapes=list(scratch),
        compiler_params=pltpu.CompilerParams(vmem_limit_bytes=32 * 1024 * 1024),
        interpret=INTERPRET,
    )(*args)


def z_neighbours():
    column, size = lax.axis_index("gz"), lax.axis_size("gz")
    return (column + size - 1) % size, (column + 1) % size


def y_ends():
    place, size = lax.axis_index("gy"), lax.axis_size("gy")
    first, last = place == 0, place == size - 1
    return (
        jnp.where(first, -1, 0),
        jnp.where(last, -1, ROWS - 1),
        jnp.where(first, 0, -1),
        jnp.where(last, ROWS - 1, -1),
    )


def moments_of(pops):
    density = pops[0]
    for member in range(1, 19):
        density = density + pops[member]
    parts = []
    for axis_no in range(3):
        total = None
        for member in range(19):
            if velocity_table[member][axis_no] == 1:
                total = pops[member] if total is None else total + pops[member]
        for member in range(19):
            if velocity_table[member][axis_no] == -1:
                total = total - pops[member]
        parts.append(total)
    inverse = 1.0 / density
    return density, [part * inverse for part in parts]


def relax_of(pops, density, speeds):
    factor = 18.0 * math.sqrt(2.0) * smag_const * smag_const
    moved = [density * part for part in speeds]
    pair = [pops[2 * k + 1] + pops[2 * k + 2] for k in range(9)]
    third = density * (1.0 / 3.0)
    xx = pair[0] + pair[3] + pair[4] + pair[5] + pair[6] - third - moved[0] * speeds[0]
    yy = pair[1] + pair[3] + pair[4] + pair[7] + pair[8] - third - moved[1] * speeds[1]
    zz = pair[2] + pair[5] + pair[6] + pair[7] + pair[8] - third - moved[2] * speeds[2]
    xy = pair[3] - pair[4] - moved[0] * speeds[1]
    xz = pair[5] - pair[6] - moved[0] * speeds[2]
    yz = pair[7] - pair[8] - moved[1] * speeds[2]
    norm_sq = xx * xx + yy * yy + zz * zz + 2.0 * (xy * xy + xz * xz + yz * yz)
    return 0.5 * (tau_base + jnp.sqrt(tau_base * tau_base + factor * jnp.sqrt(norm_sq) / density))


def along_of(member, speeds):
    total = None
    for axis_no in range(3):
        if velocity_table[member][axis_no] == 1:
            total = speeds[axis_no] if total is None else total + speeds[axis_no]
    for axis_no in range(3):
        if velocity_table[member][axis_no] == -1:
            total = total - speeds[axis_no]
    return total


def relaxed(pops, density, speeds, relax, pulls):
    pull = relax / density
    shifted = [speeds[a] + pull * pulls[a] for a in range(3)]
    shifted_sq = shifted[0] * shifted[0] + shifted[1] * shifted[1] + shifted[2] * shifted[2]
    rate = 1.0 / relax
    keep = 1.0 - rate
    scale = rate * density
    base = scale * (1.0 - 1.5 * shifted_sq)
    quad = 4.5 * scale
    results = [keep * pops[0] + base * (1.0 / 3.0)]
    for pair in range(9):
        plus = 2 * pair + 1
        along = along_of(plus, shifted)
        weight = 1.0 / 18.0 if pair < 3 else 1.0 / 36.0
        even = weight * (base + quad * along * along)
        odd = (3.0 * weight) * (scale * along)
        results.append(keep * pops[plus] + (even + odd))
        results.append(keep * pops[plus + 1] + (even - odd))
    return results


def along_x(mark, plane):
    base, frac = mark[0:1, :], mark[2:3, :]
    following = jnp.where(base == float(PLANES), 0.0, base)
    weight = jnp.where(base - 1.0 == plane, 1.0 - frac, 0.0)
    return jnp.where((base > 0.5) & (following == plane), frac, weight)


def block_weights(mark):
    base, frac = mark[1:2, :], mark[3:4, :]
    row = iota((ROWS, mark.shape[1]), 0).astype(f32)
    along_y = jnp.where(row == base, 1.0 - frac, jnp.where(row == base + 1.0, frac, 0.0))
    return [along_y * along_x(mark, float(plane)) for plane in range(PLANES)]


def spots(base_z):
    count = base_z.shape[1]
    one, none = jnp.ones((), bf16), jnp.zeros((), bf16)
    return jnp.where(iota((LANES, count), 0).astype(bf16) == base_z.astype(bf16), one, none)


def pairs_of(field):
    high, low = split_two(field)
    next_high, next_low = split_two(roll(field, -1, 1))
    return jnp.concatenate(
        [jnp.concatenate([high, low], 1), jnp.concatenate([next_high, next_low], 1)], 0
    )


def gathered(pairs, spot):
    return jnp.dot(pairs, jnp.concatenate([spot, spot], 0), preferred_element_type=f32)


def sums_of(here, there, spot):
    size = here.shape[0]
    high, low = split_two(here)
    next_high, next_low = split_two(there)
    sums = lax.dot_general(
        jnp.concatenate([high, low, next_high, next_low], 0),
        spot,
        (((1,), (1,)), ((), ())),
        preferred_element_type=f32,
    )
    first = sums[0:size] + sums[size : 2 * size]
    second = sums[2 * size : 3 * size] + sums[3 * size :]
    return first, second


def scattered(here, there, spot):
    first, second = sums_of(here, there, spot)
    return first + roll(second, 1, 1)


def forces_of(mark, weights, here, there):
    frac = mark[4:5, :]
    forces, spreads = [], []
    for axis_no in range(3):
        total = None
        for plane in range(PLANES):
            at = axis_no * PLANES + plane
            value = weights[plane] * (here[at] + frac * (there[at] - here[at]))
            total = value if total is None else total + value
        force = mark[5 + axis_no : 6 + axis_no, :] - jnp.sum(total, 0, keepdims=True)
        forces.append(force)
        for plane in range(PLANES):
            spreads.append(weights[plane] * force)
    return forces, spreads


def first_kernel(
    count_ref, owner_hbm, cell_hbm, frac_hbm, speed_hbm, pops_hbm,
    send_ref, rank_ref, live_ref, pops_ref, field_ref, density_ref, relax_ref,
    owner_ref, cell_ref, frac_ref, speed_ref, sems,
):
    copies = [
        pltpu.make_async_copy(source, target, sems.at[number])
        for number, (source, target) in enumerate(
            [
                (owner_hbm, owner_ref),
                (cell_hbm, cell_ref),
                (frac_hbm, frac_ref),
                (speed_hbm, speed_ref),
                (pops_hbm, pops_ref),
            ]
        )
    ]
    for copy in copies:
        copy.start()
    for copy in copies[0:4]:
        copy.wait()
    owners, markers = send_ref.shape[0], owner_ref.shape[1]
    live = iota((1, markers), 1) < count_ref[...]
    owner = jnp.where(live, owner_ref[...], -1)
    live_ref[...] = owner
    base_z = cell_ref[2:3, :]
    upper, lower = base_z == LANES - 2, base_z == 0
    twin = jnp.where(
        upper,
        jnp.where(owner == owners - 1, 0, owner + 1),
        jnp.where(owner == 0, owners - 1, owner - 1),
    )
    twin = jnp.where(live & (upper | lower), twin, -1)
    hit = iota((owners, markers), 0) == owner
    hits = jnp.concatenate(
        [hit.astype(f32), (hit & upper).astype(f32), (hit & lower).astype(f32)], 0
    )
    blocks = markers // LANES
    parts = [hits[:, block * LANES : (block + 1) * LANES] for block in range(blocks)]
    earlier = iota((LANES, 2 * LANES), 0) < iota((LANES, 2 * LANES), 1)
    counts = jnp.dot(
        jnp.concatenate(parts, 0).astype(bf16), earlier.astype(bf16), preferred_element_type=f32
    )
    before = None
    ranks = [[], [], []]
    for block in range(blocks):
        inner = counts[block * 3 * owners : (block + 1) * 3 * owners]
        place = inner[:, 0:LANES] if before is None else inner[:, 0:LANES] + before
        before = inner[:, LANES:] if before is None else inner[:, LANES:] + before
        picked = parts[block] * place
        for kind in range(3):
            ranks[kind].append(
                jnp.sum(picked[kind * owners : (kind + 1) * owners], 0, keepdims=True)
            )
    rank, rank_up, rank_low = [jnp.concatenate(kind, 1) for kind in ranks]
    rank_ref[...] = rank
    copies[4].wait()
    lane_up = jnp.where(rank_up < FEW, SLOTS + rank_up, FIRST_SPARE - FEW + rank_up)
    lane_low = jnp.where(
        rank_low < FEW, SLOTS + FEW + rank_low, FIRST_SPARE + SPARE - FEW + rank_low
    )
    lane_twin = jnp.where(upper, lane_up, lane_low)
    lane_z = FIRST_Z + jnp.where(rank >= 16.0, 2.0, jnp.where(rank >= 8.0, 1.0, 0.0))
    slot_z = rank - 8.0 * (lane_z - FIRST_Z)
    lane = iota((LANES, markers), 0).astype(f32)
    spot_own = (lane == rank).astype(bf16)
    spot_twin = (lane == lane_twin).astype(bf16)
    spot_z = (lane == lane_z).astype(bf16)
    row = iota((8, markers), 0)
    words = jnp.where(row == 0, cell_ref[0:1, :] + 1, cell_ref[1:2, :]).astype(f32)
    for number in range(3):
        words = jnp.where(row == 2 + number, frac_ref[number : number + 1, :], words)
        words = jnp.where(row == 5 + number, speed_ref[number : number + 1, :], words)
    high, low = split_two(words)
    high, low = high.astype(f32), low.astype(f32)
    words_z = jnp.where(row.astype(f32) == slot_z, base_z.astype(f32), 0.0)

    def to_owners(value, target):
        value = jnp.concatenate([value, value], 0).astype(bf16)
        target = jnp.broadcast_to(target.astype(f32), (16, markers)).astype(bf16)
        first = jnp.where(iota((16, markers), 0) < 8, 0.0, 1.0).astype(bf16)
        rows = []
        for number in range(0, owners, 2):
            rows.append(jnp.where(target == first + float(number), value, jnp.zeros((), bf16)))
        return jnp.concatenate(rows, 0)

    def placed(left, spot):
        return lax.dot_general(left, spot, (((1,), (1,)), ((), ())), preferred_element_type=f32)

    tiles = placed(to_owners(high, owner), spot_own) + placed(to_owners(low, owner), spot_own)
    tiles = tiles + placed(to_owners(high, twin), spot_twin)
    tiles = tiles + placed(to_owners(low, twin), spot_twin)
    tiles = tiles + placed(to_owners(words_z, owner), spot_z)
    send_ref[...] = tiles.reshape(owners, 8, LANES)


    lane = iota((ROWS, LANES), 1)
    to_right, to_left = jnp.zeros((ROWS, LANES), f32), jnp.zeros((ROWS, LANES), f32)
    for plane in range(PLANES):
        pops = [pops_ref[member, plane] for member in range(19)]
        density, speeds = moments_of(pops)
        relax = relax_of(pops, density, speeds)
        density_ref[plane] = density
        relax_ref[plane] = relax
        for axis_no in range(3):
            at = axis_no * 32 + plane * 8
            field_ref[at : at + 8, :] = speeds[axis_no]
        common = [density, *speeds, relax]
        for word in range(RIM_WORDS):
            place = FIRST_RIM + word * PLANES + plane
            if word < 5:
                right, left, shift = common[word], common[word], 0
            elif word < 10:
                right, left, shift = pops[ahead_z[word - 5]], pops[back_z[word - 5]], 0
            else:
                right, left, shift = speeds[word - 10], speeds[word - 10], 1
            here = lane == place
            to_right = jnp.where(here, roll(right, place - (LANES - 1) + shift, 1), to_right)
            to_left = jnp.where(here, roll(left, place - shift, 1), to_left)
    left, right = z_neighbours()
    send_ref[left] = send_ref[left] + to_left
    send_ref[right] = send_ref[right] + to_right


def second_kernel(
    pops_ref, got_ref, field_ref, density_ref, relax_ref,
    next_ref, up_ref, down_ref, marks_ref,
    post_ref, near_ref, far_ref, twin_ref,
):
    left, right = z_neighbours()
    lane = iota((ROWS, LANES), 1)
    row = iota((ROWS, LANES), 0)
    sources = got_ref.shape[0]

    tiles = sources * SLOTS // LANES
    marks = [None] * tiles
    twin_marks = [None] * (sources * 2 * FEW // LANES)
    for source in range(sources):
        tile, first = divmod(source * SLOTS, LANES)
        words = roll(got_ref[source], first, 1)
        marks[tile] = words if marks[tile] is None else jnp.where(lane >= first, words, marks[tile])
        if first + SLOTS > LANES:
            marks[tile + 1] = words
        tile, first = divmod(source * 2 * FEW, LANES)
        words = roll(got_ref[source], first - SLOTS, 1)
        old = twin_marks[tile]
        twin_marks[tile] = words if old is None else jnp.where(lane >= first, words, old)
    bases = []
    for tile in range(tiles):
        first, last = tile * LANES // SLOTS, ((tile + 1) * LANES - 1) // SLOTS
        rows = jnp.concatenate([got_ref[source] for source in range(first, last + 1)], 0)

        def slot_of(shape):
            member = iota(shape, 1) + tile * LANES
            source = (member * 2731) >> 16
            return source, member - SLOTS * source

        _, slot = slot_of((LANES, LANES))
        chosen = (iota((LANES, LANES), 0) == FIRST_Z + (slot >> 3)).astype(bf16)
        value = jnp.dot(rows.astype(bf16), chosen, preferred_element_type=f32)
        source, slot = slot_of(value.shape)
        here = iota(value.shape, 0) == (source - first) * 8 + (slot & 7)
        bases.append(jnp.sum(jnp.where(here, value, 0.0), 0, keepdims=True))
    for tile in range(tiles):
        marks_ref[tile * 8 : tile * 8 + 8, :] = marks[tile]
        marks_ref[AT_Z + tile : AT_Z + tile + 1, :] = bases[tile]
        for ref, base_y in ((up_ref, float(ROWS - 2)), (down_ref, 0.0)):
            words = jnp.where((row == 0) & (marks[tile][1:2, :] != base_y), 0.0, marks[tile])
            words = jnp.where(row == 1, bases[tile], words)
            ref[AT_MARKS + tile * 8 : AT_MARKS + tile * 8 + 8, :] = words
    for ref in (up_ref, down_ref):
        ref[AT_NEXT + 20 : AT_MARKS, :] = jnp.zeros((AT_MARKS - AT_NEXT - 20, LANES), f32)

    ends = jnp.where(lane >= FIRST_RIM, got_ref[left], roll(got_ref[right], 64, 1))
    rim = [roll(ends, -(FIRST_RIM + PLANES * word), 1) for word in range(RIM_WORDS)]

    def spread_lane(value, at):
        return jnp.broadcast_to(value[:, at : at + 1], (ROWS, LANES))

    for axis_no in range(3):
        for plane in range(PLANES):
            at = axis_no * PLANES + plane
            near_ref[at] = spread_lane(rim[10 + axis_no], plane)
            near_ref[12 + at] = spread_lane(rim[1 + axis_no], 64 + plane)
            far_ref[at] = spread_lane(rim[1 + axis_no], plane)
            far_ref[12 + at] = spread_lane(rim[10 + axis_no], 64 + plane)

    def twins(of_left, of_right):
        def both(ref):
            return [
                jnp.where(of_left, ref[at], jnp.where(of_right, ref[12 + at], 0.0))
                for at in range(12)
            ]

        return both(near_ref), both(far_ref)

    def sides(lefts, rights, count):
        place, member = iota((LANES, count), 0), iota((LANES, count), 1)
        chosen = jnp.where(place < 64, lefts(member).astype(f32), rights(member).astype(f32))
        return chosen.astype(bf16)

    near, far = twins(lane % (2 * FEW) < FEW, lane % (2 * FEW) >= FEW)
    side = sides(
        lambda member: member % (2 * FEW) < FEW,
        lambda member: member % (2 * FEW) >= FEW,
        2 * LANES,
    )
    rim_left = iota((96, LANES), 1) < 64
    pairs = pairs_of(field_ref[...])
    force = jnp.zeros((96, LANES), f32)
    for block in range(tiles // 2):
        mark = jnp.concatenate(marks[2 * block : 2 * block + 2], 1)
        spot = spots(jnp.concatenate(bases[2 * block : 2 * block + 2], 1))
        found = gathered(pairs, spot)
        _, spreads = forces_of(
            mark,
            block_weights(mark),
            [found[at * 8 : at * 8 + 8] for at in range(12)],
            [found[96 + at * 8 : 104 + at * 8] for at in range(12)],
        )
        spreads = jnp.concatenate(spreads, 0)
        ahead = spreads * mark[4:5, :]
        force = force + scattered(spreads - ahead, ahead, spot)
    mark = jnp.concatenate(twin_marks, 1)
    _, spreads = forces_of(
        mark,
        block_weights(mark),
        [jnp.concatenate([value] * 2, 1) for value in near],
        [jnp.concatenate([value] * 2, 1) for value in far],
    )
    spreads = jnp.concatenate(spreads, 0)
    ahead = spreads * mark[4:5, :]
    first, second = sums_of(spreads - ahead, ahead, side)
    twin_ref[...] = jnp.where(rim_left, second, first)

    further = jnp.where((lane >= FIRST_SPARE) & (lane < FIRST_Z), 1.0, 0.0)
    most = got_ref[0]
    for source in range(1, sources):
        most = jnp.maximum(most, got_ref[source])

    @pl.when(jnp.max(most * further) > 0.5)
    def _():
        near, far = twins(lane < SPARE, lane >= SPARE)
        side = sides(lambda member: member < SPARE, lambda member: member >= SPARE, LANES)

        def one(source, carry):
            mark = roll(got_ref[source], -FIRST_SPARE, 1)
            mark = jnp.where(lane < 2 * SPARE, mark, 0.0)
            _, spreads = forces_of(mark, block_weights(mark), near, far)
            spreads = jnp.concatenate(spreads, 0)
            ahead = spreads * mark[4:5, :]
            first, second = sums_of(spreads - ahead, ahead, side)
            twin_ref[...] = twin_ref[...] + jnp.where(rim_left, second, first)
            return carry

        lax.fori_loop(0, sources, one, 0)

    sums = twin_ref[...]
    pulls = []
    for axis_no in range(3):
        total = None
        for plane in range(PLANES):
            at = axis_no * 32 + plane * 8
            value = sums[at : at + 8, :]
            total = value if total is None else jnp.where(lane % PLANES == plane, value, total)
        pulls.append(total)
    density, speeds, relax = rim[0], rim[1:4], rim[4]
    pull = relax / density
    shifted = [speeds[a] + pull * pulls[a] for a in range(3)]
    shifted_sq = shifted[0] * shifted[0] + shifted[1] * shifted[1] + shifted[2] * shifted[2]
    rate = 1.0 / relax
    sign = jnp.where(lane < 64, 1.0, -1.0)
    rim_post = []
    for number, member in enumerate(ahead_z):
        along = sign * along_of(member, shifted)
        weight = 1.0 / 18.0 if number == 0 else 1.0 / 36.0
        target = weight * density * (1.0 + 3.0 * along + 4.5 * along * along - 1.5 * shifted_sq)
        rim_post.append((1.0 - rate) * rim[5 + number] + rate * target)

    for plane in range(PLANES):
        ats = [a * 32 + plane * 8 for a in range(3)]
        results = relaxed(
            [pops_ref[member, plane] for member in range(19)],
            density_ref[plane],
            [field_ref[at : at + 8, :] for at in ats],
            relax_ref[plane],
            [force[at : at + 8, :] for at in ats],
        )
        for member in range(19):
            post_ref[member, plane] = results[member]

    for plane in range(PLANES):
        pops = []
        for member in range(19):
            shift_x, shift_y, shift_z = velocity_table[member]
            source = (plane - shift_x) % PLANES
            value = post_ref[member, source]
            if shift_z == 1:
                edge = roll(rim_post[ahead_z.index(member)], -source, 1)
                value = jnp.where(lane == 0, edge, roll(value, 1, 1))
            if shift_z == -1:
                edge = roll(rim_post[back_z.index(member)], 63 - source, 1)
                value = jnp.where(lane == LANES - 1, edge, roll(value, -1, 1))
            if shift_y == 1:
                at = AT_NEXT + rising.index(member) * PLANES + plane
                up_ref[at : at + 1, :] = value[ROWS - 1 : ROWS, :]
                value = jnp.where(row == 0, post_ref[opposite[member], plane], roll(value, 1, 0))
            if shift_y == -1:
                at = AT_NEXT + falling.index(member) * PLANES + plane
                down_ref[at : at + 1, :] = value[0:1, :]
                value = jnp.where(
                    row == ROWS - 1, post_ref[opposite[member], plane], roll(value, -1, 0)
                )
            next_ref[member, plane] = value
            pops.append(value)
        _, speeds = moments_of(pops)
        for axis_no in range(3):
            at = AT_SPEED + axis_no * PLANES + plane
            up_ref[at : at + 1, :] = speeds[axis_no][ROWS - 2 : ROWS - 1, :]
            down_ref[at : at + 1, :] = speeds[axis_no][1:2, :]
        cross = pops[11] + pops[12]
        other = pops[13] + pops[14]
        across, along = pops[1] + pops[2], pops[5] + pops[6]
        lean = pops[11] - pops[12]
        tilt = pops[13] - pops[14]
        sums = [
            pops[0] + across + along + cross + other,
            pops[1] - pops[2] + lean + tilt,
            pops[5] - pops[6] + lean - tilt,
            across + cross + other,
            along + cross + other,
            cross - other,
        ]
        for number, value in enumerate(sums):
            at = AT_SUMS + number * PLANES + plane
            up_ref[at : at + 1, :] = value[ROWS - 1 : ROWS, :]
            down_ref[at : at + 1, :] = value[0:1, :]
        for number in range(5):
            at = AT_POPS + number * PLANES + plane
            up_ref[at : at + 1, :] = pops[rising[number]][ROWS - 1 : ROWS, :]
            down_ref[at : at + 1, :] = pops[falling[number]][0:1, :]


def third_kernel(
    next_ref, up_ref, down_ref, marks_ref, below_ref, above_ref,
    moved_ref, back_ref,
    wide_ref, field_ref, density_ref, post_ref, outer_ref,
):
    left, right = z_neighbours()
    first_open, last_open, first_wall, last_wall = y_ends()
    lane = iota((ROWS, LANES), 1)
    row = iota((ROWS, LANES), 0)
    sources = back_ref.shape[0]
    tiles = sources * SLOTS // LANES

    def four(ref, at):
        return ref[at : at + PLANES, :]

    for plane in range(PLANES):
        pops = []
        for member in range(19):
            value = next_ref[member, plane]
            if member in rising:
                at = AT_NEXT + rising.index(member) * PLANES + plane
                value = jnp.where(row == first_open, below_ref[at : at + 1, :], value)
            if member in falling:
                at = AT_NEXT + falling.index(member) * PLANES + plane
                value = jnp.where(row == last_open, above_ref[at : at + 1, :], value)
            wide_ref[member, plane] = value
            pops.append(value)
        density, speeds = moments_of(pops)
        density_ref[plane] = density
        for axis_no in range(3):
            at = axis_no * 32 + plane * 8
            field_ref[at : at + 8, :] = speeds[axis_no]

    outside = ((row < PLANES) & (first_wall == 0)) | ((row >= PLANES) & (last_wall > 0))
    sums = []
    for number in range(6):
        at = AT_SUMS + number * PLANES
        sums.append(jnp.concatenate([four(below_ref, at), four(above_ref, at)], 0))
    half_x, half_z = 0.5 * (sums[3] - sums[5]), 0.5 * (sums[4] - sums[5])
    nothing = jnp.zeros((ROWS, LANES), f32)
    outer = [nothing] * 19
    outer[0] = sums[0] - sums[3] - sums[4] + sums[5]
    outer[1], outer[2] = half_x + 0.5 * sums[1], half_x - 0.5 * sums[1]
    outer[5], outer[6] = half_z + 0.5 * sums[2], half_z - 0.5 * sums[2]
    outer[11] = outer[12] = 0.5 * sums[5]
    for number in range(5):
        known, mine = AT_POPS + number * PLANES, AT_NEXT + number * PLANES
        outer[rising[number]] = jnp.concatenate([four(below_ref, known), four(up_ref, mine)], 0)
        outer[falling[number]] = jnp.concatenate([four(down_ref, mine), four(above_ref, known)], 0)
    outer = [
        jnp.where(outside, 0.0 if member else 1.0, value) for member, value in enumerate(outer)
    ]
    outer_density, outer_speeds = moments_of(outer)
    lows, tops = [], []
    for axis_no in range(3):
        at = AT_SPEED + axis_no * PLANES
        second = jnp.concatenate([four(above_ref, at), four(below_ref, at)], 0)
        lows.append(jnp.where(row < PLANES, outer_speeds[axis_no], second))
        tops.append(jnp.where(row < PLANES, second, outer_speeds[axis_no]))

    def beyond(ref, field):
        pairs = pairs_of(jnp.concatenate(field, 0))
        total = jnp.zeros((24, LANES), f32)
        for block in range(tiles // 2):
            tile = AT_MARKS + 16 * block
            mark = jnp.concatenate([ref[tile : tile + 8, :], ref[tile + 8 : tile + 16, :]], 1)
            spot = spots(mark[1:2, :])
            found = gathered(pairs, spot)
            place = iota((ROWS, 2 * LANES), 0)
            frac = mark[3:4, :]
            weight = along_x(mark, (place % PLANES).astype(f32))
            weight = weight * jnp.where(place < PLANES, frac, 1.0 - frac)
            frac = mark[4:5, :]
            spreads = []
            for axis_no in range(3):
                here = found[axis_no * 8 : axis_no * 8 + 8]
                there = found[24 + axis_no * 8 : 32 + axis_no * 8]
                value = weight * (here + frac * (there - here))
                force = mark[5 + axis_no : 6 + axis_no, :] - jnp.sum(value, 0, keepdims=True)
                spreads.append(weight * force)
            spreads = jnp.concatenate(spreads, 0)
            ahead = spreads * frac
            total = total + scattered(spreads - ahead, ahead, spot)
        return total

    from_below = beyond(below_ref, lows)
    from_above = beyond(above_ref, tops)
    outer_pulls = [
        jnp.where(row < PLANES, from_below[a * 8 : a * 8 + 8], from_above[a * 8 : a * 8 + 8])
        for a in range(3)
    ]
    relax = relax_of(outer, outer_density, outer_speeds)
    outer_post = relaxed(outer, outer_density, outer_speeds, relax, outer_pulls)
    for number in range(5):
        outer_ref[number] = jnp.where(
            row < PLANES, outer_post[rising[number]], outer_post[falling[number]]
        )

    pairs = pairs_of(field_ref[...])
    total = jnp.zeros((96, LANES), f32)
    kept = [jnp.zeros((ROWS, LANES), f32) for axis_no in range(3)]
    for block in range(tiles // 2):
        tile = 16 * block
        mark = jnp.concatenate([marks_ref[tile : tile + 8, :], marks_ref[tile + 8 : tile + 16, :]], 1)
        at = AT_Z + 2 * block
        spot = spots(jnp.concatenate([marks_ref[at : at + 1, :], marks_ref[at + 1 : at + 2, :]], 1))
        found = gathered(pairs, spot)
        forces, spreads = forces_of(
            mark,
            block_weights(mark),
            [found[at * 8 : at * 8 + 8] for at in range(12)],
            [found[96 + at * 8 : 104 + at * 8] for at in range(12)],
        )
        spreads = jnp.concatenate(spreads, 0)
        ahead = spreads * mark[4:5, :]
        total = total + scattered(spreads - ahead, ahead, spot)
        for half in range(2):
            lanes = slice(half * LANES, (half + 1) * LANES)
            for axis_no in range(3):
                kept[axis_no] = jnp.where(
                    row == 2 * block + half, forces[axis_no][:, lanes], kept[axis_no]
                )
    back_ref[...] = jnp.zeros(back_ref.shape, f32)
    following = [roll(value, -1, 0) for value in kept]
    for part in range(sources // 2):
        tile, first = divmod(part * SLOTS, LANES)
        value = None
        for axis_no in range(3):
            moved = jnp.where(lane >= first, kept[axis_no], following[axis_no])
            moved = roll(moved, SHARE * axis_no - first, 1)
            value = moved if axis_no == 0 else jnp.where(lane // SHARE >= axis_no, moved, value)
        for source, at in ((part, tile), (part + sources // 2, tile + tiles // 2)):
            back_ref[source, 0:1, :] = value[at : at + 1, :]
    for plane in range(PLANES):
        ats = [a * 32 + plane * 8 for a in range(3)]
        pops = [wide_ref[member, plane] for member in range(19)]
        speeds = [field_ref[at : at + 8, :] for at in ats]
        density = density_ref[plane]
        relax = relax_of(pops, density, speeds)
        results = relaxed(pops, density, speeds, relax, [total[at : at + 8, :] for at in ats])
        for member in range(19):
            post_ref[member, plane] = results[member]

    to_right, to_left = jnp.zeros((ROWS, LANES), f32), jnp.zeros((ROWS, LANES), f32)
    for plane in range(PLANES):
        for member in range(19):
            shift_x, shift_y, shift_z = velocity_table[member]
            source = (plane - shift_x) % PLANES
            value = post_ref[member, source]
            if shift_y == 1:
                edge = outer_ref[rising.index(member), source : source + 1, :]
                value = jnp.where(row == 0, edge, roll(value, 1, 0))
            if shift_y == -1:
                at = PLANES + source
                edge = outer_ref[falling.index(member), at : at + 1, :]
                value = jnp.where(row == ROWS - 1, edge, roll(value, -1, 0))
            if shift_z:
                value = roll(value, shift_z, 1)
            if shift_z == 1:
                place = ahead_z.index(member) * PLANES + plane
                to_right = jnp.where(lane == place, roll(value, place, 1), to_right)
            if shift_z == -1:
                place = back_z.index(member) * PLANES + plane
                to_left = jnp.where(lane == place, roll(value, place + 1, 1), to_left)
            if shift_y == 1:
                value = jnp.where(row == first_wall, post_ref[opposite[member], plane], value)
            if shift_y == -1:
                value = jnp.where(row == last_wall, post_ref[opposite[member], plane], value)
            moved_ref[member, plane] = value
    for target, face in ((left, to_left), (right, to_right)):
        early, late = jnp.zeros((ROWS, LANES), f32), jnp.zeros((ROWS, LANES), f32)
        for number in range(ROWS):
            early = jnp.where(row == number, roll(face, EARLY * number, 1), early)
            late = jnp.where(row == number, roll(face, LATE_FACE - EARLY + 4 * number, 1), late)
        early = jnp.where(lane // EARLY == row, early, 0.0)
        late = jnp.where((lane - LATE_FACE) // 4 == row, late, 0.0)
        late = jnp.where(lane >= LATE_FACE, late, 0.0)
        mine = jnp.where(iota((1, LANES), 1) < LATE_FACE, back_ref[target, 0:1, :], 0.0)
        back_ref[target, 0:1, :] = mine + jnp.sum(late, 0, keepdims=True)
        back_ref[target, 1:2, :] = jnp.sum(early, 0, keepdims=True)


def last_kernel(
    moved_ref, got_ref, owner_ref, rank_ref, pops_ref, force_ref
):
    left, right = z_neighbours()
    _, _, first_wall, last_wall = y_ends()
    lane = iota((ROWS, LANES), 1)
    row = iota((ROWS, LANES), 0)

    def face_of(source):
        late = jnp.broadcast_to(got_ref[source, 0:1, :], (ROWS, LANES))
        early = jnp.broadcast_to(got_ref[source, 1:2, :], (ROWS, LANES))
        face = jnp.zeros((ROWS, LANES), f32)
        for number in range(ROWS):
            value = roll(late, EARLY - LATE_FACE - 4 * number, 1)
            value = jnp.where(lane < EARLY, roll(early, -EARLY * number, 1), value)
            face = jnp.where(row == number, value, face)
        return face

    from_left, from_right = face_of(left), face_of(right)
    changed = [i for i in range(19) if velocity_table[i][2]]
    for member in range(19):
        if member not in changed:
            pops_ref[member] = moved_ref[member]
    for number, member in enumerate(changed):
        _, shift_y, shift_z = velocity_table[member]
        for plane in range(PLANES):
            if shift_z == 1:
                place = ahead_z.index(member) * PLANES + plane
                edge, here = roll(from_left, -place, 1), lane == 0
            else:
                place = back_z.index(member) * PLANES + plane
                edge, here = roll(from_right, LANES - 1 - place, 1), lane == LANES - 1
            if shift_y == 1:
                here = here & (row != first_wall)
            if shift_y == -1:
                here = here & (row != last_wall)
            pops_ref[member, plane] = jnp.where(here, edge, moved_ref[member, plane])
    owners, markers = got_ref.shape[0], owner_ref.shape[1]
    owner = owner_ref[...]
    spot = (iota((LANES, markers), 0).astype(f32) == rank_ref[...]).astype(bf16)
    rows = got_ref[:, 0, :]
    high, low = split_two(
        jnp.concatenate([roll(rows, -SHARE * axis_no, 1) for axis_no in range(3)], 0)
    )
    found = jnp.dot(
        jnp.concatenate([high, low], 1),
        jnp.concatenate([spot, spot], 0),
        preferred_element_type=f32,
    )
    hit = iota((owners, markers), 0) == owner
    for axis_no in range(3):
        value = jnp.where(hit, found[axis_no * owners : (axis_no + 1) * owners], 0.0)
        force_ref[axis_no : axis_no + 1, :] = jnp.sum(value, 0, keepdims=True) / ref_speed


def body(populations, marker_owner, marker_cell, marker_frac, marker_speed, marker_count):
    count_gy, count_gz = lax.axis_size("gy"), lax.axis_size("gz")
    markers = marker_owner.shape[0]
    vmem = pl.BlockSpec(memory_space=pltpu.VMEM)
    shape = jax.ShapeDtypeStruct
    tiles = shape((count_gz, 8, LANES), f32)
    field = shape((96, LANES), f32)
    cells = shape((PLANES, ROWS, LANES), f32)
    lattice = shape(populations.shape, f32)
    inputs = [
        marker_owner.reshape(1, markers),
        marker_cell,
        marker_frac,
        marker_speed,
        populations,
    ]
    send, rank, live, held, speeds, density, relax = call(
        first_kernel,
        [
            tiles,
            shape((1, markers), f32),
            shape((1, markers), jnp.int32),
            lattice,
            field,
            cells,
            cells,
        ],
        [marker_count.reshape(1, 1)]
        + [pltpu.with_memory_space_constraint(value, pltpu.HBM) for value in inputs],
        [vmem] + [pl.BlockSpec(memory_space=pltpu.HBM)] * 5,
        scratch=[pltpu.VMEM(value.shape, value.dtype) for value in inputs[0:4]]
        + [pltpu.SemaphoreType.DMA((5,))],
    )
    got = lax.all_to_all(send, "gz", split_axis=0, concat_axis=0, tiled=True)
    face = shape((FACE_ROWS, LANES), f32)
    next_pops, up, down, marks = call(
        second_kernel,
        [lattice, face, face, shape((MARK_ROWS, LANES), f32)],
        [held, got, speeds, density, relax],
        [vmem] * 5,
        scratch=[
            pltpu.VMEM(populations.shape, f32),
            pltpu.VMEM((24, ROWS, LANES), f32),
            pltpu.VMEM((24, ROWS, LANES), f32),
            pltpu.VMEM((96, LANES), f32),
        ],
    )
    below = lax.ppermute(up, "gy", [(i, i + 1) for i in range(count_gy - 1)])
    above = lax.ppermute(down, "gy", [(i + 1, i) for i in range(count_gy - 1)])
    moved, back = call(
        third_kernel,
        [lattice, shape((count_gz, 2, LANES), f32)],
        [next_pops, up, down, marks, below, above],
        [vmem] * 6,
        scratch=[
            pltpu.VMEM(populations.shape, f32),
            pltpu.VMEM((96, LANES), f32),
            pltpu.VMEM((PLANES, ROWS, LANES), f32),
            pltpu.VMEM(populations.shape, f32),
            pltpu.VMEM((5, ROWS, LANES), f32),
        ],
    )
    back = lax.all_to_all(back, "gz", split_axis=0, concat_axis=0, tiled=True)
    pops, force = call(
        last_kernel,
        [lattice, shape((3, markers), f32)],
        [moved, back, live, rank],
        [vmem] * 4,
    )
    return pops, force


def solution(mesh):
    return jax.shard_map(
        body,
        mesh=mesh,
        in_specs=(
            P(None, None, "gy", "gz"),
            P(("gy", "gz"), None),
            P(None, ("gy", "gz")),
            P(None, ("gy", "gz")),
            P(None, ("gy", "gz")),
            P(("gy", "gz")),
        ),
        out_specs=(P(None, None, "gy", "gz"), P(None, ("gy", "gz"))),
        check_vma=False,
    )
```

```python
import math

import jax
import jax.numpy as jnp
from jax import lax
from jax.experimental import pallas as pl
from jax.experimental.pallas import tpu as pltpu
from jax.sharding import PartitionSpec as P

INTERPRET = False

velocity_table = (
    (0, 0, 0),
    (1, 0, 0),
    (-1, 0, 0),
    (0, 1, 0),
    (0, -1, 0),
    (0, 0, 1),
    (0, 0, -1),
    (1, 1, 0),
    (-1, -1, 0),
    (1, -1, 0),
    (-1, 1, 0),
    (1, 0, 1),
    (-1, 0, -1),
    (1, 0, -1),
    (-1, 0, 1),
    (0, 1, 1),
    (0, -1, -1),
    (0, 1, -1),
    (0, -1, 1),
)
opposite = (0, 2, 1, 4, 3, 6, 5, 8, 7, 10, 9, 12, 11, 14, 13, 16, 15, 18, 17)
rising = tuple(i for i in range(19) if velocity_table[i][1] == 1)
falling = tuple(opposite[i] for i in rising)
level = tuple(i for i in range(19) if velocity_table[i][1] == 0)
ahead_z = tuple(i for i in range(19) if velocity_table[i][2] == 1)
back_z = tuple(opposite[i] for i in ahead_z)
tau_base = 0.52
smag_const = 0.17
ref_speed = 0.05

PLANES = 4
ROWS = 8
LANES = 128
SLOTS = 24
SHARE = 32
FEW = 4
SPARE = SLOTS - FEW
FIRST_SPARE = SHARE
FIRST_Z = SHARE + 2 * SPARE
FIRST_RIM = 76
LATE_FACE = 3 * SHARE
EARLY = 16
RIM_WORDS = 13
AT_SPEED, AT_SUMS, AT_POPS, AT_NEXT, AT_MARKS, FACE_ROWS = 0, 12, 36, 56, 80, 128
AT_Z, MARK_ROWS = 48, 56

f32 = jnp.float32
bf16 = jnp.bfloat16


def iota(shape, dim):
    return lax.broadcasted_iota(jnp.int32, shape, dim)


def roll(value, shift, axis):
    shift = shift % value.shape[axis]
    return pltpu.roll(value, shift, axis) if shift else value


def split_two(value):
    high = value.astype(bf16)
    return high, (value - high.astype(f32)).astype(bf16)


def call(kernel, out_shape, args, in_specs, scratch=(), out_specs=None, aliases=()):
    vmem = pl.BlockSpec(memory_space=pltpu.VMEM)
    return pl.pallas_call(
        kernel,
        out_shape=out_shape,
        in_specs=in_specs,
        out_specs=out_specs or [vmem] * len(out_shape),
        input_output_aliases=dict(aliases),
        scratch_shapes=list(scratch),
        compiler_params=pltpu.CompilerParams(vmem_limit_bytes=32 * 1024 * 1024),
        interpret=INTERPRET,
    )(*args)


def z_neighbours():
    column, size = lax.axis_index("gz"), lax.axis_size("gz")
    return (column + size - 1) % size, (column + 1) % size


def y_ends():
    place, size = lax.axis_index("gy"), lax.axis_size("gy")
    first, last = place == 0, place == size - 1
    return (
        jnp.where(first, -1, 0),
        jnp.where(last, -1, ROWS - 1),
        jnp.where(first, 0, -1),
        jnp.where(last, ROWS - 1, -1),
    )


def moments_of(pops):
    density = pops[0]
    for member in range(1, 19):
        density = density + pops[member]
    parts = []
    for axis_no in range(3):
        total = None
        for member in range(19):
            if velocity_table[member][axis_no] == 1:
                total = pops[member] if total is None else total + pops[member]
        for member in range(19):
            if velocity_table[member][axis_no] == -1:
                total = total - pops[member]
        parts.append(total)
    inverse = 1.0 / density
    return density, [part * inverse for part in parts]


def relax_of(pops, density, speeds):
    factor = 18.0 * math.sqrt(2.0) * smag_const * smag_const
    moved = [density * part for part in speeds]
    pair = [pops[2 * k + 1] + pops[2 * k + 2] for k in range(9)]
    third = density * (1.0 / 3.0)
    xx = pair[0] + pair[3] + pair[4] + pair[5] + pair[6] - third - moved[0] * speeds[0]
    yy = pair[1] + pair[3] + pair[4] + pair[7] + pair[8] - third - moved[1] * speeds[1]
    zz = pair[2] + pair[5] + pair[6] + pair[7] + pair[8] - third - moved[2] * speeds[2]
    xy = pair[3] - pair[4] - moved[0] * speeds[1]
    xz = pair[5] - pair[6] - moved[0] * speeds[2]
    yz = pair[7] - pair[8] - moved[1] * speeds[2]
    norm_sq = xx * xx + yy * yy + zz * zz + 2.0 * (xy * xy + xz * xz + yz * yz)
    return 0.5 * (tau_base + jnp.sqrt(tau_base * tau_base + factor * jnp.sqrt(norm_sq) * (1.0 / density)))


def along_of(member, speeds):
    total = None
    for axis_no in range(3):
        if velocity_table[member][axis_no] == 1:
            total = speeds[axis_no] if total is None else total + speeds[axis_no]
    for axis_no in range(3):
        if velocity_table[member][axis_no] == -1:
            total = total - speeds[axis_no]
    return total


def relaxed(pops, density, speeds, relax, pulls):
    pull = relax * (1.0 / density)
    shifted = [speeds[a] + pull * pulls[a] for a in range(3)]
    shifted_sq = shifted[0] * shifted[0] + shifted[1] * shifted[1] + shifted[2] * shifted[2]
    rate = 1.0 / relax
    keep = 1.0 - rate
    scale = rate * density
    base = scale * (1.0 - 1.5 * shifted_sq)
    quad = 4.5 * scale
    results = [keep * pops[0] + base * (1.0 / 3.0)]
    for pair in range(9):
        plus = 2 * pair + 1
        along = along_of(plus, shifted)
        weight = 1.0 / 18.0 if pair < 3 else 1.0 / 36.0
        even = weight * (base + quad * along * along)
        odd = (3.0 * weight) * (scale * along)
        results.append(keep * pops[plus] + (even + odd))
        results.append(keep * pops[plus + 1] + (even - odd))
    return results


def along_x(mark, plane):
    base, frac = mark[0:1, :], mark[2:3, :]
    following = jnp.where(base == float(PLANES), 0.0, base)
    weight = jnp.where(base - 1.0 == plane, 1.0 - frac, 0.0)
    return jnp.where((base > 0.5) & (following == plane), frac, weight)


def block_weights(mark):
    base, frac = mark[1:2, :], mark[3:4, :]
    row = iota((ROWS, mark.shape[1]), 0).astype(f32)
    along_y = jnp.where(row == base, 1.0 - frac, jnp.where(row == base + 1.0, frac, 0.0))
    return [along_y * along_x(mark, float(plane)) for plane in range(PLANES)]


def spots(base_z):
    count = base_z.shape[1]
    one, none = jnp.ones((), bf16), jnp.zeros((), bf16)
    return jnp.where(iota((LANES, count), 0).astype(bf16) == base_z.astype(bf16), one, none)


def pairs_of(field):
    high, low = split_two(field)
    next_high, next_low = split_two(roll(field, -1, 1))
    return jnp.concatenate(
        [jnp.concatenate([high, low], 1), jnp.concatenate([next_high, next_low], 1)], 0
    )


def gathered(pairs, spot):
    return jnp.dot(pairs, jnp.concatenate([spot, spot], 0), preferred_element_type=f32)


def sums_of(here, there, spot):
    size = here.shape[0]
    high, low = split_two(here)
    next_high, next_low = split_two(there)
    sums = lax.dot_general(
        jnp.concatenate([high, low, next_high, next_low], 0),
        spot,
        (((1,), (1,)), ((), ())),
        preferred_element_type=f32,
    )
    first = sums[0:size] + sums[size : 2 * size]
    second = sums[2 * size : 3 * size] + sums[3 * size :]
    return first, second


def scattered(here, there, spot):
    first, second = sums_of(here, there, spot)
    return first + roll(second, 1, 1)


def forces_of(mark, weights, here, there):
    frac = mark[4:5, :]
    forces, spreads = [], []
    for axis_no in range(3):
        total = None
        for plane in range(PLANES):
            at = axis_no * PLANES + plane
            value = weights[plane] * (here[at] + frac * (there[at] - here[at]))
            total = value if total is None else total + value
        force = mark[5 + axis_no : 6 + axis_no, :] - jnp.sum(total, 0, keepdims=True)
        forces.append(force)
        for plane in range(PLANES):
            spreads.append(weights[plane] * force)
    return forces, spreads


def first_kernel(
    count_ref, owner_hbm, cell_hbm, frac_hbm, speed_hbm, pops_hbm,
    send_ref, rank_ref, live_ref, pops_ref, field_ref, density_ref, relax_ref,
    owner_ref, cell_ref, frac_ref, speed_ref, sems,
):
    copies = [
        pltpu.make_async_copy(source, target, sems.at[number])
        for number, (source, target) in enumerate(
            [
                (owner_hbm, owner_ref),
                (cell_hbm, cell_ref),
                (frac_hbm, frac_ref),
                (speed_hbm, speed_ref),
                (pops_hbm, pops_ref),
            ]
        )
    ]
    for copy in copies:
        copy.start()
    for copy in copies[0:4]:
        copy.wait()
    owners, markers = send_ref.shape[0], owner_ref.shape[1]
    live = iota((1, markers), 1) < count_ref[...]
    owner = jnp.where(live, owner_ref[...], -1)
    live_ref[...] = owner
    base_z = cell_ref[2:3, :]
    upper, lower = base_z == LANES - 2, base_z == 0
    twin = jnp.where(
        upper,
        jnp.where(owner == owners - 1, 0, owner + 1),
        jnp.where(owner == 0, owners - 1, owner - 1),
    )
    twin = jnp.where(live & (upper | lower), twin, -1)
    hit = iota((owners, markers), 0) == owner
    hits = jnp.concatenate(
        [hit.astype(f32), (hit & upper).astype(f32), (hit & lower).astype(f32)], 0
    )
    blocks = markers // LANES
    parts = [hits[:, block * LANES : (block + 1) * LANES] for block in range(blocks)]
    earlier = iota((LANES, 2 * LANES), 0) < iota((LANES, 2 * LANES), 1)
    counts = jnp.dot(
        jnp.concatenate(parts, 0).astype(bf16), earlier.astype(bf16), preferred_element_type=f32
    )
    before = None
    ranks = [[], [], []]
    for block in range(blocks):
        inner = counts[block * 3 * owners : (block + 1) * 3 * owners]
        place = inner[:, 0:LANES] if before is None else inner[:, 0:LANES] + before
        before = inner[:, LANES:] if before is None else inner[:, LANES:] + before
        picked = parts[block] * place
        for kind in range(3):
            ranks[kind].append(
                jnp.sum(picked[kind * owners : (kind + 1) * owners], 0, keepdims=True)
            )
    rank, rank_up, rank_low = [jnp.concatenate(kind, 1) for kind in ranks]
    rank_ref[...] = rank
    copies[4].wait()
    lane_up = jnp.where(rank_up < FEW, SLOTS + rank_up, FIRST_SPARE - FEW + rank_up)
    lane_low = jnp.where(
        rank_low < FEW, SLOTS + FEW + rank_low, FIRST_SPARE + SPARE - FEW + rank_low
    )
    lane_twin = jnp.where(upper, lane_up, lane_low)
    lane_z = FIRST_Z + jnp.where(rank >= 16.0, 2.0, jnp.where(rank >= 8.0, 1.0, 0.0))
    slot_z = rank - 8.0 * (lane_z - FIRST_Z)
    lane = iota((LANES, markers), 0).astype(f32)
    spot_own = (lane == rank).astype(bf16)
    spot_twin = (lane == lane_twin).astype(bf16)
    spot_z = (lane == lane_z).astype(bf16)
    row = iota((8, markers), 0)
    words = jnp.where(row == 0, cell_ref[0:1, :] + 1, cell_ref[1:2, :]).astype(f32)
    for number in range(3):
        words = jnp.where(row == 2 + number, frac_ref[number : number + 1, :], words)
        words = jnp.where(row == 5 + number, speed_ref[number : number + 1, :], words)
    high, low = split_two(words)
    high, low = high.astype(f32), low.astype(f32)
    words_z = jnp.where(row.astype(f32) == slot_z, base_z.astype(f32), 0.0)

    def to_owners(value, target):
        value = jnp.concatenate([value, value], 0).astype(bf16)
        target = jnp.broadcast_to(target.astype(f32), (16, markers)).astype(bf16)
        first = jnp.where(iota((16, markers), 0) < 8, 0.0, 1.0).astype(bf16)
        rows = []
        for number in range(0, owners, 2):
            rows.append(jnp.where(target == first + float(number), value, jnp.zeros((), bf16)))
        return jnp.concatenate(rows, 0)

    def placed(left, spot):
        return lax.dot_general(left, spot, (((1,), (1,)), ((), ())), preferred_element_type=f32)

    tiles = placed(to_owners(high, owner), spot_own) + placed(to_owners(low, owner), spot_own)
    tiles = tiles + placed(to_owners(high, twin), spot_twin)
    tiles = tiles + placed(to_owners(low, twin), spot_twin)
    tiles = tiles + placed(to_owners(words_z, owner), spot_z)
    send_ref[...] = tiles.reshape(owners, 8, LANES)


    lane = iota((ROWS, LANES), 1)
    to_right, to_left = jnp.zeros((ROWS, LANES), f32), jnp.zeros((ROWS, LANES), f32)
    for plane in range(PLANES):
        pops = [pops_ref[member, plane] for member in range(19)]
        density, speeds = moments_of(pops)
        relax = relax_of(pops, density, speeds)
        density_ref[plane] = density
        relax_ref[plane] = relax
        for axis_no in range(3):
            at = axis_no * 32 + plane * 8
            field_ref[at : at + 8, :] = speeds[axis_no]
        common = [density, *speeds, relax]
        for word in range(RIM_WORDS):
            place = FIRST_RIM + word * PLANES + plane
            if word < 5:
                right, left, shift = common[word], common[word], 0
            elif word < 10:
                right, left, shift = pops[ahead_z[word - 5]], pops[back_z[word - 5]], 0
            else:
                right, left, shift = speeds[word - 10], speeds[word - 10], 1
            here = lane == place
            to_right = jnp.where(here, roll(right, place - (LANES - 1) + shift, 1), to_right)
            to_left = jnp.where(here, roll(left, place - shift, 1), to_left)
    left, right = z_neighbours()
    send_ref[left] = send_ref[left] + to_left
    send_ref[right] = send_ref[right] + to_right


def second_kernel(
    pops_ref, got_ref, field_ref, density_ref, relax_ref,
    next_ref, up_ref, down_ref, marks_ref,
    post_ref, near_ref, far_ref, twin_ref,
):
    left, right = z_neighbours()
    lane = iota((ROWS, LANES), 1)
    row = iota((ROWS, LANES), 0)
    sources = got_ref.shape[0]

    tiles = sources * SLOTS // LANES
    marks = [None] * tiles
    twin_marks = [None] * (sources * 2 * FEW // LANES)
    for source in range(sources):
        tile, first = divmod(source * SLOTS, LANES)
        words = roll(got_ref[source], first, 1)
        marks[tile] = words if marks[tile] is None else jnp.where(lane >= first, words, marks[tile])
        if first + SLOTS > LANES:
            marks[tile + 1] = words
        tile, first = divmod(source * 2 * FEW, LANES)
        words = roll(got_ref[source], first - SLOTS, 1)
        old = twin_marks[tile]
        twin_marks[tile] = words if old is None else jnp.where(lane >= first, words, old)
    bases = []
    for tile in range(tiles):
        first, last = tile * LANES // SLOTS, ((tile + 1) * LANES - 1) // SLOTS
        rows = jnp.concatenate([got_ref[source] for source in range(first, last + 1)], 0)

        def slot_of(shape):
            member = iota(shape, 1) + tile * LANES
            source = (member * 2731) >> 16
            return source, member - SLOTS * source

        _, slot = slot_of((LANES, LANES))
        chosen = (iota((LANES, LANES), 0) == FIRST_Z + (slot >> 3)).astype(bf16)
        value = jnp.dot(rows.astype(bf16), chosen, preferred_element_type=f32)
        source, slot = slot_of(value.shape)
        here = iota(value.shape, 0) == (source - first) * 8 + (slot & 7)
        bases.append(jnp.sum(jnp.where(here, value, 0.0), 0, keepdims=True))
    for tile in range(tiles):
        marks_ref[tile * 8 : tile * 8 + 8, :] = marks[tile]
        marks_ref[AT_Z + tile : AT_Z + tile + 1, :] = bases[tile]
        for ref, base_y in ((up_ref, float(ROWS - 2)), (down_ref, 0.0)):
            words = jnp.where((row == 0) & (marks[tile][1:2, :] != base_y), 0.0, marks[tile])
            words = jnp.where(row == 1, bases[tile], words)
            ref[AT_MARKS + tile * 8 : AT_MARKS + tile * 8 + 8, :] = words
    for ref in (up_ref, down_ref):
        ref[AT_NEXT + 20 : AT_MARKS, :] = jnp.zeros((AT_MARKS - AT_NEXT - 20, LANES), f32)

    ends = jnp.where(lane >= FIRST_RIM, got_ref[left], roll(got_ref[right], 64, 1))
    rim = [roll(ends, -(FIRST_RIM + PLANES * word), 1) for word in range(RIM_WORDS)]

    def spread_lane(value, at):
        return jnp.broadcast_to(value[:, at : at + 1], (ROWS, LANES))

    for axis_no in range(3):
        for plane in range(PLANES):
            at = axis_no * PLANES + plane
            near_ref[at] = spread_lane(rim[10 + axis_no], plane)
            near_ref[12 + at] = spread_lane(rim[1 + axis_no], 64 + plane)
            far_ref[at] = spread_lane(rim[1 + axis_no], plane)
            far_ref[12 + at] = spread_lane(rim[10 + axis_no], 64 + plane)

    def twins(of_left, of_right):
        def both(ref):
            return [
                jnp.where(of_left, ref[at], jnp.where(of_right, ref[12 + at], 0.0))
                for at in range(12)
            ]

        return both(near_ref), both(far_ref)

    def sides(lefts, rights, count):
        place, member = iota((LANES, count), 0), iota((LANES, count), 1)
        chosen = jnp.where(place < 64, lefts(member).astype(f32), rights(member).astype(f32))
        return chosen.astype(bf16)

    near, far = twins(lane % (2 * FEW) < FEW, lane % (2 * FEW) >= FEW)
    side = sides(
        lambda member: member % (2 * FEW) < FEW,
        lambda member: member % (2 * FEW) >= FEW,
        2 * LANES,
    )
    rim_left = iota((96, LANES), 1) < 64
    pairs = pairs_of(field_ref[...])
    force = jnp.zeros((96, LANES), f32)
    for block in range(tiles // 2):
        mark = jnp.concatenate(marks[2 * block : 2 * block + 2], 1)
        spot = spots(jnp.concatenate(bases[2 * block : 2 * block + 2], 1))
        found = gathered(pairs, spot)
        _, spreads = forces_of(
            mark,
            block_weights(mark),
            [found[at * 8 : at * 8 + 8] for at in range(12)],
            [found[96 + at * 8 : 104 + at * 8] for at in range(12)],
        )
        spreads = jnp.concatenate(spreads, 0)
        ahead = spreads * mark[4:5, :]
        force = force + scattered(spreads - ahead, ahead, spot)
    mark = jnp.concatenate(twin_marks, 1)
    _, spreads = forces_of(
        mark,
        block_weights(mark),
        [jnp.concatenate([value] * 2, 1) for value in near],
        [jnp.concatenate([value] * 2, 1) for value in far],
    )
    spreads = jnp.concatenate(spreads, 0)
    ahead = spreads * mark[4:5, :]
    first, second = sums_of(spreads - ahead, ahead, side)
    twin_ref[...] = jnp.where(rim_left, second, first)

    further = jnp.where((lane >= FIRST_SPARE) & (lane < FIRST_Z), 1.0, 0.0)
    most = got_ref[0]
    for source in range(1, sources):
        most = jnp.maximum(most, got_ref[source])

    @pl.when(jnp.max(most * further) > 0.5)
    def _():
        near, far = twins(lane < SPARE, lane >= SPARE)
        side = sides(lambda member: member < SPARE, lambda member: member >= SPARE, LANES)

        def one(source, carry):
            mark = roll(got_ref[source], -FIRST_SPARE, 1)
            mark = jnp.where(lane < 2 * SPARE, mark, 0.0)
            _, spreads = forces_of(mark, block_weights(mark), near, far)
            spreads = jnp.concatenate(spreads, 0)
            ahead = spreads * mark[4:5, :]
            first, second = sums_of(spreads - ahead, ahead, side)
            twin_ref[...] = twin_ref[...] + jnp.where(rim_left, second, first)
            return carry

        lax.fori_loop(0, sources, one, 0)

    sums = twin_ref[...]
    pulls = []
    for axis_no in range(3):
        total = None
        for plane in range(PLANES):
            at = axis_no * 32 + plane * 8
            value = sums[at : at + 8, :]
            total = value if total is None else jnp.where(lane % PLANES == plane, value, total)
        pulls.append(total)
    density, speeds, relax = rim[0], rim[1:4], rim[4]
    pull = relax / density
    shifted = [speeds[a] + pull * pulls[a] for a in range(3)]
    shifted_sq = shifted[0] * shifted[0] + shifted[1] * shifted[1] + shifted[2] * shifted[2]
    rate = 1.0 / relax
    sign = jnp.where(lane < 64, 1.0, -1.0)
    rim_post = []
    for number, member in enumerate(ahead_z):
        along = sign * along_of(member, shifted)
        weight = 1.0 / 18.0 if number == 0 else 1.0 / 36.0
        target = weight * density * (1.0 + 3.0 * along + 4.5 * along * along - 1.5 * shifted_sq)
        rim_post.append((1.0 - rate) * rim[5 + number] + rate * target)

    for plane in range(PLANES):
        ats = [a * 32 + plane * 8 for a in range(3)]
        results = relaxed(
            [pops_ref[member, plane] for member in range(19)],
            density_ref[plane],
            [field_ref[at : at + 8, :] for at in ats],
            relax_ref[plane],
            [force[at : at + 8, :] for at in ats],
        )
        for member in range(19):
            post_ref[member, plane] = results[member]

    for plane in range(PLANES):
        pops = []
        for member in range(19):
            shift_x, shift_y, shift_z = velocity_table[member]
            source = (plane - shift_x) % PLANES
            value = post_ref[member, source]
            if shift_z == 1:
                edge = roll(rim_post[ahead_z.index(member)], -source, 1)
                value = jnp.where(lane == 0, edge, roll(value, 1, 1))
            if shift_z == -1:
                edge = roll(rim_post[back_z.index(member)], 63 - source, 1)
                value = jnp.where(lane == LANES - 1, edge, roll(value, -1, 1))
            if shift_y == 1:
                at = AT_NEXT + rising.index(member) * PLANES + plane
                up_ref[at : at + 1, :] = value[ROWS - 1 : ROWS, :]
                value = jnp.where(row == 0, post_ref[opposite[member], plane], roll(value, 1, 0))
            if shift_y == -1:
                at = AT_NEXT + falling.index(member) * PLANES + plane
                down_ref[at : at + 1, :] = value[0:1, :]
                value = jnp.where(
                    row == ROWS - 1, post_ref[opposite[member], plane], roll(value, -1, 0)
                )
            next_ref[member, plane] = value
            pops.append(value)
        _, speeds = moments_of(pops)
        for axis_no in range(3):
            at = AT_SPEED + axis_no * PLANES + plane
            up_ref[at : at + 1, :] = speeds[axis_no][ROWS - 2 : ROWS - 1, :]
            down_ref[at : at + 1, :] = speeds[axis_no][1:2, :]
        cross = pops[11] + pops[12]
        other = pops[13] + pops[14]
        across, along = pops[1] + pops[2], pops[5] + pops[6]
        lean = pops[11] - pops[12]
        tilt = pops[13] - pops[14]
        sums = [
            pops[0] + across + along + cross + other,
            pops[1] - pops[2] + lean + tilt,
            pops[5] - pops[6] + lean - tilt,
            across + cross + other,
            along + cross + other,
            cross - other,
        ]
        for number, value in enumerate(sums):
            at = AT_SUMS + number * PLANES + plane
            up_ref[at : at + 1, :] = value[ROWS - 1 : ROWS, :]
            down_ref[at : at + 1, :] = value[0:1, :]
        for number in range(5):
            at = AT_POPS + number * PLANES + plane
            up_ref[at : at + 1, :] = pops[rising[number]][ROWS - 1 : ROWS, :]
            down_ref[at : at + 1, :] = pops[falling[number]][0:1, :]


def third_kernel(
    next_ref, up_ref, down_ref, marks_ref, below_ref, above_ref,
    moved_ref, back_ref,
    wide_ref, field_ref, density_ref, post_ref, outer_ref,
):
    left, right = z_neighbours()
    first_open, last_open, first_wall, last_wall = y_ends()
    lane = iota((ROWS, LANES), 1)
    row = iota((ROWS, LANES), 0)
    sources = back_ref.shape[0]
    tiles = sources * SLOTS // LANES

    def four(ref, at):
        return ref[at : at + PLANES, :]

    for plane in range(PLANES):
        pops = []
        for member in range(19):
            value = next_ref[member, plane]
            if member in rising:
                at = AT_NEXT + rising.index(member) * PLANES + plane
                value = jnp.where(row == first_open, below_ref[at : at + 1, :], value)
            if member in falling:
                at = AT_NEXT + falling.index(member) * PLANES + plane
                value = jnp.where(row == last_open, above_ref[at : at + 1, :], value)
            wide_ref[member, plane] = value
            pops.append(value)
        density, speeds = moments_of(pops)
        density_ref[plane] = density
        for axis_no in range(3):
            at = axis_no * 32 + plane * 8
            field_ref[at : at + 8, :] = speeds[axis_no]

    outside = ((row < PLANES) & (first_wall == 0)) | ((row >= PLANES) & (last_wall > 0))
    sums = []
    for number in range(6):
        at = AT_SUMS + number * PLANES
        sums.append(jnp.concatenate([four(below_ref, at), four(above_ref, at)], 0))
    half_x, half_z = 0.5 * (sums[3] - sums[5]), 0.5 * (sums[4] - sums[5])
    nothing = jnp.zeros((ROWS, LANES), f32)
    outer = [nothing] * 19
    outer[0] = sums[0] - sums[3] - sums[4] + sums[5]
    outer[1], outer[2] = half_x + 0.5 * sums[1], half_x - 0.5 * sums[1]
    outer[5], outer[6] = half_z + 0.5 * sums[2], half_z - 0.5 * sums[2]
    outer[11] = outer[12] = 0.5 * sums[5]
    for number in range(5):
        known, mine = AT_POPS + number * PLANES, AT_NEXT + number * PLANES
        outer[rising[number]] = jnp.concatenate([four(below_ref, known), four(up_ref, mine)], 0)
        outer[falling[number]] = jnp.concatenate([four(down_ref, mine), four(above_ref, known)], 0)
    outer = [
        jnp.where(outside, 0.0 if member else 1.0, value) for member, value in enumerate(outer)
    ]
    outer_density, outer_speeds = moments_of(outer)
    lows, tops = [], []
    for axis_no in range(3):
        at = AT_SPEED + axis_no * PLANES
        second = jnp.concatenate([four(above_ref, at), four(below_ref, at)], 0)
        lows.append(jnp.where(row < PLANES, outer_speeds[axis_no], second))
        tops.append(jnp.where(row < PLANES, second, outer_speeds[axis_no]))

    def beyond(ref, field):
        pairs = pairs_of(jnp.concatenate(field, 0))
        total = jnp.zeros((24, LANES), f32)
        for block in range(tiles // 2):
            tile = AT_MARKS + 16 * block
            mark = jnp.concatenate([ref[tile : tile + 8, :], ref[tile + 8 : tile + 16, :]], 1)
            spot = spots(mark[1:2, :])
            found = gathered(pairs, spot)
            place = iota((ROWS, 2 * LANES), 0)
            frac = mark[3:4, :]
            weight = along_x(mark, (place % PLANES).astype(f32))
            weight = weight * jnp.where(place < PLANES, frac, 1.0 - frac)
            frac = mark[4:5, :]
            spreads = []
            for axis_no in range(3):
                here = found[axis_no * 8 : axis_no * 8 + 8]
                there = found[24 + axis_no * 8 : 32 + axis_no * 8]
                value = weight * (here + frac * (there - here))
                force = mark[5 + axis_no : 6 + axis_no, :] - jnp.sum(value, 0, keepdims=True)
                spreads.append(weight * force)
            spreads = jnp.concatenate(spreads, 0)
            ahead = spreads * frac
            total = total + scattered(spreads - ahead, ahead, spot)
        return total

    from_below = beyond(below_ref, lows)
    from_above = beyond(above_ref, tops)
    outer_pulls = [
        jnp.where(row < PLANES, from_below[a * 8 : a * 8 + 8], from_above[a * 8 : a * 8 + 8])
        for a in range(3)
    ]
    relax = relax_of(outer, outer_density, outer_speeds)
    outer_post = relaxed(outer, outer_density, outer_speeds, relax, outer_pulls)
    for number in range(5):
        outer_ref[number] = jnp.where(
            row < PLANES, outer_post[rising[number]], outer_post[falling[number]]
        )

    pairs = pairs_of(field_ref[...])
    total = jnp.zeros((96, LANES), f32)
    kept = [jnp.zeros((ROWS, LANES), f32) for axis_no in range(3)]
    for block in range(tiles // 2):
        tile = 16 * block
        mark = jnp.concatenate([marks_ref[tile : tile + 8, :], marks_ref[tile + 8 : tile + 16, :]], 1)
        at = AT_Z + 2 * block
        spot = spots(jnp.concatenate([marks_ref[at : at + 1, :], marks_ref[at + 1 : at + 2, :]], 1))
        found = gathered(pairs, spot)
        forces, spreads = forces_of(
            mark,
            block_weights(mark),
            [found[at * 8 : at * 8 + 8] for at in range(12)],
            [found[96 + at * 8 : 104 + at * 8] for at in range(12)],
        )
        spreads = jnp.concatenate(spreads, 0)
        ahead = spreads * mark[4:5, :]
        total = total + scattered(spreads - ahead, ahead, spot)
        for half in range(2):
            lanes = slice(half * LANES, (half + 1) * LANES)
            for axis_no in range(3):
                kept[axis_no] = jnp.where(
                    row == 2 * block + half, forces[axis_no][:, lanes], kept[axis_no]
                )
    back_ref[...] = jnp.zeros(back_ref.shape, f32)
    following = [roll(value, -1, 0) for value in kept]
    for part in range(sources // 2):
        tile, first = divmod(part * SLOTS, LANES)
        value = None
        for axis_no in range(3):
            moved = jnp.where(lane >= first, kept[axis_no], following[axis_no])
            moved = roll(moved, SHARE * axis_no - first, 1)
            value = moved if axis_no == 0 else jnp.where(lane // SHARE >= axis_no, moved, value)
        for source, at in ((part, tile), (part + sources // 2, tile + tiles // 2)):
            back_ref[source, 0:1, :] = value[at : at + 1, :]
    for plane in range(PLANES):
        ats = [a * 32 + plane * 8 for a in range(3)]
        pops = [wide_ref[member, plane] for member in range(19)]
        speeds = [field_ref[at : at + 8, :] for at in ats]
        density = density_ref[plane]
        relax = relax_of(pops, density, speeds)
        results = relaxed(pops, density, speeds, relax, [total[at : at + 8, :] for at in ats])
        for member in range(19):
            post_ref[member, plane] = results[member]

    to_right, to_left = jnp.zeros((ROWS, LANES), f32), jnp.zeros((ROWS, LANES), f32)
    for plane in range(PLANES):
        for member in range(19):
            shift_x, shift_y, shift_z = velocity_table[member]
            source = (plane - shift_x) % PLANES
            value = post_ref[member, source]
            if shift_y == 1:
                edge = outer_ref[rising.index(member), source : source + 1, :]
                value = jnp.where(row == 0, edge, roll(value, 1, 0))
            if shift_y == -1:
                at = PLANES + source
                edge = outer_ref[falling.index(member), at : at + 1, :]
                value = jnp.where(row == ROWS - 1, edge, roll(value, -1, 0))
            if shift_z:
                value = roll(value, shift_z, 1)
            if shift_z == 1:
                place = ahead_z.index(member) * PLANES + plane
                to_right = jnp.where(lane == place, roll(value, place, 1), to_right)
            if shift_z == -1:
                place = back_z.index(member) * PLANES + plane
                to_left = jnp.where(lane == place, roll(value, place + 1, 1), to_left)
            if shift_y == 1:
                value = jnp.where(row == first_wall, post_ref[opposite[member], plane], value)
            if shift_y == -1:
                value = jnp.where(row == last_wall, post_ref[opposite[member], plane], value)
            moved_ref[member, plane] = value
    for target, face in ((left, to_left), (right, to_right)):
        early, late = jnp.zeros((ROWS, LANES), f32), jnp.zeros((ROWS, LANES), f32)
        for number in range(ROWS):
            early = jnp.where(row == number, roll(face, EARLY * number, 1), early)
            late = jnp.where(row == number, roll(face, LATE_FACE - EARLY + 4 * number, 1), late)
        early = jnp.where(lane // EARLY == row, early, 0.0)
        late = jnp.where((lane - LATE_FACE) // 4 == row, late, 0.0)
        late = jnp.where(lane >= LATE_FACE, late, 0.0)
        mine = jnp.where(iota((1, LANES), 1) < LATE_FACE, back_ref[target, 0:1, :], 0.0)
        back_ref[target, 0:1, :] = mine + jnp.sum(late, 0, keepdims=True)
        back_ref[target, 1:2, :] = jnp.sum(early, 0, keepdims=True)


def last_kernel(
    moved_ref, got_ref, owner_ref, rank_ref, pops_ref, force_ref
):
    left, right = z_neighbours()
    _, _, first_wall, last_wall = y_ends()
    lane = iota((ROWS, LANES), 1)
    row = iota((ROWS, LANES), 0)

    def face_of(source):
        late = jnp.broadcast_to(got_ref[source, 0:1, :], (ROWS, LANES))
        early = jnp.broadcast_to(got_ref[source, 1:2, :], (ROWS, LANES))
        face = jnp.zeros((ROWS, LANES), f32)
        for number in range(ROWS):
            value = roll(late, EARLY - LATE_FACE - 4 * number, 1)
            value = jnp.where(lane < EARLY, roll(early, -EARLY * number, 1), value)
            face = jnp.where(row == number, value, face)
        return face

    from_left, from_right = face_of(left), face_of(right)
    changed = [i for i in range(19) if velocity_table[i][2]]
    for member in range(19):
        if member not in changed:
            pops_ref[member] = moved_ref[member]
    for number, member in enumerate(changed):
        _, shift_y, shift_z = velocity_table[member]
        for plane in range(PLANES):
            if shift_z == 1:
                place = ahead_z.index(member) * PLANES + plane
                edge, here = roll(from_left, -place, 1), lane == 0
            else:
                place = back_z.index(member) * PLANES + plane
                edge, here = roll(from_right, LANES - 1 - place, 1), lane == LANES - 1
            if shift_y == 1:
                here = here & (row != first_wall)
            if shift_y == -1:
                here = here & (row != last_wall)
            pops_ref[member, plane] = jnp.where(here, edge, moved_ref[member, plane])
    owners, markers = got_ref.shape[0], owner_ref.shape[1]
    owner = owner_ref[...]
    spot = (iota((LANES, markers), 0).astype(f32) == rank_ref[...]).astype(bf16)
    rows = got_ref[:, 0, :]
    high, low = split_two(
        jnp.concatenate([roll(rows, -SHARE * axis_no, 1) for axis_no in range(3)], 0)
    )
    found = jnp.dot(
        jnp.concatenate([high, low], 1),
        jnp.concatenate([spot, spot], 0),
        preferred_element_type=f32,
    )
    hit = iota((owners, markers), 0) == owner
    for axis_no in range(3):
        value = jnp.where(hit, found[axis_no * owners : (axis_no + 1) * owners], 0.0)
        force_ref[axis_no : axis_no + 1, :] = jnp.sum(value, 0, keepdims=True) / ref_speed


def body(populations, marker_owner, marker_cell, marker_frac, marker_speed, marker_count):
    count_gy, count_gz = lax.axis_size("gy"), lax.axis_size("gz")
    markers = marker_owner.shape[0]
    vmem = pl.BlockSpec(memory_space=pltpu.VMEM)
    shape = jax.ShapeDtypeStruct
    tiles = shape((count_gz, 8, LANES), f32)
    field = shape((96, LANES), f32)
    cells = shape((PLANES, ROWS, LANES), f32)
    lattice = shape(populations.shape, f32)
    inputs = [
        marker_owner.reshape(1, markers),
        marker_cell,
        marker_frac,
        marker_speed,
        populations,
    ]
    send, rank, live, held, speeds, density, relax = call(
        first_kernel,
        [
            tiles,
            shape((1, markers), f32),
            shape((1, markers), jnp.int32),
            lattice,
            field,
            cells,
            cells,
        ],
        [marker_count.reshape(1, 1)]
        + [pltpu.with_memory_space_constraint(value, pltpu.HBM) for value in inputs],
        [vmem] + [pl.BlockSpec(memory_space=pltpu.HBM)] * 5,
        scratch=[pltpu.VMEM(value.shape, value.dtype) for value in inputs[0:4]]
        + [pltpu.SemaphoreType.DMA((5,))],
    )
    got = lax.all_to_all(send, "gz", split_axis=0, concat_axis=0, tiled=True)
    face = shape((FACE_ROWS, LANES), f32)
    next_pops, up, down, marks = call(
        second_kernel,
        [lattice, face, face, shape((MARK_ROWS, LANES), f32)],
        [held, got, speeds, density, relax],
        [vmem] * 5,
        scratch=[
            pltpu.VMEM(populations.shape, f32),
            pltpu.VMEM((24, ROWS, LANES), f32),
            pltpu.VMEM((24, ROWS, LANES), f32),
            pltpu.VMEM((96, LANES), f32),
        ],
    )
    below = lax.ppermute(up, "gy", [(i, i + 1) for i in range(count_gy - 1)])
    above = lax.ppermute(down, "gy", [(i + 1, i) for i in range(count_gy - 1)])
    moved, back = call(
        third_kernel,
        [lattice, shape((count_gz, 2, LANES), f32)],
        [next_pops, up, down, marks, below, above],
        [vmem] * 6,
        scratch=[
            pltpu.VMEM(populations.shape, f32),
            pltpu.VMEM((96, LANES), f32),
            pltpu.VMEM((PLANES, ROWS, LANES), f32),
            pltpu.VMEM(populations.shape, f32),
            pltpu.VMEM((5, ROWS, LANES), f32),
        ],
    )
    back = lax.all_to_all(back, "gz", split_axis=0, concat_axis=0, tiled=True)
    pops, force = call(
        last_kernel,
        [lattice, shape((3, markers), f32)],
        [moved, back, live, rank],
        [vmem] * 4,
    )
    return pops, force


def solution(mesh):
    return jax.shard_map(
        body,
        mesh=mesh,
        in_specs=(
            P(None, None, "gy", "gz"),
            P(("gy", "gz"), None),
            P(None, ("gy", "gz")),
            P(None, ("gy", "gz")),
            P(None, ("gy", "gz")),
            P(("gy", "gz")),
        ),
        out_specs=(P(None, None, "gy", "gz"), P(None, ("gy", "gz"))),
        check_vma=False,
    )
```
